32 devices in a mesh: seg: 2 (over y), strip: 4 (over z), tile: 4 (over x, core).
Axes of the slice: x: 2, y: 2, z: 4, core: 2. Of those that a mesh axis runs over, the one named last changes fastest.
Arguments:
- positions: float32 [4, 3, 65536], P('strip', None, ('seg', 'tile')), may hold values from -4 to 4, as said below
- lever_arm: float32 [4, 3, 65536], P('strip', None, ('seg', 'tile')), may hold values from -6 to 6
- spline_time: float32 [4, 65536], P('strip', ('seg', 'tile')), may hold values from 0 to 1
- covariance: float32 [4, 6, 65536], P('strip', None, ('seg', 'tile')), may hold values from -0.35 to 1, as said below
- partner: int32 [4, 65536], P('strip', ('seg', 'tile')), may hold values from 0 to 32767
- partner_side: int32 [4, 512], P('strip', ('seg', 'tile')), may hold values from 0 to 2, as said below
- tile_knot: int32 [4, 512], P('strip', ('seg', 'tile')), may hold values from 0 to 127
Outputs:
- adjusted: float32 [4, 3, 65536], P('strip', None, ('seg', 'tile'))
- corrections: float32 [4, 6, 256], P('strip', None, 'seg')
The draws below stay inside these ranges and needn't reach their ends.
Inputs may be any that keep to these rules, and one draw needn't show every extreme that they name: `partner_side`: 0: the intersecting strip is the one below, 1: the one above, 2: the tile has no partner; the first strip never has 0 and the last never 1. Index of the partner among the 32768 points of the neighbour strip in the same along-track block. `tile_knot`: segment number within the tile's along-track block of 128 segments. `covariance`: each point's six entries form a positive definite matrix. `positions`: coordinates in a local frame.
All inputs are finite; a program needn't handle non-finite values.
Results may differ from the reference program's by a relative error of at most 0.00014.
Values sent between devices are 32-bit elements; how exact they have to be, the bound alone decides.
No kernel may reach another device: no remote copies, remote signals or barrier semaphores. Data moves between devices by JAX's collectives and lax.ppermute only.
A program may use at most 128 MiB of HBM per device.

```python
import math
import jax
import jax.numpy as jnp
from jax import lax

KNOT_DEV = 128
TILE_PTS = 128
STRIPS = 4
TILES_DEV = 64
BLOCK_PTS = 32768
POINTS = 65536
TILES = 512
KNOTS = 256
N_TILE = 4


def draw_positions(key, part):
    noise_key, offset_key = jax.random.split(key)
    noise = 0.3 * jax.random.normal(noise_key, (STRIPS, 3, POINTS), jnp.float32)
    offsets = jax.random.uniform(offset_key, (STRIPS, 3, TILES, 1), jnp.float32, -1.0, 1.0)
    spread_out = jnp.broadcast_to(offsets, (STRIPS, 3, TILES, TILE_PTS)).reshape(STRIPS, 3, POINTS)
    return jnp.clip(spread_out + noise, -4.0, 4.0)


def draw_covariance(key, part):
    scale_key, correl_key = jax.random.split(key, 2)
    logs = jax.random.uniform(scale_key, (STRIPS, 3, POINTS), jnp.float32, math.log(0.05), 0.0)
    correl = jax.random.uniform(correl_key, (STRIPS, 3, POINTS), jnp.float32, -0.35, 0.35)
    roots = jnp.exp(0.5 * logs)
    diagonal = roots * roots
    cross = jnp.stack([correl[:, 0] * roots[:, 0] * roots[:, 1], correl[:, 1] * roots[:, 0] * roots[:, 2], correl[:, 2] * roots[:, 1] * roots[:, 2]], axis=1)
    return jnp.concatenate([diagonal, cross], axis=1)


def draw_partner_side(key, part):
    level_key, roll_key, direction_key = jax.random.split(key, 3)
    level = jax.random.randint(level_key, (STRIPS, TILES // 8, 1), 0, 4)
    level = jnp.broadcast_to(level, (STRIPS, TILES // 8, 8)).reshape(STRIPS, TILES)
    roll_value = jax.random.randint(roll_key, (STRIPS, TILES), 0, 4)
    direction = jax.random.randint(direction_key, (STRIPS, TILES), 0, 2)
    strip_ids = lax.broadcasted_iota(jnp.int32, (STRIPS, TILES), 0)
    direction = jnp.where(strip_ids == 0, 1, jnp.where(strip_ids == STRIPS - 1, 0, direction))
    return jnp.where(roll_value <= level, direction, 2).astype(jnp.int32)


def touch_ends(result, rng, low, high):
    place = [jax.random.randint(jax.random.fold_in(rng, axis), (), 0, length) for axis, length in enumerate(result.shape)]
    longest = result.shape.index(max(result.shape))
    beside = place[:longest] + [(place[longest] + 1) % result.shape[longest]] + place[longest + 1:]
    return result.at[tuple(place)].set(low).at[tuple(beside)].set(high)


def level_of(stream_key, shape, cuts, least, top_value):
    def one(dim, shards_of):
        steps = jax.random.uniform(jax.random.fold_in(jax.random.fold_in(stream_key, 6), dim), (shards_of,), jnp.float32, least / len(cuts), top_value / len(cuts))
        return jnp.repeat(jnp.exp(steps), shape[dim] // shards_of).reshape((-1,) + (1,) * (len(shape) - dim - 1))

    gain = one(*cuts[0])
    for cut in cuts[1:]:
        gain = gain * one(*cut)
    return gain


def centred(own_key, dims, scale, reach, pieces=(), kind=jnp.bfloat16):
    gain = level_of(own_key, dims, pieces, -0.22, 0.18) if pieces else 1.0
    result = jax.random.normal(own_key, dims, jnp.float32) * scale * gain
    return jnp.minimum(jnp.maximum(result, -reach), reach).astype(kind)


def setup_inputs(seed: int = 0) -> dict:
    arg_keys = jax.random.split(jax.random.key(seed), 8)
    return {
        "positions": draw_positions(jax.random.fold_in(arg_keys[7], 71), 0),
        "lever_arm": centred(arg_keys[1], (STRIPS, 3, POINTS), 1.0, 6.0, ((0, 4), (2, 8)), jnp.float32),
        "spline_time": jnp.clip(1.0 * jax.random.uniform(arg_keys[2], (STRIPS, POINTS), jnp.float32) ** level_of(arg_keys[2], (STRIPS, POINTS), ((0, 4), (1, 8)), -0.2, 0.2), 0.0, 1.0),
        "covariance": draw_covariance(jax.random.fold_in(arg_keys[7], 71), 0),
        "partner": touch_ends(jax.random.randint(arg_keys[4], (STRIPS, POINTS), 0, BLOCK_PTS), jax.random.fold_in(arg_keys[4], 1), 0, BLOCK_PTS - 1).astype(jnp.int32),
        "partner_side": draw_partner_side(jax.random.fold_in(arg_keys[7], 71), 0),
        "tile_knot": touch_ends(jax.random.randint(arg_keys[6], (STRIPS, TILES), 0, KNOT_DEV), jax.random.fold_in(arg_keys[6], 1), 0, KNOT_DEV - 1).astype(jnp.int32),
    }


damping = 1.0

def information(spread):
    values = [spread[column] for column in range(6)]
    adjunct = [values[1] * values[2] - values[5] * values[5], values[0] * values[2] - values[4] * values[4], values[0] * values[1] - values[3] * values[3], values[4] * values[5] - values[3] * values[2], values[3] * values[5] - values[4] * values[1], values[3] * values[4] - values[0] * values[5]]
    determinant = values[0] * adjunct[0] + values[3] * adjunct[3] + values[4] * adjunct[4]
    return [entry_value / determinant for entry_value in adjunct]

def apply_information(inverse, vector):
    return jnp.stack([inverse[0] * vector[0] + inverse[3] * vector[1] + inverse[4] * vector[2], inverse[3] * vector[0] + inverse[1] * vector[1] + inverse[5] * vector[2], inverse[4] * vector[0] + inverse[5] * vector[1] + inverse[2] * vector[2]])

def rigid_columns(levers):
    blanks = jnp.zeros_like(levers[0])
    filled = jnp.ones_like(levers[0])
    layout = [[blanks, levers[2], -levers[1], filled, blanks, blanks], [-levers[2], blanks, levers[0], blanks, filled, blanks], [levers[1], -levers[0], blanks, blanks, blanks, filled]]
    return jnp.stack([jnp.stack(layout_row) for layout_row in layout])

def tile_terms(coords, columns, stamps, spread, target, live_mask):
    inverse = [entry_value * live_mask for entry_value in information(spread + target[3:])]
    weighted = jnp.stack([apply_information(inverse, columns[:, column]) for column in range(6)], axis=1)
    residual = coords - target[:3]
    pulled = apply_information(inverse, residual)
    gram = columns[0][:, None] * weighted[0][None] + columns[1][:, None] * weighted[1][None] + columns[2][:, None] * weighted[2][None]
    gradient = lax.optimization_barrier(jnp.sum(columns * pulled[:, None], axis=0))
    point_count = coords.shape[1]
    tile_count = point_count // TILE_PTS
    later = stamps.reshape(tile_count, TILE_PTS)
    early = 1.0 - later
    weights = jnp.stack([early * early, early * later, later * later])
    blocks = jnp.einsum('abtk,wtk->wabt', gram.reshape(6, 6, tile_count, TILE_PTS), weights, precision=lax.Precision.HIGHEST)
    vectors = jnp.einsum('atk,wtk->wat', gradient.reshape(6, tile_count, TILE_PTS), jnp.stack([early, later]), precision=lax.Precision.HIGHEST)
    return jnp.concatenate([blocks.reshape(108, tile_count), vectors.reshape(12, tile_count)], axis=0)

def solve_blocks(matrix, right_side):
    factor = [[None] * 6 for column in range(6)]
    for column in range(6):
        pivot_sum = matrix[column, column]
        for inner_col in range(column):
            pivot_sum = pivot_sum - factor[column][inner_col] * factor[column][inner_col]
        factor[column][column] = jnp.sqrt(pivot_sum)
        for target_row in range(column + 1, 6):
            entry_sum = matrix[target_row, column]
            for inner_col in range(column):
                entry_sum = entry_sum - factor[target_row][inner_col] * factor[column][inner_col]
            factor[target_row][column] = entry_sum / factor[column][column]
    forward = []
    for target_row in range(6):
        entry_sum = right_side[target_row]
        for inner_col in range(target_row):
            entry_sum = entry_sum - factor[target_row][inner_col] * forward[inner_col]
        forward.append(entry_sum / factor[target_row][target_row])
    answer = [None] * 6
    for target_row in reversed(range(6)):
        entry_sum = forward[target_row]
        for inner_col in range(target_row + 1, 6):
            entry_sum = entry_sum - factor[inner_col][target_row] * answer[inner_col]
        answer[target_row] = entry_sum / factor[target_row][target_row]
    return jnp.stack(answer)

def knot_system(totals, earlier_curve, earlier_grad):
    knots_here = totals.shape[1]
    identity = jnp.eye(6, dtype=jnp.float32)[:, :, None]
    matrix = (earlier_curve + totals[0:36]).reshape(6, 6, knots_here) + damping * identity
    return (matrix, earlier_grad + totals[108:114])

def couple(flat, vector):
    return lax.optimization_barrier(jnp.sum(flat.reshape(6, 6, -1) * vector[None], axis=1))

def reproject(coords, columns, stamps, lower_pose, upper_pose):
    tile_count = lower_pose.shape[1]
    later = stamps.reshape(tile_count, TILE_PTS)
    early = 1.0 - later
    pose = early[None] * lower_pose[:, :, None] + later[None] * upper_pose[:, :, None]
    return coords + lax.optimization_barrier(jnp.sum(columns * pose.reshape(6, -1)[None], axis=1))

def one_strip(strip_items):
    coords, levers, stamps, spread, target_data, live_mask, segment_ids = strip_items
    columns = rigid_columns(levers)
    tile_sums = tile_terms(coords, columns, stamps, spread, target_data, live_mask)
    totals = jax.ops.segment_sum(tile_sums.T, segment_ids, num_segments=KNOTS).T
    blank_column = jnp.zeros((120, 1), jnp.float32)
    earlier = jnp.concatenate([blank_column, totals[:, :-1]], axis=1)
    matrix, right_side = knot_system(totals, earlier[72:108], earlier[114:120])
    first_step = -solve_blocks(matrix, right_side)
    blank_six = jnp.zeros((6, 1), jnp.float32)
    below_step = jnp.concatenate([blank_six, first_step[:, :-1]], axis=1)
    above_step = jnp.concatenate([first_step[:, 1:], blank_six], axis=1)
    corrected = right_side + couple(earlier[36:72], below_step) + couple(totals[36:72], above_step)
    second_step = -solve_blocks(matrix, corrected)
    extended = jnp.concatenate([second_step, blank_six], axis=1)
    lower_pose = jnp.take(extended, segment_ids, axis=1)
    upper_pose = jnp.take(extended, segment_ids + 1, axis=1)
    return (reproject(coords, columns, stamps, lower_pose, upper_pose), second_step)

def reference(positions, lever_arm, spline_time, covariance, partner, partner_side, tile_knot):
    side_pts = jnp.repeat(partner_side, TILE_PTS, axis=1)
    strip_ids = lax.broadcasted_iota(jnp.int32, (STRIPS, POINTS), 0)
    neighbour = strip_ids + jnp.where(side_pts == 0, -1, jnp.where(side_pts == 1, 1, 0))
    block_start = lax.broadcasted_iota(jnp.int32, (STRIPS, POINTS), 1) // BLOCK_PTS * BLOCK_PTS
    flat_index = (neighbour * POINTS + block_start + partner).astype(jnp.int32).reshape(STRIPS * POINTS)
    point_table = jnp.concatenate([positions, covariance], axis=1).transpose(1, 0, 2).reshape(9, STRIPS * POINTS)
    target = jnp.take(point_table, flat_index, axis=1).reshape(9, STRIPS, POINTS).transpose(1, 0, 2)
    live_mask = (side_pts != 2).astype(jnp.float32)
    segment_ids = (lax.broadcasted_iota(jnp.int32, (STRIPS, TILES), 1) // (TILES_DEV * N_TILE) * KNOT_DEV + tile_knot).astype(jnp.int32)
    adjusted, corrections = lax.map(one_strip, (positions, lever_arm, spline_time, covariance, target, live_mask, segment_ids))
    return (adjusted, corrections)
```

```python
import functools

import jax
import jax.numpy as jnp
from jax import lax
from jax.experimental import pallas as pl
from jax.experimental.pallas import tpu as pltpu
from jax.sharding import PartitionSpec as P

KNOT_DEV = 128
TILE_PTS = 128
CHANNELS = 9
BLOCK_TILES = 4
SUM_ROWS = 80

damping = 1.0

PAIRS = [(a, b) for a in range(6) for b in range(a, 6)]


def params():
    return pltpu.CompilerParams(vmem_limit_bytes=48 * 2**20)


def vmem(count):
    return [pl.BlockSpec(memory_space=pltpu.VMEM)] * count


def smem(count):
    return [pl.BlockSpec(memory_space=pltpu.SMEM)] * count


def pack_kernel(pos_ref, cov_ref, out_ref):
    tiles = out_ref.shape[1]
    for source, count, base in ((pos_ref, 3, 0), (cov_ref, 6, 3)):
        for channel in range(count):
            for tile in range(tiles):
                out_ref[base + channel, tile : tile + 1, :] = source[
                    0, channel : channel + 1, tile * TILE_PTS : (tile + 1) * TILE_PTS
                ]


def side_kernel(lever_ref, time_ref, partner_ref, out_ref, index_ref):
    tiles = index_ref.shape[0]
    for tile in range(tiles):
        span = slice(tile * TILE_PTS, (tile + 1) * TILE_PTS)
        for channel in range(3):
            out_ref[channel, tile : tile + 1, :] = lever_ref[0, channel : channel + 1, span]
        out_ref[3, tile : tile + 1, :] = time_ref[0:1, span]
        index_ref[tile : tile + 1, :] = partner_ref[0:1, span]


def split_two(value):
    high = value.astype(jnp.bfloat16)
    low = (value - high.astype(jnp.float32)).astype(jnp.bfloat16)
    return high, low


def gather_phase(shards, side_ref, owner_ref, index_ref, tables, target, work):
    weights_high, weights_low, key_ref, row_ref, order_ref, hot_refs = work
    tiles = index_ref.shape[0]
    index = index_ref[...]
    point_row = index >> 7
    lane = index & (TILE_PTS - 1)
    key = lane
    row = jnp.full_like(index, -1)
    for place in range(shards):
        offset = point_row - owner_ref[place] * tiles
        inside = (offset >= 0) & (offset < tiles)
        key = jnp.where(inside, lane + place * TILE_PTS, key)
        row = jnp.where(inside, offset, row)
    key_ref[...] = key
    row_ref[...] = row
    for side in range(2):
        for place in range(shards):
            for channel in range(CHANNELS):
                high, low = split_two(tables[side][place][channel])
                rows = slice(channel * tiles, (channel + 1) * tiles)
                cols = slice(place * TILE_PTS, (place + 1) * TILE_PTS)
                weights_high[side, rows, cols] = high
                weights_low[side, rows, cols] = low

    def list_side(side, start):
        def step(tile, count):
            here = side_ref[tile] == side

            @pl.when(here)
            def _():
                order_ref[count] = tile

            return count + here.astype(jnp.int32)

        end = lax.fori_loop(0, tiles, step, start)
        whole = start + (end - start + BLOCK_TILES - 1) // BLOCK_TILES * BLOCK_TILES

        def fill(place, carry):
            order_ref[place] = order_ref[end - 1]
            return carry

        lax.fori_loop(end, whole, fill, 0)
        return whole

    first_end = list_side(0, jnp.int32(0))
    second_end = list_side(1, first_end)
    first_blocks = first_end // BLOCK_TILES
    blocks = second_end // BLOCK_TILES
    queries = BLOCK_TILES * TILE_PTS
    depth = shards * TILE_PTS

    def names(block):
        return [order_ref[block * BLOCK_TILES + j] for j in range(BLOCK_TILES)]

    def body(block, carry):
        ids = names(block)
        side = (block >= first_blocks).astype(jnp.int32)
        keys = jnp.concatenate([key_ref[pl.ds(i, 1), :] for i in ids], axis=1)
        rows = jnp.concatenate([row_ref[pl.ds(i, 1), :] for i in ids], axis=1)
        hot = jnp.where(lax.broadcasted_iota(jnp.int32, (depth, queries), 0) == keys, 1.0, 0.0)
        hot = hot.astype(jnp.bfloat16)
        picked = jnp.dot(weights_high[side], hot, preferred_element_type=jnp.float32)
        picked = picked + jnp.dot(weights_low[side], hot, preferred_element_type=jnp.float32)
        spread_rows = jnp.broadcast_to(rows, (8, queries))
        eight = lax.broadcasted_iota(jnp.int32, (8, queries), 0)
        totals = [jnp.zeros((8, queries), jnp.float32) for _ in range(CHANNELS)]
        for step in range(tiles // 8):
            here = spread_rows == eight + 8 * step
            for channel in range(CHANNELS):
                begin = channel * tiles + 8 * step
                totals[channel] = jnp.where(here, picked[begin : begin + 8], totals[channel])
        for channel in range(CHANNELS):
            flat = jnp.sum(totals[channel], axis=0, keepdims=True)
            for j in range(BLOCK_TILES):
                target[channel, pl.ds(ids[j], 1), :] = flat[:, j * TILE_PTS : (j + 1) * TILE_PTS]
        return carry

    lax.fori_loop(0, blocks, body, 0)


def gather_kernel(shards, *refs):
    side_ref, owner_ref, index_ref = refs[:3]
    lower = refs[3 : 3 + shards]
    upper = refs[3 + shards : 3 + 2 * shards]
    own_ref, extra_ref, live_ref, knot_ref, sums_ref = refs[3 + 2 * shards : 8 + 2 * shards]
    target = refs[8 + 2 * shards]
    totals_ref, parts_ref = refs[9 + 2 * shards : 11 + 2 * shards]
    work = refs[11 + 2 * shards : 16 + 2 * shards] + (None,)
    target[...] = jnp.zeros_like(target)
    gather_phase(shards, side_ref, owner_ref, index_ref, (lower, upper), target, work)
    sum_phase(target, own_ref, extra_ref, live_ref, knot_ref, sums_ref, totals_ref, parts_ref)


def sum_phase(target, own_ref, extra_ref, live_ref, knot_ref, sums_ref, totals_ref, parts_ref):
    tiles = target.shape[1]
    group = 16
    ones = jnp.ones((3 * TILE_PTS, KNOT_DEV), jnp.bfloat16)
    for begin in range(0, tiles, group):
        span = slice(begin, begin + group)
        live = (live_ref[span, :] != 2).astype(jnp.float32)
        m = [own_ref[3 + c, span, :] + target[3 + c, span, :] for c in range(6)]
        residual = [own_ref[c, span, :] - target[c, span, :] for c in range(3)]
        lever = [extra_ref[c, span, :] for c in range(3)]
        later = extra_ref[3, span, :]
        early = 1.0 - later
        adjunct = [
            m[1] * m[2] - m[5] * m[5],
            m[0] * m[2] - m[4] * m[4],
            m[0] * m[1] - m[3] * m[3],
            m[4] * m[5] - m[3] * m[2],
            m[3] * m[5] - m[4] * m[1],
            m[3] * m[4] - m[0] * m[5],
        ]
        determinant = m[0] * adjunct[0] + m[3] * adjunct[3] + m[4] * adjunct[4]
        scale = live / determinant
        inv = [entry * scale for entry in adjunct]
        info = [[inv[0], inv[3], inv[4]], [inv[3], inv[1], inv[5]], [inv[4], inv[5], inv[2]]]
        weighted = [[None] * 6 for _ in range(3)]
        for i in range(3):
            weighted[i][0] = lever[1] * info[i][2] - lever[2] * info[i][1]
            weighted[i][1] = lever[2] * info[i][0] - lever[0] * info[i][2]
            weighted[i][2] = lever[0] * info[i][1] - lever[1] * info[i][0]
            for j in range(3):
                weighted[i][3 + j] = info[i][j]

        def turned(column):
            return [
                lever[1] * column[2] - lever[2] * column[1],
                lever[2] * column[0] - lever[0] * column[2],
                lever[0] * column[1] - lever[1] * column[0],
            ] + list(column)

        pulled = [
            info[i][0] * residual[0] + info[i][1] * residual[1] + info[i][2] * residual[2]
            for i in range(3)
        ]
        gradient = turned(pulled)
        gram = {}
        for b in range(6):
            column = turned([weighted[i][b] for i in range(3)])
            for a in range(b + 1):
                gram[a, b] = column[a]
        both = early * later
        terms = []
        for weight in (early * early, both, later * later):
            terms += [gram[pair] * weight for pair in PAIRS]
        for weight in (early, later):
            terms += [entry * weight for entry in gradient]
        for place, term in enumerate(terms):
            rows = slice(place * group, (place + 1) * group)
            high = term.astype(jnp.bfloat16)
            rest = term - high.astype(jnp.float32)
            middle = rest.astype(jnp.bfloat16)
            low = (rest - middle.astype(jnp.float32)).astype(jnp.bfloat16)
            parts_ref[rows, 0:TILE_PTS] = high
            parts_ref[rows, TILE_PTS : 2 * TILE_PTS] = middle
            parts_ref[rows, 2 * TILE_PTS : 3 * TILE_PTS] = low
        tile_sums = jnp.dot(parts_ref[...], ones, preferred_element_type=jnp.float32)
        knots = knot_ref[span, :]
        chosen = knots == lax.broadcasted_iota(jnp.int32, (group, KNOT_DEV), 1)
        for place in range(len(terms)):
            piece = tile_sums[place * group : (place + 1) * group]
            piece = jnp.where(chosen, piece, 0.0)
            piece = piece[0:8] + piece[8:16]
            rows = slice(place * 8, (place + 1) * 8)
            if begin:
                piece = totals_ref[rows, :] + piece
            totals_ref[rows, :] = piece
    for place in range(SUM_ROWS):
        if place < 75:
            rows = totals_ref[place * 8 : (place + 1) * 8, :]
            sums_ref[place : place + 1, :] = jnp.sum(rows, axis=0, keepdims=True)
        else:
            sums_ref[place : place + 1, :] = jnp.zeros((1, KNOT_DEV), jnp.float32)


def gather_sums(sides, owners, index, lower, upper, own, extra, live, knots):
    shards = len(lower)
    tiles = index.shape[0]
    return pl.pallas_call(
        functools.partial(gather_kernel, shards),
        out_shape=jax.ShapeDtypeStruct((SUM_ROWS, KNOT_DEV), jnp.float32),
        in_specs=smem(2) + vmem(2 * shards + 5),
        out_specs=pl.BlockSpec(memory_space=pltpu.VMEM),
        scratch_shapes=[
            pltpu.VMEM((CHANNELS, tiles, TILE_PTS), jnp.float32),
            pltpu.VMEM((75 * 8, KNOT_DEV), jnp.float32),
            pltpu.VMEM((75 * 16, 3 * TILE_PTS), jnp.bfloat16),
            pltpu.VMEM((2, CHANNELS * tiles, shards * TILE_PTS), jnp.bfloat16),
            pltpu.VMEM((2, CHANNELS * tiles, shards * TILE_PTS), jnp.bfloat16),
            pltpu.VMEM((tiles, TILE_PTS), jnp.int32),
            pltpu.VMEM((tiles, TILE_PTS), jnp.int32),
            pltpu.SMEM((tiles + 4 * BLOCK_TILES,), jnp.int32),
        ],
        compiler_params=params(),
    )(sides, owners, index, *lower, *upper, own, extra, live, knots)


def cholesky(matrix):
    factor = {}
    inverse = []
    for column in range(6):
        pivot = matrix[column, column]
        for inner in range(column):
            pivot = pivot - factor[column, inner] * factor[column, inner]
        inverse.append(1.0 / jnp.sqrt(pivot))
        for row in range(column + 1, 6):
            entry = matrix[column, row]
            for inner in range(column):
                entry = entry - factor[row, inner] * factor[column, inner]
            factor[row, column] = entry * inverse[column]
    return factor, inverse


def solve(system, right_side):
    factor, inverse = system
    forward = []
    for row in range(6):
        entry = right_side[row]
        for inner in range(row):
            entry = entry - factor[row, inner] * forward[inner]
        forward.append(entry * inverse[row])
    answer = [None] * 6
    for row in reversed(range(6)):
        entry = forward[row]
        for inner in range(row + 1, 6):
            entry = entry - factor[inner, row] * answer[inner]
        answer[row] = entry * inverse[row]
    return answer


def step_kernel(blocks_count, edge_ref, sums_ref, own_ref, extra_ref, knot_ref, adjusted_ref, out_ref, held):
    tiles = knot_ref.shape[0]
    for place in range(3):
        seg = edge_ref[place]
        there = edge_ref[3 + place] > 0
        first = seg * blocks_count
        total = sums_ref[first]
        for other in range(1, blocks_count):
            total = total + sums_ref[first + other]
        held[place * SUM_ROWS : (place + 1) * SUM_ROWS, :] = jnp.where(there, total, 0.0)
    for place in range(3, 8):
        held[place * SUM_ROWS : (place + 1) * SUM_ROWS, :] = jnp.zeros(
            (SUM_ROWS, KNOT_DEV), jnp.float32
        )
    shape = (8, KNOT_DEV)
    lanes = lax.broadcasted_iota(jnp.int32, shape, 1)
    rows = lax.broadcasted_iota(jnp.int32, shape, 0)

    def earlier(value):
        turned = pltpu.roll(value, 1, 1)
        return jnp.where(lanes == 0, pltpu.roll(turned, 1, 0), turned)

    def following(value):
        turned = pltpu.roll(value, KNOT_DEV - 1, 1)
        return jnp.where(lanes == KNOT_DEV - 1, pltpu.roll(turned, 7, 0), turned)

    def quantity(place):
        return held[pl.ds(place, 8, stride=SUM_ROWS), :]

    pair_place = {pair: place for place, pair in enumerate(PAIRS)}
    matrix, cross, cross_before = {}, {}, {}
    for pair, place in pair_place.items():
        value = quantity(place) + earlier(quantity(42 + place))
        matrix[pair] = value + damping if pair[0] == pair[1] else value
        cross[pair] = quantity(21 + place)
        cross_before[pair] = earlier(cross[pair])
    right_side = [quantity(63 + a) + earlier(quantity(69 + a)) for a in range(6)]
    system = cholesky(matrix)
    beyond = (rows >= 2) & (edge_ref[5] == 0)
    first = [jnp.where(beyond, 0.0, -entry) for entry in solve(system, right_side)]
    before = [earlier(entry) for entry in first]
    after = [following(entry) for entry in first]
    corrected = []
    for a in range(6):
        total = right_side[a]
        for b in range(6):
            pair = (min(a, b), max(a, b))
            total = total + cross_before[pair] * before[b] + cross[pair] * after[b]
        corrected.append(total)
    second = [jnp.where(beyond, 0.0, -entry) for entry in solve(system, corrected)]
    upper = [following(entry) for entry in second]
    for a in range(6):
        out_ref[0, a : a + 1, :] = second[a][1:2]
    low_rows = [jnp.broadcast_to(second[a][1:2], shape) for a in range(6)]
    high_rows = [jnp.broadcast_to(upper[a][1:2], shape) for a in range(6)]
    for begin in range(0, tiles, 8):
        span = slice(begin, begin + 8)
        knots = knot_ref[span, :]
        later = extra_ref[3, span, :]
        early = 1.0 - later
        pose = []
        for a in range(6):
            low = jnp.take_along_axis(low_rows[a], knots, axis=1, mode="promise_in_bounds")
            high = jnp.take_along_axis(high_rows[a], knots, axis=1, mode="promise_in_bounds")
            pose.append(early * low + later * high)
        lever = [extra_ref[c, span, :] for c in range(3)]
        moved = [
            pose[1] * lever[2] - pose[2] * lever[1] + pose[3],
            pose[2] * lever[0] - pose[0] * lever[2] + pose[4],
            pose[0] * lever[1] - pose[1] * lever[0] + pose[5],
        ]
        for c in range(3):
            value = own_ref[c, span, :] + moved[c]
            for j in range(8):
                at = (begin + j) * TILE_PTS
                adjusted_ref[0, c : c + 1, at : at + TILE_PTS] = value[j : j + 1]


def local(positions, lever_arm, spline_time, covariance, partner, partner_side, tile_knot):
    points = positions.shape[2]
    tiles = points // TILE_PTS
    strips = lax.axis_size("strip")
    members = lax.axis_size("tile")
    segs = lax.axis_size("seg")
    place = lax.axis_index("tile")
    seg = lax.axis_index("seg")

    own = pl.pallas_call(
        pack_kernel,
        out_shape=jax.ShapeDtypeStruct((CHANNELS, tiles, TILE_PTS), jnp.float32),
        in_specs=vmem(2),
        out_specs=pl.BlockSpec(memory_space=pltpu.VMEM),
        compiler_params=params(),
    )(positions, covariance)
    extra, index = pl.pallas_call(
        side_kernel,
        out_shape=(
            jax.ShapeDtypeStruct((4, tiles, TILE_PTS), jnp.float32),
            jax.ShapeDtypeStruct((tiles, TILE_PTS), jnp.int32),
        ),
        in_specs=vmem(3),
        out_specs=(pl.BlockSpec(memory_space=pltpu.VMEM),) * 2,
        compiler_params=params(),
    )(lever_arm, spline_time, partner)
    live = jnp.broadcast_to(partner_side[0][:, None], (tiles, TILE_PTS))
    knots = jnp.broadcast_to(tile_knot[0][:, None], (tiles, TILE_PTS))

    def pick(steps, hop):
        pairs = []
        for strip in range(strips):
            for member in range(members):
                target = strip + steps
                if 0 <= target < strips:
                    source = strip * members + (member + hop) % members
                    pairs.append((source, target * members + member))
        return lax.ppermute(own, ("strip", "tile"), pairs)

    swap = [(member, member ^ 1) for member in range(members)]
    lower, upper, owners = [], [], []
    for hop in range(0, members, 2):
        below = pick(1, hop)
        above = pick(-1, hop)
        other = lax.ppermute(jnp.stack([below, above]), "tile", swap)
        lower += [below, other[0]]
        upper += [above, other[1]]
        owners += [(place + hop) % members, ((place ^ 1) + hop) % members]
    sums = gather_sums(
        partner_side[0], jnp.stack(owners).astype(jnp.int32), index, lower, upper, own, extra, live, knots
    )
    all_sums = lax.all_gather(sums, ("seg", "tile"), axis=0)
    edges = jnp.stack(
        [
            jnp.maximum(seg - 1, 0),
            seg,
            jnp.minimum(seg + 1, segs - 1),
            (seg > 0).astype(jnp.int32),
            jnp.ones((), jnp.int32),
            (seg < segs - 1).astype(jnp.int32),
        ]
    ).astype(jnp.int32)
    return pl.pallas_call(
        functools.partial(step_kernel, members),
        out_shape=(
            jax.ShapeDtypeStruct((1, 3, points), jnp.float32),
            jax.ShapeDtypeStruct((1, 6, KNOT_DEV), jnp.float32),
        ),
        in_specs=smem(1) + vmem(4),
        out_specs=(pl.BlockSpec(memory_space=pltpu.VMEM),) * 2,
        scratch_shapes=[pltpu.VMEM((8 * SUM_ROWS, KNOT_DEV), jnp.float32)],
        compiler_params=params(),
    )(edges, all_sums, own, extra, knots)


def solution(mesh):
    in_specs = (
        P("strip", None, ("seg", "tile")),
        P("strip", None, ("seg", "tile")),
        P("strip", ("seg", "tile")),
        P("strip", None, ("seg", "tile")),
        P("strip", ("seg", "tile")),
        P("strip", ("seg", "tile")),
        P("strip", ("seg", "tile")),
    )
    out_specs = (P("strip", None, ("seg", "tile")), P("strip", None, "seg"))
    return jax.shard_map(local, mesh=mesh, in_specs=in_specs, out_specs=out_specs, check_vma=False)
```

```python
import functools

import jax
import jax.numpy as jnp
from jax import lax
from jax.experimental import pallas as pl
from jax.experimental.pallas import tpu as pltpu
from jax.sharding import PartitionSpec as P

KNOT_DEV = 128
TILE_PTS = 128
CHANNELS = 9
BLOCK_TILES = 4
SUM_ROWS = 80

damping = 1.0

PAIRS = [(a, b) for a in range(6) for b in range(a, 6)]


def params(mebibytes=48):
    return pltpu.CompilerParams(vmem_limit_bytes=mebibytes * 2**20)


def vmem(count):
    return [pl.BlockSpec(memory_space=pltpu.VMEM)] * count


def smem(count):
    return [pl.BlockSpec(memory_space=pltpu.SMEM)] * count


def pack_kernel(pos, cov, lever, time, partner, sides, knots, table_ref, points_ref, ints, small, sems):
    tiles = time.shape[0]
    base = 14 * tiles

    def span(first, count):
        return points_ref.at[pl.ds(first * tiles, count * tiles)]

    copies = [
        pltpu.make_async_copy(pos, table_ref.at[pl.ds(0, 3)], sems.at[0]),
        pltpu.make_async_copy(cov, table_ref.at[pl.ds(3, 6)], sems.at[1]),
        pltpu.make_async_copy(partner, ints, sems.at[2]),
        pltpu.make_async_copy(sides, small.at[0], sems.at[3]),
        pltpu.make_async_copy(knots, small.at[1], sems.at[4]),
        pltpu.make_async_copy(time, span(12, 1), sems.at[5]),
    ]
    copies += [
        pltpu.make_async_copy(lever.at[c], span(9 + c, 1), sems.at[6 + c]) for c in range(3)
    ]
    for copy in copies:
        copy.start()
    for copy in copies:
        copy.wait()
    for channel in range(CHANNELS):
        points_ref[channel * tiles : (channel + 1) * tiles, :] = table_ref[channel]
    points_ref[13 * tiles : 14 * tiles, :] = ints[...].astype(jnp.float32)
    for place in range(2):
        row = base + place
        points_ref[row : row + 1, 0:tiles] = small[place].astype(jnp.float32)


def split_two(value):
    high = value.astype(jnp.bfloat16)
    low = (value - high.astype(jnp.float32)).astype(jnp.bfloat16)
    return high, low


def list_tiles(names, tiles, order_ref):
    count = len(names) * tiles
    limit = order_ref.shape[0] // 2
    first = jnp.int32(0)
    second = jnp.int32(limit)
    for tile in range(count):
        side = names[tile // tiles][0, tile % tiles]
        order_ref[first] = tile
        first = first + (side == 0.0).astype(jnp.int32)
        order_ref[second] = tile
        second = second + (side == 1.0).astype(jnp.int32)
    last_first = order_ref[jnp.maximum(first - 1, 0)]
    last_second = order_ref[jnp.maximum(second - 1, limit)]
    for extra in range(BLOCK_TILES):
        order_ref[first + extra] = last_first
        order_ref[second + extra] = last_second
    blocks = lambda number: lax.shift_right_logical(number + BLOCK_TILES - 1, 2)
    return blocks(first), blocks(second - limit), limit


def gather_kernel(groups, *refs):
    points = refs[:groups]
    tables = (refs[groups : groups + 2], refs[groups + 2 : groups + 4])
    sums_ref = refs[groups + 4]
    target, key_ref, row_ref, live_ref, knot_ref, weights, totals_ref, parts_ref, order_ref, sems = refs[
        groups + 5 : groups + 15
    ]
    names = refs[groups + 15 :]
    tiles = tables[0][0].shape[1]
    base = 14 * tiles
    copies = [
        pltpu.make_async_copy(points[p].at[pl.ds(base, 8)], names[p], sems.at[p]) for p in range(groups)
    ]
    for copy in copies:
        copy.start()

    for side in range(2):
        for place in range(2):
            for channel in range(CHANNELS):
                high, low = split_two(tables[side][place][channel])
                rows = slice(channel * tiles, (channel + 1) * tiles)
                at = place * TILE_PTS
                weights[side, rows, at : at + TILE_PTS] = high
                weights[side, rows, at + 2 * TILE_PTS : at + 3 * TILE_PTS] = low
    member = lax.axis_index("tile")
    for p in range(groups):
        index = points[p][13 * tiles : 14 * tiles, :].astype(jnp.int32)
        point_row = lax.shift_right_logical(index, 7)
        lane = index & (TILE_PTS - 1)
        key = lane
        row = jnp.full_like(index, -1)
        for place in range(2):
            offset = point_row - (member ^ place) * tiles
            inside = (offset >= 0) & (offset < tiles)
            key = jnp.where(inside, lane + place * TILE_PTS, key)
            row = jnp.where(inside, offset, row)
        key_ref[p * tiles : (p + 1) * tiles, :] = key
        row_ref[p * tiles : (p + 1) * tiles, :] = row
    target[...] = jnp.zeros_like(target)
    for copy in copies:
        copy.wait()
    for p in range(groups):
        for tile in range(tiles):
            at = p * tiles + tile
            live = (names[p][0, tile] != 2.0).astype(jnp.float32)
            live_ref[at : at + 1, :] = jnp.full((1, TILE_PTS), live, jnp.float32)
            knot_ref[at : at + 1, :] = jnp.full((1, KNOT_DEV), names[p][1, tile], jnp.float32)
    first_blocks, second_blocks, limit = list_tiles(names, tiles, order_ref)
    blocks = first_blocks + second_blocks
    queries = BLOCK_TILES * TILE_PTS

    def one_block(block):
        block = jnp.minimum(block, blocks - 1)
        later_side = block >= first_blocks
        side = later_side.astype(jnp.int32)
        start = jnp.where(later_side, limit + (block - first_blocks) * BLOCK_TILES, block * BLOCK_TILES)
        ids = [order_ref[start + j] for j in range(BLOCK_TILES)]
        keys = jnp.concatenate([key_ref[pl.ds(i, 1), :] for i in ids], axis=1)
        rows = jnp.concatenate([row_ref[pl.ds(i, 1), :] for i in ids], axis=1)
        hot = jnp.where(
            lax.broadcasted_iota(jnp.int32, (2 * TILE_PTS, queries), 0) == keys, 1.0, 0.0
        ).astype(jnp.bfloat16)
        picked = jnp.dot(
            weights[side], jnp.concatenate([hot, hot], axis=0), preferred_element_type=jnp.float32
        )
        spread_rows = jnp.broadcast_to(rows, (8, queries))
        eight = lax.broadcasted_iota(jnp.int32, (8, queries), 0)
        found = [jnp.zeros((8, queries), jnp.float32) for _ in range(CHANNELS)]
        for step in range(tiles // 8):
            here = spread_rows == eight + 8 * step
            for channel in range(CHANNELS):
                begin = channel * tiles + 8 * step
                found[channel] = jnp.where(here, picked[begin : begin + 8], found[channel])
        return ids, [jnp.sum(entry, axis=0, keepdims=True) for entry in found]

    def body(step, carry):
        results = [one_block(2 * step), one_block(2 * step + 1)]
        for ids, flat in results:
            for channel in range(CHANNELS):
                for j in range(BLOCK_TILES):
                    piece = flat[channel][:, j * TILE_PTS : (j + 1) * TILE_PTS]
                    target[channel, pl.ds(ids[j], 1), :] = piece
        return carry

    lax.fori_loop(0, lax.shift_right_logical(blocks + 1, 1), body, 0)

    totals_ref[...] = jnp.zeros_like(totals_ref)
    for p in range(groups):
        sum_points(p, tiles, points[p], target, row_ref, live_ref, knot_ref, totals_ref, parts_ref)
    for place in range(SUM_ROWS):
        if place < 75:
            rows = totals_ref[place * 8 : (place + 1) * 8, :]
            sums_ref[place : place + 1, :] = jnp.sum(rows, axis=0, keepdims=True)
        else:
            sums_ref[place : place + 1, :] = jnp.zeros((1, KNOT_DEV), jnp.float32)


def sum_points(p, tiles, points, target, row_ref, live_ref, knot_ref, totals_ref, parts_ref):
    group = 16
    ones = jnp.ones((2 * TILE_PTS, KNOT_DEV), jnp.bfloat16)

    def body(step, carry):
        begin = pl.multiple_of(step * group, group)
        span = pl.ds(pl.multiple_of(p * tiles + begin, group), group)

        def own(channel):
            return points[pl.ds(pl.multiple_of(channel * tiles + begin, group), group), :]

        live = jnp.where(row_ref[span, :] >= 0, live_ref[span, :], 0.0)
        m = [own(3 + c) + target[3 + c, span, :] for c in range(6)]
        residual = [own(c) - target[c, span, :] for c in range(3)]
        lever = [own(9 + c) for c in range(3)]
        later = own(12)
        early = 1.0 - later
        adjunct = [
            m[1] * m[2] - m[5] * m[5],
            m[0] * m[2] - m[4] * m[4],
            m[0] * m[1] - m[3] * m[3],
            m[4] * m[5] - m[3] * m[2],
            m[3] * m[5] - m[4] * m[1],
            m[3] * m[4] - m[0] * m[5],
        ]
        determinant = m[0] * adjunct[0] + m[3] * adjunct[3] + m[4] * adjunct[4]
        scale = live / determinant
        inv = [entry * scale for entry in adjunct]
        info = [[inv[0], inv[3], inv[4]], [inv[3], inv[1], inv[5]], [inv[4], inv[5], inv[2]]]

        def turned(column):
            return [
                lever[1] * column[2] - lever[2] * column[1],
                lever[2] * column[0] - lever[0] * column[2],
                lever[0] * column[1] - lever[1] * column[0],
            ] + list(column)

        weighted = [turned(info[i]) for i in range(3)]
        pulled = [
            info[i][0] * residual[0] + info[i][1] * residual[1] + info[i][2] * residual[2]
            for i in range(3)
        ]
        gradient = turned(pulled)
        gram = {}
        for b in range(6):
            column = turned([weighted[i][b] for i in range(3)])
            for a in range(b + 1):
                gram[a, b] = column[a]
        both = early * later
        terms = []
        for weight in (early * early, both, later * later):
            terms += [gram[pair] * weight for pair in PAIRS]
        for weight in (early, later):
            terms += [entry * weight for entry in gradient]
        for place, term in enumerate(terms):
            rows = slice(place * group, (place + 1) * group)
            high, low = split_two(term)
            parts_ref[rows, 0:TILE_PTS] = high
            parts_ref[rows, TILE_PTS : 2 * TILE_PTS] = low
        tile_sums = jnp.dot(parts_ref[...], ones, preferred_element_type=jnp.float32)
        lanes = lax.broadcasted_iota(jnp.int32, (group, KNOT_DEV), 1).astype(jnp.float32)
        chosen = knot_ref[span, :] == lanes
        for place in range(len(terms)):
            piece = jnp.where(chosen, tile_sums[place * group : (place + 1) * group], 0.0)
            rows = slice(place * 8, (place + 1) * 8)
            totals_ref[rows, :] = totals_ref[rows, :] + piece[0:8] + piece[8:16]
        return carry

    lax.fori_loop(0, tiles // group, body, 0)


def gather_sums(points, lower, upper):
    groups = len(points)
    tiles = lower[0].shape[1]
    count = groups * tiles
    return pl.pallas_call(
        functools.partial(gather_kernel, groups),
        out_shape=jax.ShapeDtypeStruct((SUM_ROWS, KNOT_DEV), jnp.float32),
        in_specs=vmem(groups + 4),
        out_specs=pl.BlockSpec(memory_space=pltpu.VMEM),
        scratch_shapes=[
            pltpu.VMEM((CHANNELS, count, TILE_PTS), jnp.float32),
            pltpu.VMEM((count, TILE_PTS), jnp.int32),
            pltpu.VMEM((count, TILE_PTS), jnp.int32),
            pltpu.VMEM((count, TILE_PTS), jnp.float32),
            pltpu.VMEM((count, KNOT_DEV), jnp.float32),
            pltpu.VMEM((2, CHANNELS * tiles, 4 * TILE_PTS), jnp.bfloat16),
            pltpu.VMEM((75 * 8, KNOT_DEV), jnp.float32),
            pltpu.VMEM((75 * 16, 2 * TILE_PTS), jnp.bfloat16),
            pltpu.SMEM((2 * (count + 2 * BLOCK_TILES),), jnp.int32),
            pltpu.SemaphoreType.DMA((groups,)),
        ]
        + [pltpu.SMEM((8, TILE_PTS), jnp.float32) for _ in range(groups)],
        compiler_params=params(14),
    )(*points, *lower, *upper)


def cholesky(matrix):
    factor = {}
    inverse = []
    for column in range(6):
        pivot = matrix[column, column]
        for inner in range(column):
            pivot = pivot - factor[column, inner] * factor[column, inner]
        inverse.append(1.0 / jnp.sqrt(pivot))
        for row in range(column + 1, 6):
            entry = matrix[column, row]
            for inner in range(column):
                entry = entry - factor[row, inner] * factor[column, inner]
            factor[row, column] = entry * inverse[column]
    return factor, inverse


def solve(system, right_side):
    factor, inverse = system
    forward = []
    for row in range(6):
        entry = right_side[row]
        for inner in range(row):
            entry = entry - factor[row, inner] * forward[inner]
        forward.append(entry * inverse[row])
    answer = [None] * 6
    for row in reversed(range(6)):
        entry = forward[row]
        for inner in range(row + 1, 6):
            entry = entry - factor[inner, row] * answer[inner]
        answer[row] = entry * inverse[row]
    return answer


def step_kernel(segs, members, knot_ref, sums_ref, points_ref, adjusted_ref, out_ref, held, index_ref):
    tiles = knot_ref.shape[1]
    for tile in range(tiles):
        index_ref[tile : tile + 1, :] = jnp.full((1, KNOT_DEV), knot_ref[0, tile], jnp.int32)
    seg = lax.axis_index("seg")
    for place in range(3):
        wanted = seg + place - 1
        there = (wanted >= 0) & (wanted < segs)
        first = jnp.minimum(jnp.maximum(wanted, 0), segs - 1) * members
        total = sums_ref[first]
        for other in range(1, members):
            total = total + sums_ref[first + other]
        held[place * SUM_ROWS : (place + 1) * SUM_ROWS, :] = jnp.where(there, total, 0.0)
    for place in range(3, 8):
        held[place * SUM_ROWS : (place + 1) * SUM_ROWS, :] = jnp.zeros(
            (SUM_ROWS, KNOT_DEV), jnp.float32
        )
    shape = (8, KNOT_DEV)
    lanes = lax.broadcasted_iota(jnp.int32, shape, 1)
    rows = lax.broadcasted_iota(jnp.int32, shape, 0)

    def earlier(value):
        turned = pltpu.roll(value, 1, 1)
        return jnp.where(lanes == 0, pltpu.roll(turned, 1, 0), turned)

    def following(value):
        turned = pltpu.roll(value, KNOT_DEV - 1, 1)
        return jnp.where(lanes == KNOT_DEV - 1, pltpu.roll(turned, 7, 0), turned)

    def quantity(place):
        return held[pl.ds(place, 8, stride=SUM_ROWS), :]

    pair_place = {pair: place for place, pair in enumerate(PAIRS)}
    matrix, cross, cross_before = {}, {}, {}
    for pair, place in pair_place.items():
        value = quantity(place) + earlier(quantity(42 + place))
        matrix[pair] = value + damping if pair[0] == pair[1] else value
        cross[pair] = quantity(21 + place)
        cross_before[pair] = earlier(cross[pair])
    right_side = [quantity(63 + a) + earlier(quantity(69 + a)) for a in range(6)]
    system = cholesky(matrix)
    beyond = (rows >= 2) & (seg == segs - 1)
    first = [jnp.where(beyond, 0.0, -entry) for entry in solve(system, right_side)]
    before = [earlier(entry) for entry in first]
    after = [following(entry) for entry in first]
    corrected = []
    for a in range(6):
        total = right_side[a]
        for b in range(6):
            pair = (min(a, b), max(a, b))
            total = total + cross_before[pair] * before[b] + cross[pair] * after[b]
        corrected.append(total)
    second = [jnp.where(beyond, 0.0, -entry) for entry in solve(system, corrected)]
    upper = [following(entry) for entry in second]
    for a in range(6):
        out_ref[a] = second[a][1:2]
    low_rows = [jnp.broadcast_to(second[a][1:2], shape) for a in range(6)]
    high_rows = [jnp.broadcast_to(upper[a][1:2], shape) for a in range(6)]
    for begin in range(0, tiles, 8):
        span = slice(begin, begin + 8)
        knots = index_ref[span, :]
        later = points_ref[12 * tiles + begin : 12 * tiles + begin + 8, :]
        early = 1.0 - later
        pose = []
        for a in range(6):
            low = jnp.take_along_axis(low_rows[a], knots, axis=1, mode="promise_in_bounds")
            high = jnp.take_along_axis(high_rows[a], knots, axis=1, mode="promise_in_bounds")
            pose.append(early * low + later * high)
        lever = [
            points_ref[c * tiles + begin : c * tiles + begin + 8, :] for c in range(9, 12)
        ]
        moved = [
            pose[1] * lever[2] - pose[2] * lever[1] + pose[3],
            pose[2] * lever[0] - pose[0] * lever[2] + pose[4],
            pose[0] * lever[1] - pose[1] * lever[0] + pose[5],
        ]
        for c in range(3):
            coords = points_ref[c * tiles + begin : c * tiles + begin + 8, :]
            adjusted_ref[c, span, :] = coords + moved[c]


def local(positions, lever_arm, spline_time, covariance, partner, partner_side, tile_knot):
    tiles = positions.shape[2] // TILE_PTS
    strips = lax.axis_size("strip")
    members = lax.axis_size("tile")
    segs = lax.axis_size("seg")

    table, points = pl.pallas_call(
        pack_kernel,
        out_shape=(
            jax.ShapeDtypeStruct((CHANNELS, tiles, TILE_PTS), jnp.float32),
            jax.ShapeDtypeStruct((14 * tiles + 8, TILE_PTS), jnp.float32),
        ),
        in_specs=[pl.BlockSpec(memory_space=pltpu.HBM)] * 7,
        out_specs=(pl.BlockSpec(memory_space=pltpu.VMEM),) * 2,
        scratch_shapes=[
            pltpu.VMEM((tiles, TILE_PTS), jnp.int32),
            pltpu.VMEM((2, 1, tiles), jnp.int32),
            pltpu.SemaphoreType.DMA((9,)),
        ],
        compiler_params=params(63),
    )(
        positions.reshape(3, tiles, TILE_PTS),
        covariance.reshape(6, tiles, TILE_PTS),
        lever_arm.reshape(3, tiles, TILE_PTS),
        spline_time.reshape(tiles, TILE_PTS),
        partner.reshape(tiles, TILE_PTS),
        partner_side,
        tile_knot,
    )

    below = lax.ppermute(table, "strip", [(i, i + 1) for i in range(strips - 1)])
    above = lax.ppermute(table, "strip", [(i + 1, i) for i in range(strips - 1)])
    worked = [points]
    for hop in range(2, members, 2):
        pairs = [((member + hop) % members, member) for member in range(members)]
        worked.append(lax.ppermute(points, "tile", pairs))
    swap = [(member, member ^ 1) for member in range(members)]
    lower = [below, lax.ppermute(below, "tile", swap)]
    upper = [above, lax.ppermute(above, "tile", swap)]
    sums = gather_sums(worked, lower, upper)
    all_sums = lax.all_gather(sums, ("seg", "tile"), axis=0)
    adjusted, corrections = pl.pallas_call(
        functools.partial(step_kernel, segs, members),
        out_shape=(
            jax.ShapeDtypeStruct((3, tiles, TILE_PTS), jnp.float32),
            jax.ShapeDtypeStruct((6, 1, KNOT_DEV), jnp.float32),
        ),
        in_specs=smem(1) + vmem(2),
        out_specs=(pl.BlockSpec(memory_space=pltpu.VMEM),) * 2,
        scratch_shapes=[
            pltpu.VMEM((8 * SUM_ROWS, KNOT_DEV), jnp.float32),
            pltpu.VMEM((tiles, KNOT_DEV), jnp.int32),
        ],
        compiler_params=params(6),
    )(tile_knot, all_sums, points)
    return adjusted.reshape(positions.shape), corrections.reshape(1, 6, KNOT_DEV)


def solution(mesh):
    in_specs = (
        P("strip", None, ("seg", "tile")),
        P("strip", None, ("seg", "tile")),
        P("strip", ("seg", "tile")),
        P("strip", None, ("seg", "tile")),
        P("strip", ("seg", "tile")),
        P("strip", ("seg", "tile")),
        P("strip", ("seg", "tile")),
    )
    out_specs = (P("strip", None, ("seg", "tile")), P("strip", None, "seg"))
    return jax.shard_map(local, mesh=mesh, in_specs=in_specs, out_specs=out_specs, check_vma=False)
```

```python
import functools

import jax
import jax.numpy as jnp
from jax import lax
from jax.experimental import pallas as pl
from jax.experimental.pallas import tpu as pltpu
from jax.sharding import PartitionSpec as P

KNOT_DEV = 128
TILE_PTS = 128
CHANNELS = 9
BLOCK_TILES = 4
SUM_ROWS = 80

damping = 1.0

PAIRS = [(a, b) for a in range(6) for b in range(a, 6)]


def params(mebibytes=48):
    return pltpu.CompilerParams(vmem_limit_bytes=mebibytes * 2**20)


def vmem(count):
    return [pl.BlockSpec(memory_space=pltpu.VMEM)] * count


def smem(count):
    return [pl.BlockSpec(memory_space=pltpu.SMEM)] * count


def pack_kernel(pos, cov, lever, time, partner, sides, knots, table_ref, points_ref, ints, small, sems):
    tiles = time.shape[0]
    base = 14 * tiles

    def span(first, count):
        return points_ref.at[pl.ds(first * tiles, count * tiles)]

    copies = [
        pltpu.make_async_copy(pos, table_ref.at[pl.ds(0, 3)], sems.at[0]),
        pltpu.make_async_copy(cov, table_ref.at[pl.ds(3, 6)], sems.at[1]),
        pltpu.make_async_copy(partner, ints, sems.at[2]),
        pltpu.make_async_copy(sides, small.at[0], sems.at[3]),
        pltpu.make_async_copy(knots, small.at[1], sems.at[4]),
        pltpu.make_async_copy(time, span(12, 1), sems.at[5]),
    ]
    copies += [
        pltpu.make_async_copy(lever.at[c], span(9 + c, 1), sems.at[6 + c]) for c in range(3)
    ]
    for copy in copies:
        copy.start()
    for copy in copies:
        copy.wait()
    for channel in range(CHANNELS):
        points_ref[channel * tiles : (channel + 1) * tiles, :] = table_ref[channel]
    points_ref[13 * tiles : 14 * tiles, :] = ints[...].astype(jnp.float32)
    for place in range(2):
        row = base + place
        points_ref[row : row + 1, 0:tiles] = small[place].astype(jnp.float32)


def split_two(value):
    high = value.astype(jnp.bfloat16)
    low = (value - high.astype(jnp.float32)).astype(jnp.bfloat16)
    return high, low


def list_tiles(names, tiles, order_ref, sides):
    count = len(names) * tiles
    room = order_ref.shape[0] // len(sides)
    starts = [jnp.int32(place * room) for place in range(len(sides))]
    ends = list(starts)
    for tile in range(count):
        side = names[tile // tiles][0, tile % tiles]
        for place in range(len(sides)):
            order_ref[ends[place]] = tile
            ends[place] = ends[place] + (side == sides[place]).astype(jnp.int32)
    blocks = []
    for start, end in zip(starts, ends):
        last = order_ref[jnp.maximum(end - 1, start)]
        for extra in range(BLOCK_TILES):
            order_ref[end + extra] = last
        blocks.append(lax.shift_right_logical(end - start + BLOCK_TILES - 1, 2))
    return blocks, room


def weigh_tables(tables, weights, slot):
    tiles = tables[0].shape[1]
    for place in range(2):
        for channel in range(CHANNELS):
            high, low = split_two(tables[place][channel])
            rows = slice(channel * tiles, (channel + 1) * tiles)
            at = place * TILE_PTS
            weights[slot, rows, at : at + TILE_PTS] = high
            weights[slot, rows, at + 2 * TILE_PTS : at + 3 * TILE_PTS] = low


def near_kernel(points, first, second, weights, target, *work):
    picking = start_picks((points,), work)
    weigh_tables((first, second), weights, 0)
    target[...] = jnp.zeros_like(target)
    picks((points,), weights, (0,), target, picking, work)


def far_kernel(points, first, second, near_weights, found, weights, totals_ref, *work):
    target, live_ref, knot_ref, parts_ref = work[:4]
    work = work[4:]
    picking = start_picks((points,), work)
    weights[0] = near_weights[0]
    weigh_tables((first, second), weights, 1)
    target[...] = found[...]
    picks((points,), weights, (1,), target, picking, work)
    add_points((points,), target, work, live_ref, knot_ref, totals_ref, parts_ref)


def other_kernel(groups, *refs):
    points = refs[:groups]
    weights, before_ref, sums_ref, totals_ref = refs[groups : groups + 4]
    target, live_ref, knot_ref, parts_ref = refs[groups + 4 : groups + 8]
    work = refs[groups + 8 :]
    picking = start_picks(points, work)
    target[...] = jnp.zeros_like(target)
    picks(points, weights, (0, 1), target, picking, work)
    add_points(points, target, work, live_ref, knot_ref, totals_ref, parts_ref)
    for place in range(SUM_ROWS):
        if place < 75:
            rows = slice(place * 8, (place + 1) * 8)
            value = totals_ref[rows, :] + before_ref[rows, :]
            sums_ref[place : place + 1, :] = jnp.sum(value, axis=0, keepdims=True)
        else:
            sums_ref[place : place + 1, :] = jnp.zeros((1, KNOT_DEV), jnp.float32)


def start_picks(points, work):
    sems, names = work[3], work[4:]
    base = points[0].shape[0] - 8
    copies = [
        pltpu.make_async_copy(points[p].at[pl.ds(base, 8)], names[p], sems.at[p])
        for p in range(len(points))
    ]
    for copy in copies:
        copy.start()
    return copies


def picks(points, weights, slots, target, copies, work):
    key_ref, row_ref, order_ref = work[:3]
    names = work[4:]
    tiles = weights.shape[1] // CHANNELS
    member = lax.axis_index("tile")
    near = jnp.where(lax.axis_index("strip") % 2 == 1, 0.0, 1.0)
    sides = [(near, 1.0 - near)[slot] for slot in slots]
    for p in range(len(points)):
        index = points[p][13 * tiles : 14 * tiles, :].astype(jnp.int32)
        point_row = lax.shift_right_logical(index, 7)
        lane = index & (TILE_PTS - 1)
        key = lane
        row = jnp.full_like(index, -1)
        for place in range(2):
            offset = point_row - (member ^ place) * tiles
            inside = (offset >= 0) & (offset < tiles)
            key = jnp.where(inside, lane + place * TILE_PTS, key)
            row = jnp.where(inside, offset, row)
        key_ref[p * tiles : (p + 1) * tiles, :] = key
        row_ref[p * tiles : (p + 1) * tiles, :] = row
    for copy in copies:
        copy.wait()
    counts, room = list_tiles(names, tiles, order_ref, sides)
    blocks = sum(counts)
    queries = BLOCK_TILES * TILE_PTS

    def one_block(block):
        block = jnp.minimum(block, blocks - 1)
        if len(slots) == 1:
            slot = slots[0]
            start = block * BLOCK_TILES
        else:
            second = block >= counts[0]
            slot = second.astype(jnp.int32)
            start = jnp.where(second, room + (block - counts[0]) * BLOCK_TILES, block * BLOCK_TILES)
        ids = [order_ref[start + j] for j in range(BLOCK_TILES)]
        keys = jnp.concatenate([key_ref[pl.ds(i, 1), :] for i in ids], axis=1)
        rows = jnp.concatenate([row_ref[pl.ds(i, 1), :] for i in ids], axis=1)
        hot = jnp.where(
            lax.broadcasted_iota(jnp.int32, (2 * TILE_PTS, queries), 0) == keys, 1.0, 0.0
        ).astype(jnp.bfloat16)
        picked = jnp.dot(
            weights[slot], jnp.concatenate([hot, hot], axis=0), preferred_element_type=jnp.float32
        )
        spread_rows = jnp.broadcast_to(rows, (8, queries))
        eight = lax.broadcasted_iota(jnp.int32, (8, queries), 0)
        found = [jnp.zeros((8, queries), jnp.float32) for _ in range(CHANNELS)]
        for step in range(tiles // 8):
            here = spread_rows == eight + 8 * step
            for channel in range(CHANNELS):
                begin = channel * tiles + 8 * step
                found[channel] = jnp.where(here, picked[begin : begin + 8], found[channel])
        return ids, [jnp.sum(entry, axis=0, keepdims=True) for entry in found]

    def body(step, carry):
        results = [one_block(2 * step), one_block(2 * step + 1)]
        for ids, flat in results:
            for channel in range(CHANNELS):
                for j in range(BLOCK_TILES):
                    piece = flat[channel][:, j * TILE_PTS : (j + 1) * TILE_PTS]
                    target[channel, pl.ds(ids[j], 1), :] = piece
        return carry

    lax.fori_loop(0, lax.shift_right_logical(blocks + 1, 1), body, 0)


def add_points(points, target, work, live_ref, knot_ref, totals_ref, parts_ref):
    row_ref, names = work[1], work[4:]
    tiles = target.shape[1] // len(points)
    for p in range(len(points)):
        for tile in range(tiles):
            at = p * tiles + tile
            live = (names[p][0, tile] != 2.0).astype(jnp.float32)
            live_ref[at : at + 1, :] = jnp.full((1, TILE_PTS), live, jnp.float32)
            knot_ref[at : at + 1, :] = jnp.full((1, KNOT_DEV), names[p][1, tile], jnp.float32)
    totals_ref[...] = jnp.zeros_like(totals_ref)
    for p in range(len(points)):
        sum_points(p, tiles, points[p], target, row_ref, live_ref, knot_ref, totals_ref, parts_ref)


def sum_points(p, tiles, points, target, row_ref, live_ref, knot_ref, totals_ref, parts_ref):
    group = 16
    ones = jnp.ones((2 * TILE_PTS, KNOT_DEV), jnp.bfloat16)

    def body(step, carry):
        begin = pl.multiple_of(step * group, group)
        span = pl.ds(pl.multiple_of(p * tiles + begin, group), group)

        def own(channel):
            return points[pl.ds(pl.multiple_of(channel * tiles + begin, group), group), :]

        live = jnp.where(row_ref[span, :] >= 0, live_ref[span, :], 0.0)
        m = [own(3 + c) + target[3 + c, span, :] for c in range(6)]
        residual = [own(c) - target[c, span, :] for c in range(3)]
        lever = [own(9 + c) for c in range(3)]
        later = own(12)
        early = 1.0 - later
        adjunct = [
            m[1] * m[2] - m[5] * m[5],
            m[0] * m[2] - m[4] * m[4],
            m[0] * m[1] - m[3] * m[3],
            m[4] * m[5] - m[3] * m[2],
            m[3] * m[5] - m[4] * m[1],
            m[3] * m[4] - m[0] * m[5],
        ]
        determinant = m[0] * adjunct[0] + m[3] * adjunct[3] + m[4] * adjunct[4]
        scale = live / determinant
        inv = [entry * scale for entry in adjunct]
        info = [[inv[0], inv[3], inv[4]], [inv[3], inv[1], inv[5]], [inv[4], inv[5], inv[2]]]

        def turned(column):
            return [
                lever[1] * column[2] - lever[2] * column[1],
                lever[2] * column[0] - lever[0] * column[2],
                lever[0] * column[1] - lever[1] * column[0],
            ] + list(column)

        weighted = [turned(info[i]) for i in range(3)]
        pulled = [
            info[i][0] * residual[0] + info[i][1] * residual[1] + info[i][2] * residual[2]
            for i in range(3)
        ]
        gradient = turned(pulled)
        gram = {}
        for b in range(6):
            column = turned([weighted[i][b] for i in range(3)])
            for a in range(b + 1):
                gram[a, b] = column[a]
        both = early * later
        terms = []
        for weight in (early * early, both, later * later):
            terms += [gram[pair] * weight for pair in PAIRS]
        for weight in (early, later):
            terms += [entry * weight for entry in gradient]
        for place, term in enumerate(terms):
            rows = slice(place * group, (place + 1) * group)
            high, low = split_two(term)
            parts_ref[rows, 0:TILE_PTS] = high
            parts_ref[rows, TILE_PTS : 2 * TILE_PTS] = low
        tile_sums = jnp.dot(parts_ref[...], ones, preferred_element_type=jnp.float32)
        lanes = lax.broadcasted_iota(jnp.int32, (group, KNOT_DEV), 1).astype(jnp.float32)
        chosen = knot_ref[span, :] == lanes
        for place in range(len(terms)):
            piece = jnp.where(chosen, tile_sums[place * group : (place + 1) * group], 0.0)
            rows = slice(place * 8, (place + 1) * 8)
            totals_ref[rows, :] = totals_ref[rows, :] + piece[0:8] + piece[8:16]
        return carry

    lax.fori_loop(0, tiles // group, body, 0)


def work_shapes(groups, tiles, slots, adding):
    count = groups * tiles
    found = [
        pltpu.VMEM((CHANNELS, count, TILE_PTS), jnp.float32),
        pltpu.VMEM((count, TILE_PTS), jnp.float32),
        pltpu.VMEM((count, KNOT_DEV), jnp.float32),
        pltpu.VMEM((75 * 16, 2 * TILE_PTS), jnp.bfloat16),
    ]
    picked = [
        pltpu.VMEM((count, TILE_PTS), jnp.int32),
        pltpu.VMEM((count, TILE_PTS), jnp.int32),
        pltpu.SMEM((slots * (count + 2 * BLOCK_TILES),), jnp.int32),
        pltpu.SemaphoreType.DMA((groups,)),
    ] + [pltpu.SMEM((8, TILE_PTS), jnp.float32) for _ in range(groups)]
    return found + picked if adding else picked


def weight_shape(slots, tiles):
    return jax.ShapeDtypeStruct((slots, CHANNELS * tiles, 4 * TILE_PTS), jnp.bfloat16)


def near_picks(points, near):
    tiles = near[0].shape[1]
    return pl.pallas_call(
        near_kernel,
        out_shape=(
            weight_shape(1, tiles),
            jax.ShapeDtypeStruct((CHANNELS, tiles, TILE_PTS), jnp.float32),
        ),
        in_specs=vmem(3),
        out_specs=(pl.BlockSpec(memory_space=pltpu.VMEM),) * 2,
        scratch_shapes=work_shapes(1, tiles, 1, False),
        compiler_params=params(14),
    )(points, *near)


def own_totals(points, far, weights, found):
    tiles = far[0].shape[1]
    return pl.pallas_call(
        far_kernel,
        out_shape=(
            weight_shape(2, tiles),
            jax.ShapeDtypeStruct((75 * 8, KNOT_DEV), jnp.float32),
        ),
        in_specs=vmem(5),
        out_specs=(pl.BlockSpec(memory_space=pltpu.VMEM),) * 2,
        scratch_shapes=work_shapes(1, tiles, 1, True),
        compiler_params=params(14),
    )(points, *far, weights, found)


def all_totals(points, weights, totals):
    groups = len(points)
    tiles = weights.shape[1] // CHANNELS
    return pl.pallas_call(
        functools.partial(other_kernel, groups),
        out_shape=jax.ShapeDtypeStruct((SUM_ROWS, KNOT_DEV), jnp.float32),
        in_specs=vmem(groups + 2),
        out_specs=pl.BlockSpec(memory_space=pltpu.VMEM),
        scratch_shapes=[pltpu.VMEM((75 * 8, KNOT_DEV), jnp.float32)] + work_shapes(groups, tiles, 2, True),
        compiler_params=params(14),
    )(*points, weights, totals)


def cholesky(matrix):
    factor = {}
    inverse = []
    for column in range(6):
        pivot = matrix[column, column]
        for inner in range(column):
            pivot = pivot - factor[column, inner] * factor[column, inner]
        inverse.append(1.0 / jnp.sqrt(pivot))
        for row in range(column + 1, 6):
            entry = matrix[column, row]
            for inner in range(column):
                entry = entry - factor[row, inner] * factor[column, inner]
            factor[row, column] = entry * inverse[column]
    return factor, inverse


def solve(system, right_side):
    factor, inverse = system
    forward = []
    for row in range(6):
        entry = right_side[row]
        for inner in range(row):
            entry = entry - factor[row, inner] * forward[inner]
        forward.append(entry * inverse[row])
    answer = [None] * 6
    for row in reversed(range(6)):
        entry = forward[row]
        for inner in range(row + 1, 6):
            entry = entry - factor[inner, row] * answer[inner]
        answer[row] = entry * inverse[row]
    return answer


def step_kernel(segs, members, knot_ref, sums_ref, points_ref, adjusted_ref, out_ref, held, index_ref):
    tiles = knot_ref.shape[1]
    for tile in range(tiles):
        index_ref[tile : tile + 1, :] = jnp.full((1, KNOT_DEV), knot_ref[0, tile], jnp.int32)
    seg = lax.axis_index("seg")
    for place in range(3):
        wanted = seg + place - 1
        there = (wanted >= 0) & (wanted < segs)
        first = jnp.minimum(jnp.maximum(wanted, 0), segs - 1) * members
        total = sums_ref[first]
        for other in range(1, members):
            total = total + sums_ref[first + other]
        held[place * SUM_ROWS : (place + 1) * SUM_ROWS, :] = jnp.where(there, total, 0.0)
    for place in range(3, 8):
        held[place * SUM_ROWS : (place + 1) * SUM_ROWS, :] = jnp.zeros(
            (SUM_ROWS, KNOT_DEV), jnp.float32
        )
    shape = (8, KNOT_DEV)
    lanes = lax.broadcasted_iota(jnp.int32, shape, 1)
    rows = lax.broadcasted_iota(jnp.int32, shape, 0)

    def earlier(value):
        turned = pltpu.roll(value, 1, 1)
        return jnp.where(lanes == 0, pltpu.roll(turned, 1, 0), turned)

    def following(value):
        turned = pltpu.roll(value, KNOT_DEV - 1, 1)
        return jnp.where(lanes == KNOT_DEV - 1, pltpu.roll(turned, 7, 0), turned)

    def quantity(place):
        return held[pl.ds(place, 8, stride=SUM_ROWS), :]

    pair_place = {pair: place for place, pair in enumerate(PAIRS)}
    matrix, cross, cross_before = {}, {}, {}
    for pair, place in pair_place.items():
        value = quantity(place) + earlier(quantity(42 + place))
        matrix[pair] = value + damping if pair[0] == pair[1] else value
        cross[pair] = quantity(21 + place)
        cross_before[pair] = earlier(cross[pair])
    right_side = [quantity(63 + a) + earlier(quantity(69 + a)) for a in range(6)]
    system = cholesky(matrix)
    beyond = (rows >= 2) & (seg == segs - 1)
    first = [jnp.where(beyond, 0.0, -entry) for entry in solve(system, right_side)]
    before = [earlier(entry) for entry in first]
    after = [following(entry) for entry in first]
    corrected = []
    for a in range(6):
        total = right_side[a]
        for b in range(6):
            pair = (min(a, b), max(a, b))
            total = total + cross_before[pair] * before[b] + cross[pair] * after[b]
        corrected.append(total)
    second = [jnp.where(beyond, 0.0, -entry) for entry in solve(system, corrected)]
    upper = [following(entry) for entry in second]
    for a in range(6):
        out_ref[a] = second[a][1:2]
    low_rows = [jnp.broadcast_to(second[a][1:2], shape) for a in range(6)]
    high_rows = [jnp.broadcast_to(upper[a][1:2], shape) for a in range(6)]
    for begin in range(0, tiles, 8):
        span = slice(begin, begin + 8)
        knots = index_ref[span, :]
        later = points_ref[12 * tiles + begin : 12 * tiles + begin + 8, :]
        early = 1.0 - later
        pose = []
        for a in range(6):
            low = jnp.take_along_axis(low_rows[a], knots, axis=1, mode="promise_in_bounds")
            high = jnp.take_along_axis(high_rows[a], knots, axis=1, mode="promise_in_bounds")
            pose.append(early * low + later * high)
        lever = [
            points_ref[c * tiles + begin : c * tiles + begin + 8, :] for c in range(9, 12)
        ]
        moved = [
            pose[1] * lever[2] - pose[2] * lever[1] + pose[3],
            pose[2] * lever[0] - pose[0] * lever[2] + pose[4],
            pose[0] * lever[1] - pose[1] * lever[0] + pose[5],
        ]
        for c in range(3):
            coords = points_ref[c * tiles + begin : c * tiles + begin + 8, :]
            adjusted_ref[c, span, :] = coords + moved[c]


def local(positions, lever_arm, spline_time, covariance, partner, partner_side, tile_knot):
    tiles = positions.shape[2] // TILE_PTS
    strips = lax.axis_size("strip")
    members = lax.axis_size("tile")
    segs = lax.axis_size("seg")

    table, points = pl.pallas_call(
        pack_kernel,
        out_shape=(
            jax.ShapeDtypeStruct((CHANNELS, tiles, TILE_PTS), jnp.float32),
            jax.ShapeDtypeStruct((14 * tiles + 8, TILE_PTS), jnp.float32),
        ),
        in_specs=[pl.BlockSpec(memory_space=pltpu.HBM)] * 7,
        out_specs=(pl.BlockSpec(memory_space=pltpu.VMEM),) * 2,
        scratch_shapes=[
            pltpu.VMEM((tiles, TILE_PTS), jnp.int32),
            pltpu.VMEM((2, 1, tiles), jnp.int32),
            pltpu.SemaphoreType.DMA((9,)),
        ],
        compiler_params=params(14),
    )(
        *[
            pltpu.with_memory_space_constraint(array, pltpu.HBM)
            for array in (
                positions.reshape(3, tiles, TILE_PTS),
                covariance.reshape(6, tiles, TILE_PTS),
                lever_arm.reshape(3, tiles, TILE_PTS),
                spline_time.reshape(tiles, TILE_PTS),
                partner.reshape(tiles, TILE_PTS),
                partner_side,
                tile_knot,
            )
        ]
    )

    def trade(first):
        pairs = []
        for strip in range(first, strips - 1, 2):
            pairs += [(strip, strip + 1), (strip + 1, strip)]
        return lax.ppermute(table, "strip", pairs)

    near, far = trade(0), trade(1)
    others = []
    for hop in range(2, members, 2):
        pairs = [((member + hop) % members, member) for member in range(members)]
        others.append(lax.ppermute(points, "tile", pairs))
    swap = [(member, member ^ 1) for member in range(members)]
    near = [near, lax.ppermute(near, "tile", swap)]
    far = [far, lax.ppermute(far, "tile", swap)]
    weights, found = near_picks(points, near)
    weights, totals = own_totals(points, far, weights, found)
    sums = all_totals(others, weights, totals)
    all_sums = lax.all_gather(sums, ("seg", "tile"), axis=0)
    adjusted, corrections = pl.pallas_call(
        functools.partial(step_kernel, segs, members),
        out_shape=(
            jax.ShapeDtypeStruct((3, tiles, TILE_PTS), jnp.float32),
            jax.ShapeDtypeStruct((6, 1, KNOT_DEV), jnp.float32),
        ),
        in_specs=smem(1) + vmem(2),
        out_specs=(pl.BlockSpec(memory_space=pltpu.VMEM),) * 2,
        scratch_shapes=[
            pltpu.VMEM((8 * SUM_ROWS, KNOT_DEV), jnp.float32),
            pltpu.VMEM((tiles, KNOT_DEV), jnp.int32),
        ],
        compiler_params=params(6),
    )(tile_knot, all_sums, points)
    return adjusted.reshape(positions.shape), corrections.reshape(1, 6, KNOT_DEV)


def solution(mesh):
    in_specs = (
        P("strip", None, ("seg", "tile")),
        P("strip", None, ("seg", "tile")),
        P("strip", ("seg", "tile")),
        P("strip", None, ("seg", "tile")),
        P("strip", ("seg", "tile")),
        P("strip", ("seg", "tile")),
        P("strip", ("seg", "tile")),
    )
    out_specs = (P("strip", None, ("seg", "tile")), P("strip", None, "seg"))
    return jax.shard_map(local, mesh=mesh, in_specs=in_specs, out_specs=out_specs, check_vma=False)
```

```python
import functools

import jax
import jax.numpy as jnp
from jax import lax
from jax.experimental import pallas as pl
from jax.experimental.pallas import tpu as pltpu
from jax.sharding import PartitionSpec as P

KNOT_DEV = 128
TILE_PTS = 128
CHANNELS = 9
BLOCK_TILES = 4
ROW_GROUP = 16
POINT_ROWS = 16
PARTNER = 13
KNOT = 14
SIDE = 15
VALID = 15
SUM_ROWS = 80

damping = 1.0

PAIRS = [(a, b) for a in range(6) for b in range(a, 6)]


def params(mebibytes=48):
    return pltpu.CompilerParams(vmem_limit_bytes=mebibytes * 2**20)


def vmem(count):
    return [pl.BlockSpec(memory_space=pltpu.VMEM)] * count


def smem(count):
    return [pl.BlockSpec(memory_space=pltpu.SMEM)] * count


def pack_kernel(pos, cov, lever, time, partner, sides, knots, table_ref, points_ref, ints, small, sems):
    tiles = time.shape[0]
    copies = [
        pltpu.make_async_copy(sides, small.at[0], sems.at[0]),
        pltpu.make_async_copy(knots, small.at[1], sems.at[1]),
        pltpu.make_async_copy(partner, ints, sems.at[2]),
        pltpu.make_async_copy(pos, table_ref.at[pl.ds(0, 3)], sems.at[3]),
        pltpu.make_async_copy(cov, table_ref.at[pl.ds(3, 6)], sems.at[4]),
        pltpu.make_async_copy(lever, points_ref.at[pl.ds(9, 3)], sems.at[5]),
        pltpu.make_async_copy(time, points_ref.at[12], sems.at[6]),
    ]
    for copy in copies:
        copy.start()
    for copy in copies:
        copy.wait()
    points_ref[0:CHANNELS] = table_ref[...]
    points_ref[PARTNER] = ints[...].astype(jnp.float32)
    for place, channel in ((0, SIDE), (1, KNOT)):
        for tile in range(tiles):
            value = jnp.full((1, TILE_PTS), small[place, 0, tile], jnp.int32)
            points_ref[channel, tile : tile + 1, :] = value.astype(jnp.float32)


def split_two(value):
    high = value.astype(jnp.bfloat16)
    low = (value - high.astype(jnp.float32)).astype(jnp.bfloat16)
    return high, low


def row_room(groups, tiles):
    return groups * tiles + 4 * ROW_GROUP


def arrange(points, packed, work):
    compact, numbers, counts, sems = work
    tiles = points[0].shape[1]
    upper = (
        lax.broadcasted_iota(jnp.int32, (TILE_PTS, TILE_PTS), 0)
        <= lax.broadcasted_iota(jnp.int32, (TILE_PTS, TILE_PTS), 1)
    )
    upper = jnp.where(upper, 1.0, 0.0).astype(jnp.bfloat16)
    member = lax.axis_index("tile")
    near = jnp.where(lax.axis_index("strip") % 2 == 1, 0.0, 1.0)
    copies = []
    for p, group in enumerate(points):
        index = group[PARTNER].astype(jnp.int32)
        offset = lax.shift_right_logical(index, 7) - member * tiles
        side = group[SIDE]
        wanted = (offset >= 0) & (offset < tiles) & (side != 2.0)
        marks = jnp.where(wanted, 1.0, 0.0).astype(jnp.bfloat16)
        ranks = jnp.dot(marks, upper, preferred_element_type=jnp.float32).astype(jnp.int32)
        numbers[p * tiles : (p + 1) * tiles, :] = ranks + jnp.where(side == near, 0, 256)
        span = pl.ds(p * tiles, tiles)
        copies.append(pltpu.make_async_copy(numbers.at[span], counts.at[span], sems.at[p]))
    for copy in copies:
        copy.start()
    lanes = lax.broadcasted_iota(jnp.int32, (tiles, TILE_PTS), 1)
    for p, group in enumerate(points):
        ranks = numbers[p * tiles : (p + 1) * tiles, :] & 255
        source = jnp.zeros_like(lanes)
        for jump in (64, 32, 16, 8, 4, 2, 1):
            there = jnp.take_along_axis(ranks, source + (jump - 1), axis=1, mode="promise_in_bounds")
            source = jnp.where(there <= lanes, source + jump, source)
        count = jnp.broadcast_to(ranks[:, TILE_PTS - 1 :], lanes.shape)
        for channel in range(POINT_ROWS):
            if channel == VALID:
                value = jnp.where(lanes < count, 1.0, 0.0)
            else:
                value = group[channel]
                if channel != KNOT:
                    value = jnp.take_along_axis(value, source, axis=1, mode="promise_in_bounds")
            at = p * tiles * POINT_ROWS + channel
            compact[pl.ds(at, tiles, stride=POINT_ROWS), :] = value
    for copy in copies:
        copy.wait()

    room = packed.shape[0] // POINT_ROWS
    last = room - 1
    blank = jnp.zeros((POINT_ROWS, TILE_PTS), jnp.float32)

    def rows_at(row):
        return pl.ds(pl.multiple_of(row * POINT_ROWS, POINT_ROWS), POINT_ROWS)

    packed[rows_at(0), :] = blank
    packed[rows_at(last), :] = blank
    wide = lax.broadcasted_iota(jnp.int32, (POINT_ROWS, TILE_PTS), 1)

    def place(tile, carry):
        near_row, near_start, far_row, far_start = carry
        code = counts[tile, TILE_PTS - 1]
        count = code & 255
        far = code >= 256
        row = jnp.where(far, far_row, near_row)
        start = jnp.where(far, far_start, near_start)
        full = start + count > TILE_PTS
        row = jnp.where(full, row + 1, row)
        start = jnp.where(full, 0, start)
        at = rows_at(jnp.where(far, last - row, row))
        value = pltpu.roll(compact[rows_at(tile), :], start, 1)
        packed[at, :] = jnp.where(wide >= start, value, packed[at, :])
        end = start + count
        return (
            jnp.where(far, near_row, row),
            jnp.where(far, near_start, end),
            jnp.where(far, row, far_row),
            jnp.where(far, end, far_start),
        )

    zero = jnp.int32(0)
    total = len(points) * tiles
    unroll = 8

    def several(step, carry):
        for tile in range(unroll):
            carry = place(step * unroll + tile, carry)
        return carry

    near_row, near_start, far_row, far_start = lax.fori_loop(
        0, total // unroll, several, (zero, zero, zero, zero)
    )
    near_rows = near_row + (near_start > 0).astype(jnp.int32)
    far_rows = far_row + (far_start > 0).astype(jnp.int32)
    for extra in range(ROW_GROUP):
        packed[rows_at(near_rows + extra), :] = blank
        packed[rows_at(last - far_rows - extra), :] = blank
    return near_rows, far_rows


def weigh_table(table, weights, slot):
    tiles = table.shape[1]
    for channel in range(CHANNELS):
        high, low = split_two(table[channel])
        rows = slice(channel * tiles, (channel + 1) * tiles)
        weights[slot, rows, 0:TILE_PTS] = high
        weights[slot, rows, TILE_PTS : 2 * TILE_PTS] = low


def process(packed, near_rows, far_rows, weights, totals_ref, work):
    target, key_ref, row_ref, terms_ref = work
    tiles = weights.shape[1] // CHANNELS
    room = packed.shape[0] // POINT_ROWS
    member = lax.axis_index("tile")

    def keys(step, carry):
        begin = pl.multiple_of(step * 8, 8)
        span = pl.ds(begin, 8)

        def channel(place):
            return packed[pl.ds(begin * POINT_ROWS + place, 8, stride=POINT_ROWS), :]

        index = channel(PARTNER).astype(jnp.int32)
        key_ref[span, :] = index & (TILE_PTS - 1)
        row = lax.shift_right_logical(index, 7) - member * tiles
        row_ref[span, :] = jnp.where(channel(VALID) > 0.0, row, -1)
        return carry

    lax.fori_loop(0, room // 8, keys, 0)
    target[...] = jnp.zeros_like(target)
    near_blocks = lax.shift_right_logical(near_rows + BLOCK_TILES - 1, 2)
    far_blocks = lax.shift_right_logical(far_rows + BLOCK_TILES - 1, 2)
    blocks = near_blocks + far_blocks
    queries = BLOCK_TILES * TILE_PTS

    def one_block(block):
        block = jnp.minimum(block, blocks - 1)
        far = block >= near_blocks
        slot = far.astype(jnp.int32)
        base = jnp.where(far, room - BLOCK_TILES * (block - near_blocks + 1), block * BLOCK_TILES)
        ids = [base + j for j in range(BLOCK_TILES)]
        keys = jnp.concatenate([key_ref[pl.ds(i, 1), :] for i in ids], axis=1)
        rows = jnp.concatenate([row_ref[pl.ds(i, 1), :] for i in ids], axis=1)
        hot = jnp.where(
            lax.broadcasted_iota(jnp.int32, (TILE_PTS, queries), 0) == keys, 1.0, 0.0
        ).astype(jnp.bfloat16)
        picked = jnp.dot(
            weights[slot], jnp.concatenate([hot, hot], axis=0), preferred_element_type=jnp.float32
        )
        spread_rows = jnp.broadcast_to(rows, (8, queries))
        eight = lax.broadcasted_iota(jnp.int32, (8, queries), 0)
        found = [jnp.zeros((8, queries), jnp.float32) for _ in range(CHANNELS)]
        for step in range(tiles // 8):
            here = spread_rows == eight + 8 * step
            for channel in range(CHANNELS):
                begin = channel * tiles + 8 * step
                found[channel] = jnp.where(here, picked[begin : begin + 8], found[channel])
        return ids, [jnp.sum(entry, axis=0, keepdims=True) for entry in found]

    def body(step, carry):
        results = [one_block(2 * step), one_block(2 * step + 1)]
        for ids, flat in results:
            for channel in range(CHANNELS):
                for j in range(BLOCK_TILES):
                    piece = flat[channel][:, j * TILE_PTS : (j + 1) * TILE_PTS]
                    target[channel, pl.ds(ids[j], 1), :] = piece
        return carry

    lax.fori_loop(0, lax.shift_right_logical(blocks + 1, 1), body, 0)

    totals_ref[...] = jnp.zeros_like(totals_ref)
    terms_ref[75 * ROW_GROUP :, :] = jnp.zeros((5 * ROW_GROUP, TILE_PTS), jnp.float32)
    near_groups = lax.shift_right_logical(near_rows + ROW_GROUP - 1, 4)
    far_groups = lax.shift_right_logical(far_rows + ROW_GROUP - 1, 4)

    def add(step, carry):
        far = step >= near_groups
        base = jnp.where(far, room - ROW_GROUP * (step - near_groups + 1), step * ROW_GROUP)
        add_rows(pl.multiple_of(base, ROW_GROUP), packed, target, totals_ref, terms_ref)
        return carry

    lax.fori_loop(0, near_groups + far_groups, add, 0)


def add_rows(base, packed, target, totals_ref, terms_ref):
    group = ROW_GROUP
    span = pl.ds(base, group)

    def own(channel):
        return packed[pl.ds(base * POINT_ROWS + channel, group, stride=POINT_ROWS), :]

    valid = own(VALID) > 0.0
    m = [own(3 + c) + target[3 + c, span, :] for c in range(6)]
    residual = [own(c) - target[c, span, :] for c in range(3)]
    lever = [own(9 + c) for c in range(3)]
    later = own(12)
    early = 1.0 - later
    adjunct = [
        m[1] * m[2] - m[5] * m[5],
        m[0] * m[2] - m[4] * m[4],
        m[0] * m[1] - m[3] * m[3],
        m[4] * m[5] - m[3] * m[2],
        m[3] * m[5] - m[4] * m[1],
        m[3] * m[4] - m[0] * m[5],
    ]
    determinant = m[0] * adjunct[0] + m[3] * adjunct[3] + m[4] * adjunct[4]
    scale = jnp.where(valid, 1.0 / determinant, 0.0)
    inv = [entry * scale for entry in adjunct]
    info = [[inv[0], inv[3], inv[4]], [inv[3], inv[1], inv[5]], [inv[4], inv[5], inv[2]]]

    def turned(column):
        return [
            lever[1] * column[2] - lever[2] * column[1],
            lever[2] * column[0] - lever[0] * column[2],
            lever[0] * column[1] - lever[1] * column[0],
        ] + list(column)

    weighted = [turned(info[i]) for i in range(3)]
    pulled = [
        info[i][0] * residual[0] + info[i][1] * residual[1] + info[i][2] * residual[2]
        for i in range(3)
    ]
    gradient = turned(pulled)
    gram = {}
    for b in range(6):
        column = turned([weighted[i][b] for i in range(3)])
        for a in range(b + 1):
            gram[a, b] = column[a]
    both = early * later
    terms = []
    for weight in (early * early, both, later * later):
        terms += [gram[pair] * weight for pair in PAIRS]
    for weight in (early, later):
        terms += [entry * weight for entry in gradient]
    for place, term in enumerate(terms):
        terms_ref[place * group : (place + 1) * group, :] = term
    knots = own(KNOT).astype(jnp.int32)
    stacked = lax.broadcasted_iota(jnp.int32, (KNOT_DEV, TILE_PTS), 0)
    total = totals_ref[...]
    for row in range(0, group, 2):
        parts, hots = [], []
        for r in (row, row + 1):
            high, low = split_two(terms_ref[pl.ds(r, SUM_ROWS, stride=group), :])
            parts.append(jnp.concatenate([high, low], axis=0))
            hots.append(jnp.where(stacked == knots[r : r + 1], 1.0, 0.0).astype(jnp.bfloat16))
        sums = lax.dot_general(
            jnp.concatenate(parts, axis=1),
            jnp.concatenate(hots, axis=1),
            (((1,), (1,)), ((), ())),
            preferred_element_type=jnp.float32,
        )
        total = total + sums[0:SUM_ROWS] + sums[SUM_ROWS:]
    totals_ref[...] = total


def early_kernel(groups, *refs):
    points = refs[:groups]
    packed, rows_ref = refs[groups : groups + 2]
    near_rows, far_rows = arrange(points, packed, refs[groups + 2 :])
    rows_ref[0:4, :] = jnp.full((4, TILE_PTS), near_rows, jnp.int32)
    rows_ref[4:8, :] = jnp.full((4, TILE_PTS), far_rows, jnp.int32)


def own_kernel(packed, rows_ref, near, far, weights, totals_ref, rows_here, sem, *work):
    copy = pltpu.make_async_copy(rows_ref, rows_here, sem.at[0])
    copy.start()
    weigh_table(near, weights, 0)
    weigh_table(far, weights, 1)
    copy.wait()
    process(packed, rows_here[0, 0], rows_here[4, 0], weights, totals_ref, work)


def other_kernel(groups, *refs):
    points = refs[:groups]
    weights, before_ref, totals_ref, packed = refs[groups : groups + 4]
    arranging, work = refs[groups + 4 : groups + 8], refs[groups + 8 :]
    near_rows, far_rows = arrange(points, packed, arranging)
    process(packed, near_rows, far_rows, weights, totals_ref, work)
    totals_ref[...] = totals_ref[...] + before_ref[...]


def arrange_shapes(groups, tiles):
    count = groups * tiles
    return [
        pltpu.VMEM((count * POINT_ROWS, TILE_PTS), jnp.float32),
        pltpu.VMEM((count, TILE_PTS), jnp.int32),
        pltpu.SMEM((count, TILE_PTS), jnp.int32),
        pltpu.SemaphoreType.DMA((groups,)),
    ]


def process_shapes(groups, tiles):
    room = row_room(groups, tiles)
    return [
        pltpu.VMEM((CHANNELS, room, TILE_PTS), jnp.float32),
        pltpu.VMEM((room, TILE_PTS), jnp.int32),
        pltpu.VMEM((room, TILE_PTS), jnp.int32),
        pltpu.VMEM((SUM_ROWS * ROW_GROUP, TILE_PTS), jnp.float32),
    ]


def packed_shape(groups, tiles):
    return (row_room(groups, tiles) * POINT_ROWS, TILE_PTS)


def early_rows(points):
    groups, tiles = len(points), points[0].shape[1]
    return pl.pallas_call(
        functools.partial(early_kernel, groups),
        out_shape=(
            jax.ShapeDtypeStruct(packed_shape(groups, tiles), jnp.float32),
            jax.ShapeDtypeStruct((8, TILE_PTS), jnp.int32),
        ),
        in_specs=vmem(groups),
        out_specs=(pl.BlockSpec(memory_space=pltpu.VMEM),) * 2,
        scratch_shapes=arrange_shapes(groups, tiles),
        compiler_params=params(14),
    )(*points)


def own_totals(groups, packed, rows, near, far):
    tiles = near.shape[1]
    return pl.pallas_call(
        own_kernel,
        out_shape=(
            jax.ShapeDtypeStruct((2, CHANNELS * tiles, 2 * TILE_PTS), jnp.bfloat16),
            jax.ShapeDtypeStruct((SUM_ROWS, KNOT_DEV), jnp.float32),
        ),
        in_specs=vmem(4),
        out_specs=(pl.BlockSpec(memory_space=pltpu.VMEM),) * 2,
        scratch_shapes=[pltpu.SMEM((8, TILE_PTS), jnp.int32), pltpu.SemaphoreType.DMA((1,))]
        + process_shapes(groups, tiles),
        compiler_params=params(14),
    )(packed, rows, near, far)


def all_totals(points, weights, totals):
    groups, tiles = len(points), points[0].shape[1]
    return pl.pallas_call(
        functools.partial(other_kernel, groups),
        out_shape=jax.ShapeDtypeStruct((SUM_ROWS, KNOT_DEV), jnp.float32),
        in_specs=vmem(groups + 2),
        out_specs=pl.BlockSpec(memory_space=pltpu.VMEM),
        scratch_shapes=[pltpu.VMEM(packed_shape(groups, tiles), jnp.float32)]
        + arrange_shapes(groups, tiles)
        + process_shapes(groups, tiles),
        compiler_params=params(24),
    )(*points, weights, totals)


def cholesky(matrix):
    factor = {}
    inverse = []
    for column in range(6):
        pivot = matrix[column, column]
        for inner in range(column):
            pivot = pivot - factor[column, inner] * factor[column, inner]
        inverse.append(1.0 / jnp.sqrt(pivot))
        for row in range(column + 1, 6):
            entry = matrix[column, row]
            for inner in range(column):
                entry = entry - factor[row, inner] * factor[column, inner]
            factor[row, column] = entry * inverse[column]
    return factor, inverse


def solve(system, right_side):
    factor, inverse = system
    forward = []
    for row in range(6):
        entry = right_side[row]
        for inner in range(row):
            entry = entry - factor[row, inner] * forward[inner]
        forward.append(entry * inverse[row])
    answer = [None] * 6
    for row in reversed(range(6)):
        entry = forward[row]
        for inner in range(row + 1, 6):
            entry = entry - factor[inner, row] * answer[inner]
        answer[row] = entry * inverse[row]
    return answer


def step_kernel(segs, members, knot_ref, sums_ref, points_ref, adjusted_ref, out_ref, held, index_ref):
    tiles = knot_ref.shape[1]
    for tile in range(tiles):
        index_ref[tile : tile + 1, :] = jnp.full((1, KNOT_DEV), knot_ref[0, tile], jnp.int32)
    seg = lax.axis_index("seg")
    for place in range(3):
        wanted = seg + place - 1
        there = (wanted >= 0) & (wanted < segs)
        first = jnp.minimum(jnp.maximum(wanted, 0), segs - 1) * members
        total = sums_ref[first]
        for other in range(1, members):
            total = total + sums_ref[first + other]
        held[place * SUM_ROWS : (place + 1) * SUM_ROWS, :] = jnp.where(there, total, 0.0)
    for place in range(3, 8):
        held[place * SUM_ROWS : (place + 1) * SUM_ROWS, :] = jnp.zeros(
            (SUM_ROWS, KNOT_DEV), jnp.float32
        )
    shape = (8, KNOT_DEV)
    lanes = lax.broadcasted_iota(jnp.int32, shape, 1)
    rows = lax.broadcasted_iota(jnp.int32, shape, 0)

    def earlier(value):
        turned = pltpu.roll(value, 1, 1)
        return jnp.where(lanes == 0, pltpu.roll(turned, 1, 0), turned)

    def following(value):
        turned = pltpu.roll(value, KNOT_DEV - 1, 1)
        return jnp.where(lanes == KNOT_DEV - 1, pltpu.roll(turned, 7, 0), turned)

    def quantity(place):
        return held[pl.ds(place, 8, stride=SUM_ROWS), :]

    pair_place = {pair: place for place, pair in enumerate(PAIRS)}
    matrix, cross, cross_before = {}, {}, {}
    for pair, place in pair_place.items():
        value = quantity(place) + earlier(quantity(42 + place))
        matrix[pair] = value + damping if pair[0] == pair[1] else value
        cross[pair] = quantity(21 + place)
        cross_before[pair] = earlier(cross[pair])
    right_side = [quantity(63 + a) + earlier(quantity(69 + a)) for a in range(6)]
    system = cholesky(matrix)
    beyond = (rows >= 2) & (seg == segs - 1)
    first = [jnp.where(beyond, 0.0, -entry) for entry in solve(system, right_side)]
    before = [earlier(entry) for entry in first]
    after = [following(entry) for entry in first]
    corrected = []
    for a in range(6):
        total = right_side[a]
        for b in range(6):
            pair = (min(a, b), max(a, b))
            total = total + cross_before[pair] * before[b] + cross[pair] * after[b]
        corrected.append(total)
    second = [jnp.where(beyond, 0.0, -entry) for entry in solve(system, corrected)]
    upper = [following(entry) for entry in second]
    for a in range(6):
        out_ref[a] = second[a][1:2]
    low_rows = [jnp.broadcast_to(second[a][1:2], shape) for a in range(6)]
    high_rows = [jnp.broadcast_to(upper[a][1:2], shape) for a in range(6)]
    for begin in range(0, tiles, 8):
        span = slice(begin, begin + 8)
        knots = index_ref[span, :]
        later = points_ref[12, span, :]
        early = 1.0 - later
        pose = []
        for a in range(6):
            low = jnp.take_along_axis(low_rows[a], knots, axis=1, mode="promise_in_bounds")
            high = jnp.take_along_axis(high_rows[a], knots, axis=1, mode="promise_in_bounds")
            pose.append(early * low + later * high)
        lever = [points_ref[c, span, :] for c in range(9, 12)]
        moved = [
            pose[1] * lever[2] - pose[2] * lever[1] + pose[3],
            pose[2] * lever[0] - pose[0] * lever[2] + pose[4],
            pose[0] * lever[1] - pose[1] * lever[0] + pose[5],
        ]
        for c in range(3):
            adjusted_ref[c, span, :] = points_ref[c, span, :] + moved[c]


def local(positions, lever_arm, spline_time, covariance, partner, partner_side, tile_knot):
    tiles = positions.shape[2] // TILE_PTS
    strips = lax.axis_size("strip")
    members = lax.axis_size("tile")
    segs = lax.axis_size("seg")

    table, points = pl.pallas_call(
        pack_kernel,
        out_shape=(
            jax.ShapeDtypeStruct((CHANNELS, tiles, TILE_PTS), jnp.float32),
            jax.ShapeDtypeStruct((POINT_ROWS, tiles, TILE_PTS), jnp.float32),
        ),
        in_specs=[pl.BlockSpec(memory_space=pltpu.HBM)] * 7,
        out_specs=(pl.BlockSpec(memory_space=pltpu.VMEM),) * 2,
        scratch_shapes=[
            pltpu.VMEM((tiles, TILE_PTS), jnp.int32),
            pltpu.SMEM((2, 1, tiles), jnp.int32),
            pltpu.SemaphoreType.DMA((7,)),
        ],
        compiler_params=params(14),
    )(
        *[
            pltpu.with_memory_space_constraint(array, pltpu.HBM)
            for array in (
                positions.reshape(3, tiles, TILE_PTS),
                covariance.reshape(6, tiles, TILE_PTS),
                lever_arm.reshape(3, tiles, TILE_PTS),
                spline_time.reshape(tiles, TILE_PTS),
                partner.reshape(tiles, TILE_PTS),
                partner_side,
                tile_knot,
            )
        ]
    )

    def trade(first):
        pairs = []
        for strip in range(first, strips - 1, 2):
            pairs += [(strip, strip + 1), (strip + 1, strip)]
        return lax.ppermute(table, "strip", pairs)

    swap = [(member, member ^ 1) for member in range(members)]
    arrived = []
    for hop in range(2, members, 2):
        pairs = [((member + hop) % members, member) for member in range(members)]
        arrived.append(lax.ppermute(points, "tile", pairs))
    near, far = trade(0), trade(1)
    packed, rows = early_rows([points, lax.ppermute(points, "tile", swap)])
    weights, totals = own_totals(2, packed, rows, near, far)
    arrived = lax.optimization_barrier((arrived, near, far, packed))[0]
    others = arrived + [lax.ppermute(group, "tile", swap) for group in arrived]
    sums = all_totals(others, weights, totals)
    all_sums = lax.all_gather(sums, ("seg", "tile"), axis=0)
    adjusted, corrections = pl.pallas_call(
        functools.partial(step_kernel, segs, members),
        out_shape=(
            jax.ShapeDtypeStruct((3, tiles, TILE_PTS), jnp.float32),
            jax.ShapeDtypeStruct((6, 1, KNOT_DEV), jnp.float32),
        ),
        in_specs=smem(1) + vmem(2),
        out_specs=(pl.BlockSpec(memory_space=pltpu.VMEM),) * 2,
        scratch_shapes=[
            pltpu.VMEM((8 * SUM_ROWS, KNOT_DEV), jnp.float32),
            pltpu.VMEM((tiles, KNOT_DEV), jnp.int32),
        ],
        compiler_params=params(6),
    )(tile_knot, all_sums, points)
    return adjusted.reshape(positions.shape), corrections.reshape(1, 6, KNOT_DEV)


def solution(mesh):
    in_specs = (
        P("strip", None, ("seg", "tile")),
        P("strip", None, ("seg", "tile")),
        P("strip", ("seg", "tile")),
        P("strip", None, ("seg", "tile")),
        P("strip", ("seg", "tile")),
        P("strip", ("seg", "tile")),
        P("strip", ("seg", "tile")),
    )
    out_specs = (P("strip", None, ("seg", "tile")), P("strip", None, "seg"))
    return jax.shard_map(local, mesh=mesh, in_specs=in_specs, out_specs=out_specs, check_vma=False)
```

```python
import functools

import jax
import jax.numpy as jnp
from jax import lax
from jax.experimental import pallas as pl
from jax.experimental.pallas import tpu as pltpu
from jax.sharding import PartitionSpec as P

KNOT_DEV = 128
TILE_PTS = 128
CHANNELS = 9
BLOCK_TILES = 4
ROW_GROUP = 16
POINT_ROWS = 16
PARTNER = 13
KNOT = 14
VALID = 15
TILE_ROW = 14
SUM_ROWS = 80

damping = 1.0

PAIRS = [(a, b) for a in range(6) for b in range(a, 6)]


def params(mebibytes=48):
    return pltpu.CompilerParams(vmem_limit_bytes=mebibytes * 2**20)


def vmem(count):
    return [pl.BlockSpec(memory_space=pltpu.VMEM)] * count


def smem(count):
    return [pl.BlockSpec(memory_space=pltpu.SMEM)] * count


def pack_kernel(pos, cov, lever, time, partner, sides, knots, table_ref, points_ref, ints, small, sems):
    tiles = time.shape[0]
    base = TILE_ROW * tiles

    def span(first):
        return points_ref.at[pl.ds(first * tiles, tiles)]

    copies = [
        pltpu.make_async_copy(partner, ints, sems.at[0]),
        pltpu.make_async_copy(sides, small.at[0], sems.at[1]),
        pltpu.make_async_copy(knots, small.at[1], sems.at[2]),
        pltpu.make_async_copy(pos, table_ref.at[pl.ds(0, 3)], sems.at[3]),
        pltpu.make_async_copy(cov, table_ref.at[pl.ds(3, 6)], sems.at[4]),
        pltpu.make_async_copy(time, span(12), sems.at[5]),
    ]
    copies += [pltpu.make_async_copy(lever.at[c], span(9 + c), sems.at[6 + c]) for c in range(3)]
    for copy in copies:
        copy.start()
    for copy in copies:
        copy.wait()
    for channel in range(CHANNELS):
        points_ref[channel * tiles : (channel + 1) * tiles, :] = table_ref[channel]
    points_ref[PARTNER * tiles : (PARTNER + 1) * tiles, :] = ints[...].astype(jnp.float32)
    points_ref[base : base + 8, :] = jnp.zeros((8, TILE_PTS), jnp.float32)
    for place in range(2):
        points_ref[base + place : base + place + 1, 0:tiles] = small[place].astype(jnp.float32)


def split_two(value):
    high = value.astype(jnp.bfloat16)
    low = (value - high.astype(jnp.float32)).astype(jnp.bfloat16)
    return high, low


def row_room(groups, tiles):
    return groups * tiles + 4 * ROW_GROUP


def arrange(points, packed, work):
    compact, codes, places, sem = work
    tiles = (points[0].shape[0] - 8) // TILE_ROW
    total = len(points) * tiles
    room = packed.shape[0] // POINT_ROWS
    shape = (tiles, TILE_PTS)
    lanes = lax.broadcasted_iota(jnp.int32, shape, 1)
    own_tile = lax.broadcasted_iota(jnp.int32, shape, 0)

    def ordered(size, test):
        rows = lax.broadcasted_iota(jnp.int32, (size, size), 0)
        return jnp.where(test(rows, lax.broadcasted_iota(jnp.int32, (size, size), 1)), 1.0, 0.0)

    upper = ordered(TILE_PTS, lambda row, lane: row <= lane).astype(jnp.bfloat16)
    lower = ordered(total, lambda row, lane: row > lane).astype(jnp.bfloat16)
    member = lax.axis_index("tile")
    near = jnp.where(lax.axis_index("strip") % 2 == 1, 0.0, 1.0)

    def tile_value(group, place):
        at = TILE_ROW * tiles + place
        return jnp.take_along_axis(
            jnp.broadcast_to(group[at : at + 1, :], shape), own_tile, axis=1, mode="promise_in_bounds"
        )

    ranks, numbers, farther = [], [], []
    for group in points:
        index = group[PARTNER * tiles : (PARTNER + 1) * tiles, :].astype(jnp.int32)
        offset = lax.shift_right_logical(index, 7) - member * tiles
        side = tile_value(group, 0)
        wanted = (offset >= 0) & (offset < tiles) & (side != 2.0)
        marks = jnp.where(wanted, 1.0, 0.0).astype(jnp.bfloat16)
        rank = jnp.dot(marks, upper, preferred_element_type=jnp.float32)
        ranks.append(rank.astype(jnp.int32))
        numbers.append(jnp.broadcast_to(rank[:, TILE_PTS - 1 :], shape))
        farther.append(jnp.where(side == near, 0.0, 1.0))
    number, far = jnp.concatenate(numbers, axis=0), jnp.concatenate(farther, axis=0)
    ends = []
    for chosen in (number * (1.0 - far), number * far):
        before = jnp.dot(lower, chosen.astype(jnp.bfloat16), preferred_element_type=jnp.float32)
        ends.append((before.astype(jnp.int32), (before + chosen).astype(jnp.int32)))
    start = jnp.where(far > 0.0, ends[1][0], ends[0][0])
    row = lax.shift_right_logical(start, 7)
    first = jnp.where(far > 0.0, room - 1 - row, row) * POINT_ROWS
    second = jnp.where(far > 0.0, first - POINT_ROWS, first + POINT_ROWS)
    lane = lax.broadcasted_iota(jnp.int32, (total, TILE_PTS), 1)
    code = jnp.where(lane == 0, first, jnp.where(lane == 1, second, start & (TILE_PTS - 1)))
    code = jnp.where(lane == 3, ends[0][1], jnp.where(lane == 4, ends[1][1], code))
    codes[...] = code
    copy = pltpu.make_async_copy(codes, places, sem.at[0])
    copy.start()
    for p, group in enumerate(points):
        source = jnp.zeros_like(lanes)
        for jump in (64, 32, 16, 8, 4, 2, 1):
            there = jnp.take_along_axis(
                ranks[p], source + (jump - 1), axis=1, mode="promise_in_bounds"
            )
            source = jnp.where(there <= lanes, source + jump, source)
        for channel in range(POINT_ROWS):
            if channel == VALID:
                value = jnp.where(lanes.astype(jnp.float32) < numbers[p], 1.0, 0.0)
            elif channel == KNOT:
                value = tile_value(group, 1)
            else:
                value = group[channel * tiles : (channel + 1) * tiles, :]
                value = jnp.take_along_axis(value, source, axis=1, mode="promise_in_bounds")
            at = p * tiles * POINT_ROWS + channel
            compact[pl.ds(at, tiles, stride=POINT_ROWS), :] = value
    copy.wait()

    wide = lax.broadcasted_iota(jnp.int32, (POINT_ROWS, TILE_PTS), 1)

    def span(first):
        return pl.ds(pl.multiple_of(first, POINT_ROWS), POINT_ROWS)

    def place(tile):
        shift = places[tile, 2]
        value = pltpu.roll(compact[span(tile * POINT_ROWS), :], shift, 1)
        at = span(places[tile, 0])
        packed[at, :] = jnp.where(wide >= shift, value, packed[at, :])
        packed[span(places[tile, 1]), :] = jnp.where(wide < shift, value, 0.0)

    unroll = 16

    def several(step, carry):
        for tile in range(unroll):
            place(step * unroll + tile)
        return carry

    lax.fori_loop(0, total // unroll, several, 0)
    near_rows = lax.shift_right_logical(places[total - 1, 3] + TILE_PTS - 1, 7)
    far_rows = lax.shift_right_logical(places[total - 1, 4] + TILE_PTS - 1, 7)
    blank = jnp.zeros((POINT_ROWS, TILE_PTS), jnp.float32)
    for extra in range(ROW_GROUP):
        packed[span((near_rows + extra) * POINT_ROWS), :] = blank
        packed[span((room - 1 - far_rows - extra) * POINT_ROWS), :] = blank
    return near_rows, far_rows


def weigh_table(table, weights, slot):
    tiles = table.shape[1]
    for channel in range(CHANNELS):
        high, low = split_two(table[channel])
        rows = slice(channel * tiles, (channel + 1) * tiles)
        weights[slot, rows, 0:TILE_PTS] = high
        weights[slot, rows, TILE_PTS : 2 * TILE_PTS] = low


def process(packed, near_rows, far_rows, weights, totals_ref, work):
    target, terms_ref = work
    tiles = weights.shape[1] // CHANNELS
    room = packed.shape[0] // POINT_ROWS
    member = lax.axis_index("tile")
    near_blocks = lax.shift_right_logical(near_rows + BLOCK_TILES - 1, 2)
    far_blocks = lax.shift_right_logical(far_rows + BLOCK_TILES - 1, 2)
    blocks = near_blocks + far_blocks
    queries = BLOCK_TILES * TILE_PTS

    def one_block(block):
        block = jnp.minimum(block, blocks - 1)
        far = block >= near_blocks
        slot = far.astype(jnp.int32)
        base = jnp.where(far, room - BLOCK_TILES * (block - near_blocks + 1), block * BLOCK_TILES)
        ids = [base + j for j in range(BLOCK_TILES)]

        def channel(place):
            rows = [
                packed[pl.ds(base * POINT_ROWS + j * POINT_ROWS + place, 1), :]
                for j in range(BLOCK_TILES)
            ]
            return jnp.concatenate(rows, axis=1)

        index = channel(PARTNER).astype(jnp.int32)
        keys = index & (TILE_PTS - 1)
        rows = lax.shift_right_logical(index, 7) - member * tiles
        rows = jnp.where(channel(VALID) > 0.0, rows, -1)
        hot = jnp.where(
            lax.broadcasted_iota(jnp.int32, (TILE_PTS, queries), 0) == keys, 1.0, 0.0
        ).astype(jnp.bfloat16)
        picked = jnp.dot(
            weights[slot], jnp.concatenate([hot, hot], axis=0), preferred_element_type=jnp.float32
        )
        spread_rows = jnp.broadcast_to(rows, (8, queries))
        eight = lax.broadcasted_iota(jnp.int32, (8, queries), 0)
        found = [jnp.zeros((8, queries), jnp.float32) for _ in range(CHANNELS)]
        for step in range(tiles // 8):
            here = spread_rows == eight + 8 * step
            for channel in range(CHANNELS):
                begin = channel * tiles + 8 * step
                found[channel] = jnp.where(here, picked[begin : begin + 8], found[channel])
        return ids, [jnp.sum(entry, axis=0, keepdims=True) for entry in found]

    def body(step, carry):
        results = [one_block(2 * step), one_block(2 * step + 1)]
        for ids, flat in results:
            for channel in range(CHANNELS):
                for j in range(BLOCK_TILES):
                    piece = flat[channel][:, j * TILE_PTS : (j + 1) * TILE_PTS]
                    target[channel, pl.ds(ids[j], 1), :] = piece
        return carry

    lax.fori_loop(0, lax.shift_right_logical(blocks + 1, 1), body, 0)

    totals_ref[...] = jnp.zeros_like(totals_ref)
    terms_ref[75 * ROW_GROUP :, :] = jnp.zeros((5 * ROW_GROUP, TILE_PTS), jnp.float32)
    near_groups = lax.shift_right_logical(near_rows + ROW_GROUP - 1, 4)
    far_groups = lax.shift_right_logical(far_rows + ROW_GROUP - 1, 4)

    def add(step, carry):
        far = step >= near_groups
        base = jnp.where(far, room - ROW_GROUP * (step - near_groups + 1), step * ROW_GROUP)
        add_rows(pl.multiple_of(base, ROW_GROUP), packed, target, totals_ref, terms_ref)
        return carry

    lax.fori_loop(0, near_groups + far_groups, add, 0)


def add_rows(base, packed, target, totals_ref, terms_ref):
    group = ROW_GROUP
    span = pl.ds(base, group)

    def own(channel):
        return packed[pl.ds(base * POINT_ROWS + channel, group, stride=POINT_ROWS), :]

    valid = own(VALID) > 0.0
    m = [own(3 + c) + target[3 + c, span, :] for c in range(6)]
    residual = [jnp.where(valid, own(c) - target[c, span, :], 0.0) for c in range(3)]
    lever = [own(9 + c) for c in range(3)]
    later = own(12)
    early = 1.0 - later
    adjunct = [
        m[1] * m[2] - m[5] * m[5],
        m[0] * m[2] - m[4] * m[4],
        m[0] * m[1] - m[3] * m[3],
        m[4] * m[5] - m[3] * m[2],
        m[3] * m[5] - m[4] * m[1],
        m[3] * m[4] - m[0] * m[5],
    ]
    determinant = m[0] * adjunct[0] + m[3] * adjunct[3] + m[4] * adjunct[4]
    inv = [jnp.where(valid, entry / determinant, 0.0) for entry in adjunct]
    info = [[inv[0], inv[3], inv[4]], [inv[3], inv[1], inv[5]], [inv[4], inv[5], inv[2]]]

    def turned(column):
        return [
            lever[1] * column[2] - lever[2] * column[1],
            lever[2] * column[0] - lever[0] * column[2],
            lever[0] * column[1] - lever[1] * column[0],
        ] + list(column)

    weighted = [turned(info[i]) for i in range(3)]
    pulled = [
        info[i][0] * residual[0] + info[i][1] * residual[1] + info[i][2] * residual[2]
        for i in range(3)
    ]
    gradient = turned(pulled)
    gram = {}
    for b in range(6):
        column = turned([weighted[i][b] for i in range(3)])
        for a in range(b + 1):
            gram[a, b] = column[a]
    both = early * later
    terms = []
    for weight in (early * early, both, later * later):
        terms += [gram[pair] * weight for pair in PAIRS]
    for weight in (early, later):
        terms += [entry * weight for entry in gradient]
    for place, term in enumerate(terms):
        terms_ref[place * group : (place + 1) * group, :] = term
    knots = own(KNOT).astype(jnp.int32)
    stacked = lax.broadcasted_iota(jnp.int32, (KNOT_DEV, TILE_PTS), 0)
    total = totals_ref[...]
    for row in range(0, group, 2):
        parts, hots = [], []
        for r in (row, row + 1):
            high, low = split_two(terms_ref[pl.ds(r, SUM_ROWS, stride=group), :])
            parts.append(jnp.concatenate([high, low], axis=0))
            hots.append(jnp.where(stacked == knots[r : r + 1], 1.0, 0.0).astype(jnp.bfloat16))
        sums = lax.dot_general(
            jnp.concatenate(parts, axis=1),
            jnp.concatenate(hots, axis=1),
            (((1,), (1,)), ((), ())),
            preferred_element_type=jnp.float32,
        )
        total = total + sums[0:SUM_ROWS] + sums[SUM_ROWS:]
    totals_ref[...] = total


def early_kernel(groups, *refs):
    points = refs[:groups]
    packed, rows_ref = refs[groups : groups + 2]
    near_rows, far_rows = arrange(points, packed, refs[groups + 2 :])
    rows_ref[0:4, :] = jnp.full((4, TILE_PTS), near_rows, jnp.int32)
    rows_ref[4:8, :] = jnp.full((4, TILE_PTS), far_rows, jnp.int32)


def own_kernel(packed, rows_ref, near, far, weights, totals_ref, rows_here, sem, *work):
    copy = pltpu.make_async_copy(rows_ref, rows_here, sem.at[0])
    copy.start()
    weigh_table(near, weights, 0)
    weigh_table(far, weights, 1)
    copy.wait()
    process(packed, rows_here[0, 0], rows_here[4, 0], weights, totals_ref, work)


def other_kernel(groups, *refs):
    points = refs[:groups]
    weights, before_ref, totals_ref, packed = refs[groups : groups + 4]
    arranging, work = refs[groups + 4 : groups + 8], refs[groups + 8 :]
    near_rows, far_rows = arrange(points, packed, arranging)
    process(packed, near_rows, far_rows, weights, totals_ref, work)
    totals_ref[...] = totals_ref[...] + before_ref[...]


def arrange_shapes(groups, tiles):
    count = groups * tiles
    return [
        pltpu.VMEM((count * POINT_ROWS, TILE_PTS), jnp.float32),
        pltpu.VMEM((count, TILE_PTS), jnp.int32),
        pltpu.SMEM((count, TILE_PTS), jnp.int32),
        pltpu.SemaphoreType.DMA((1,)),
    ]


def process_shapes(groups, tiles):
    return [
        pltpu.VMEM((CHANNELS, row_room(groups, tiles), TILE_PTS), jnp.float32),
        pltpu.VMEM((SUM_ROWS * ROW_GROUP, TILE_PTS), jnp.float32),
    ]


def packed_shape(groups, tiles):
    return (row_room(groups, tiles) * POINT_ROWS, TILE_PTS)


def early_rows(points):
    groups, tiles = len(points), (points[0].shape[0] - 8) // TILE_ROW
    return pl.pallas_call(
        functools.partial(early_kernel, groups),
        out_shape=(
            jax.ShapeDtypeStruct(packed_shape(groups, tiles), jnp.float32),
            jax.ShapeDtypeStruct((8, TILE_PTS), jnp.int32),
        ),
        in_specs=vmem(groups),
        out_specs=(pl.BlockSpec(memory_space=pltpu.VMEM),) * 2,
        scratch_shapes=arrange_shapes(groups, tiles),
        compiler_params=params(14),
    )(*points)


def own_totals(groups, packed, rows, near, far):
    tiles = near.shape[1]
    return pl.pallas_call(
        own_kernel,
        out_shape=(
            jax.ShapeDtypeStruct((2, CHANNELS * tiles, 2 * TILE_PTS), jnp.bfloat16),
            jax.ShapeDtypeStruct((SUM_ROWS, KNOT_DEV), jnp.float32),
        ),
        in_specs=vmem(4),
        out_specs=(pl.BlockSpec(memory_space=pltpu.VMEM),) * 2,
        scratch_shapes=[pltpu.SMEM((8, TILE_PTS), jnp.int32), pltpu.SemaphoreType.DMA((1,))]
        + process_shapes(groups, tiles),
        compiler_params=params(14),
    )(packed, rows, near, far)


def all_totals(points, weights, totals):
    groups, tiles = len(points), (points[0].shape[0] - 8) // TILE_ROW
    return pl.pallas_call(
        functools.partial(other_kernel, groups),
        out_shape=jax.ShapeDtypeStruct((SUM_ROWS, KNOT_DEV), jnp.float32),
        in_specs=vmem(groups + 2),
        out_specs=pl.BlockSpec(memory_space=pltpu.VMEM),
        scratch_shapes=[pltpu.VMEM(packed_shape(groups, tiles), jnp.float32)]
        + arrange_shapes(groups, tiles)
        + process_shapes(groups, tiles),
        compiler_params=params(24),
    )(*points, weights, totals)


def cholesky(matrix):
    factor = {}
    inverse = []
    for column in range(6):
        pivot = matrix[column, column]
        for inner in range(column):
            pivot = pivot - factor[column, inner] * factor[column, inner]
        inverse.append(1.0 / jnp.sqrt(pivot))
        for row in range(column + 1, 6):
            entry = matrix[column, row]
            for inner in range(column):
                entry = entry - factor[row, inner] * factor[column, inner]
            factor[row, column] = entry * inverse[column]
    return factor, inverse


def solve(system, right_side):
    factor, inverse = system
    forward = []
    for row in range(6):
        entry = right_side[row]
        for inner in range(row):
            entry = entry - factor[row, inner] * forward[inner]
        forward.append(entry * inverse[row])
    answer = [None] * 6
    for row in reversed(range(6)):
        entry = forward[row]
        for inner in range(row + 1, 6):
            entry = entry - factor[inner, row] * answer[inner]
        answer[row] = entry * inverse[row]
    return answer


def step_kernel(segs, members, knot_ref, sums_ref, points_ref, adjusted_ref, out_ref, held, index_ref):
    tiles = knot_ref.shape[1]
    for tile in range(tiles):
        index_ref[tile : tile + 1, :] = jnp.full((1, KNOT_DEV), knot_ref[0, tile], jnp.int32)
    seg = lax.axis_index("seg")
    for place in range(3):
        wanted = seg + place - 1
        there = (wanted >= 0) & (wanted < segs)
        first = jnp.minimum(jnp.maximum(wanted, 0), segs - 1) * members
        total = sums_ref[first]
        for other in range(1, members):
            total = total + sums_ref[first + other]
        held[place * SUM_ROWS : (place + 1) * SUM_ROWS, :] = jnp.where(there, total, 0.0)
    for place in range(3, 8):
        held[place * SUM_ROWS : (place + 1) * SUM_ROWS, :] = jnp.zeros(
            (SUM_ROWS, KNOT_DEV), jnp.float32
        )
    shape = (8, KNOT_DEV)
    lanes = lax.broadcasted_iota(jnp.int32, shape, 1)
    rows = lax.broadcasted_iota(jnp.int32, shape, 0)

    def earlier(value):
        turned = pltpu.roll(value, 1, 1)
        return jnp.where(lanes == 0, pltpu.roll(turned, 1, 0), turned)

    def following(value):
        turned = pltpu.roll(value, KNOT_DEV - 1, 1)
        return jnp.where(lanes == KNOT_DEV - 1, pltpu.roll(turned, 7, 0), turned)

    def quantity(place):
        return held[pl.ds(place, 8, stride=SUM_ROWS), :]

    pair_place = {pair: place for place, pair in enumerate(PAIRS)}
    matrix, cross, cross_before = {}, {}, {}
    for pair, place in pair_place.items():
        value = quantity(place) + earlier(quantity(42 + place))
        matrix[pair] = value + damping if pair[0] == pair[1] else value
        cross[pair] = quantity(21 + place)
        cross_before[pair] = earlier(cross[pair])
    right_side = [quantity(63 + a) + earlier(quantity(69 + a)) for a in range(6)]
    system = cholesky(matrix)
    beyond = (rows >= 2) & (seg == segs - 1)
    first = [jnp.where(beyond, 0.0, -entry) for entry in solve(system, right_side)]
    before = [earlier(entry) for entry in first]
    after = [following(entry) for entry in first]
    corrected = []
    for a in range(6):
        total = right_side[a]
        for b in range(6):
            pair = (min(a, b), max(a, b))
            total = total + cross_before[pair] * before[b] + cross[pair] * after[b]
        corrected.append(total)
    second = [jnp.where(beyond, 0.0, -entry) for entry in solve(system, corrected)]
    upper = [following(entry) for entry in second]
    for a in range(6):
        out_ref[a] = second[a][1:2]
    low_rows = [jnp.broadcast_to(second[a][1:2], shape) for a in range(6)]
    high_rows = [jnp.broadcast_to(upper[a][1:2], shape) for a in range(6)]
    for begin in range(0, tiles, 8):
        span = slice(begin, begin + 8)
        knots = index_ref[span, :]

        def own(channel):
            return points_ref[channel * tiles + begin : channel * tiles + begin + 8, :]

        later = own(12)
        early = 1.0 - later
        pose = []
        for a in range(6):
            low = jnp.take_along_axis(low_rows[a], knots, axis=1, mode="promise_in_bounds")
            high = jnp.take_along_axis(high_rows[a], knots, axis=1, mode="promise_in_bounds")
            pose.append(early * low + later * high)
        lever = [own(c) for c in range(9, 12)]
        moved = [
            pose[1] * lever[2] - pose[2] * lever[1] + pose[3],
            pose[2] * lever[0] - pose[0] * lever[2] + pose[4],
            pose[0] * lever[1] - pose[1] * lever[0] + pose[5],
        ]
        for c in range(3):
            adjusted_ref[c, span, :] = own(c) + moved[c]


def local(positions, lever_arm, spline_time, covariance, partner, partner_side, tile_knot):
    tiles = positions.shape[2] // TILE_PTS
    strips = lax.axis_size("strip")
    members = lax.axis_size("tile")
    segs = lax.axis_size("seg")

    table, points = pl.pallas_call(
        pack_kernel,
        out_shape=(
            jax.ShapeDtypeStruct((CHANNELS, tiles, TILE_PTS), jnp.float32),
            jax.ShapeDtypeStruct((TILE_ROW * tiles + 8, TILE_PTS), jnp.float32),
        ),
        in_specs=[pl.BlockSpec(memory_space=pltpu.HBM)] * 7,
        out_specs=(pl.BlockSpec(memory_space=pltpu.VMEM),) * 2,
        scratch_shapes=[
            pltpu.VMEM((tiles, TILE_PTS), jnp.int32),
            pltpu.VMEM((2, 1, tiles), jnp.int32),
            pltpu.SemaphoreType.DMA((9,)),
        ],
        compiler_params=params(14),
    )(
        *[
            pltpu.with_memory_space_constraint(array, pltpu.HBM)
            for array in (
                positions.reshape(3, tiles, TILE_PTS),
                covariance.reshape(6, tiles, TILE_PTS),
                lever_arm.reshape(3, tiles, TILE_PTS),
                spline_time.reshape(tiles, TILE_PTS),
                partner.reshape(tiles, TILE_PTS),
                partner_side,
                tile_knot,
            )
        ]
    )

    def trade(first):
        pairs = []
        for strip in range(first, strips - 1, 2):
            pairs += [(strip, strip + 1), (strip + 1, strip)]
        return lax.ppermute(table, "strip", pairs)

    swap = [(member, member ^ 1) for member in range(members)]
    arrived = []
    for hop in range(2, members, 2):
        pairs = [((member + hop) % members, member) for member in range(members)]
        arrived.append(lax.ppermute(points, "tile", pairs))
    near, far = trade(0), trade(1)
    packed, rows = early_rows([points, lax.ppermute(points, "tile", swap)])
    weights, totals = own_totals(2, packed, rows, near, far)
    arrived = lax.optimization_barrier((arrived, near, far, packed))[0]
    others = arrived + [lax.ppermute(group, "tile", swap) for group in arrived]
    sums = all_totals(others, weights, totals)
    all_sums = lax.all_gather(sums, ("seg", "tile"), axis=0)
    adjusted, corrections = pl.pallas_call(
        functools.partial(step_kernel, segs, members),
        out_shape=(
            jax.ShapeDtypeStruct((3, tiles, TILE_PTS), jnp.float32),
            jax.ShapeDtypeStruct((6, 1, KNOT_DEV), jnp.float32),
        ),
        in_specs=smem(1) + vmem(2),
        out_specs=(pl.BlockSpec(memory_space=pltpu.VMEM),) * 2,
        scratch_shapes=[
            pltpu.VMEM((8 * SUM_ROWS, KNOT_DEV), jnp.float32),
            pltpu.VMEM((tiles, KNOT_DEV), jnp.int32),
        ],
        compiler_params=params(6),
    )(tile_knot, all_sums, points)
    return adjusted.reshape(positions.shape), corrections.reshape(1, 6, KNOT_DEV)


def solution(mesh):
    in_specs = (
        P("strip", None, ("seg", "tile")),
        P("strip", None, ("seg", "tile")),
        P("strip", ("seg", "tile")),
        P("strip", None, ("seg", "tile")),
        P("strip", ("seg", "tile")),
        P("strip", ("seg", "tile")),
        P("strip", ("seg", "tile")),
    )
    out_specs = (P("strip", None, ("seg", "tile")), P("strip", None, "seg"))
    return jax.shard_map(local, mesh=mesh, in_specs=in_specs, out_specs=out_specs, check_vma=False)
```

```python
import functools

import jax
import jax.numpy as jnp
from jax import lax
from jax.experimental import pallas as pl
from jax.experimental.pallas import tpu as pltpu
from jax.sharding import PartitionSpec as P

KNOT_DEV = 128
TILE_PTS = 128
CHANNELS = 9
BLOCK_TILES = 4
ROW_GROUP = 16
POINT_ROWS = 16
PARTNER = 13
KNOT = 14
VALID = 15
TILE_ROW = 14
SUM_ROWS = 80

damping = 1.0

PAIRS = [(a, b) for a in range(6) for b in range(a, 6)]


def params(mebibytes=48):
    return pltpu.CompilerParams(vmem_limit_bytes=mebibytes * 2**20)


def vmem(count):
    return [pl.BlockSpec(memory_space=pltpu.VMEM)] * count


def smem(count):
    return [pl.BlockSpec(memory_space=pltpu.SMEM)] * count


def pack_kernel(pos, cov, lever, time, partner, sides, knots, table_ref, points_ref, ints, small, sems):
    tiles = time.shape[0]
    base = TILE_ROW * tiles

    def span(first):
        return points_ref.at[pl.ds(first * tiles, tiles)]

    copies = [
        pltpu.make_async_copy(partner, ints, sems.at[0]),
        pltpu.make_async_copy(sides, small.at[0], sems.at[1]),
        pltpu.make_async_copy(knots, small.at[1], sems.at[2]),
        pltpu.make_async_copy(pos, table_ref.at[pl.ds(0, 3)], sems.at[3]),
        pltpu.make_async_copy(cov, table_ref.at[pl.ds(3, 6)], sems.at[4]),
        pltpu.make_async_copy(time, span(12), sems.at[5]),
    ]
    copies += [pltpu.make_async_copy(lever.at[c], span(9 + c), sems.at[6 + c]) for c in range(3)]
    for copy in copies:
        copy.start()
    for copy in copies:
        copy.wait()
    for channel in range(CHANNELS):
        points_ref[channel * tiles : (channel + 1) * tiles, :] = table_ref[channel]
    points_ref[PARTNER * tiles : (PARTNER + 1) * tiles, :] = ints[...].astype(jnp.float32)
    points_ref[base : base + 8, :] = jnp.zeros((8, TILE_PTS), jnp.float32)
    for place in range(2):
        points_ref[base + place : base + place + 1, 0:tiles] = small[place].astype(jnp.float32)


def split_two(value):
    high = value.astype(jnp.bfloat16)
    low = (value - high.astype(jnp.float32)).astype(jnp.bfloat16)
    return high, low


def row_room(groups, tiles):
    return groups * tiles + 4 * ROW_GROUP


def arrange(points, packed, work):
    compact, codes, places, sem = work
    tiles = (points[0].shape[0] - 8) // TILE_ROW
    total = len(points) * tiles
    room = packed.shape[0] // POINT_ROWS
    shape = (tiles, TILE_PTS)
    lanes = lax.broadcasted_iota(jnp.int32, shape, 1)
    own_tile = lax.broadcasted_iota(jnp.int32, shape, 0)

    def ordered(size, test):
        rows = lax.broadcasted_iota(jnp.int32, (size, size), 0)
        marks = test(rows, lax.broadcasted_iota(jnp.int32, (size, size), 1))
        return jnp.where(marks, 1.0, 0.0).astype(jnp.bfloat16)

    member = lax.axis_index("tile")
    near = jnp.where(lax.axis_index("strip") % 2 == 1, 0.0, 1.0)

    def tile_value(group, place):
        at = TILE_ROW * tiles + place
        return jnp.take_along_axis(
            jnp.broadcast_to(group[at : at + 1, :], shape), own_tile, axis=1, mode="promise_in_bounds"
        )

    marks = []
    for group in points:
        index = group[PARTNER * tiles : (PARTNER + 1) * tiles, :].astype(jnp.int32)
        offset = lax.shift_right_logical(index, 7) - member * tiles
        wanted = (offset >= 0) & (offset < tiles) & (tile_value(group, 0) != 2.0)
        marks.append(jnp.where(wanted, 1.0, 0.0).astype(jnp.bfloat16))
    marks = jnp.concatenate(marks, axis=0)
    number = lax.dot_general(
        jnp.ones((16, TILE_PTS), jnp.bfloat16),
        marks,
        (((1,), (1,)), ((), ())),
        preferred_element_type=jnp.float32,
    )
    base = TILE_ROW * tiles
    sides = jnp.concatenate([group[base : base + 1, 0:tiles] for group in points], axis=1)
    far = jnp.broadcast_to(jnp.where(sides == near, 0.0, 1.0), number.shape)
    upper_rows = lax.broadcasted_iota(jnp.int32, number.shape, 0) < 8
    chosen = jnp.where(upper_rows, number * (1.0 - far), number * far)
    before = jnp.dot(
        chosen.astype(jnp.bfloat16),
        ordered(total, lambda row, lane: row < lane),
        preferred_element_type=jnp.float32,
    )
    ends = (before + chosen).astype(jnp.int32)
    before = before.astype(jnp.int32)
    far = far[0:8] > 0.0
    start = jnp.where(far, before[8:16], before[0:8])
    row = lax.shift_right_logical(start, 7)
    first = jnp.where(far, room - 1 - row, row) * POINT_ROWS
    second = jnp.where(far, first - POINT_ROWS, first + POINT_ROWS)
    line = lax.broadcasted_iota(jnp.int32, (8, total), 0)
    code = jnp.where(line == 0, first, jnp.where(line == 1, second, start & (TILE_PTS - 1)))
    code = jnp.where(line == 3, ends[0:8], jnp.where(line == 4, ends[8:16], code))
    codes[...] = code
    copy = pltpu.make_async_copy(codes, places, sem.at[0])
    copy.start()
    ranks = jnp.dot(
        marks, ordered(TILE_PTS, lambda row, lane: row <= lane), preferred_element_type=jnp.float32
    ).astype(jnp.int32)
    for p, group in enumerate(points):
        rank = ranks[p * tiles : (p + 1) * tiles]
        source = jnp.zeros_like(lanes)
        for jump in (64, 32, 16, 8, 4, 2, 1):
            there = jnp.take_along_axis(
                rank, source + (jump - 1), axis=1, mode="promise_in_bounds"
            )
            source = jnp.where(there <= lanes, source + jump, source)
        for channel in range(POINT_ROWS):
            if channel == VALID:
                value = jnp.where(lanes < jnp.broadcast_to(rank[:, TILE_PTS - 1 :], shape), 1.0, 0.0)
            elif channel == KNOT:
                value = tile_value(group, 1)
            else:
                value = group[channel * tiles : (channel + 1) * tiles, :]
                value = jnp.take_along_axis(value, source, axis=1, mode="promise_in_bounds")
            at = p * tiles * POINT_ROWS + channel
            compact[pl.ds(at, tiles, stride=POINT_ROWS), :] = value
    copy.wait()

    wide = lax.broadcasted_iota(jnp.int32, (POINT_ROWS, TILE_PTS), 1)

    def span(first):
        return pl.ds(pl.multiple_of(first, POINT_ROWS), POINT_ROWS)

    def place(tile):
        shift = places[2, tile]
        value = pltpu.roll(compact[span(tile * POINT_ROWS), :], shift, 1)
        at = span(places[0, tile])
        packed[at, :] = jnp.where(wide >= shift, value, packed[at, :])
        packed[span(places[1, tile]), :] = jnp.where(wide < shift, value, 0.0)

    unroll = tiles

    def several(step, carry):
        for tile in range(unroll):
            place(step * unroll + tile)
        return carry

    lax.fori_loop(0, total // unroll, several, 0)
    near_rows = lax.shift_right_logical(places[3, total - 1] + TILE_PTS - 1, 7)
    far_rows = lax.shift_right_logical(places[4, total - 1] + TILE_PTS - 1, 7)
    blank = jnp.zeros((POINT_ROWS, TILE_PTS), jnp.float32)
    for extra in range(ROW_GROUP):
        packed[span((near_rows + extra) * POINT_ROWS), :] = blank
        packed[span((room - 1 - far_rows - extra) * POINT_ROWS), :] = blank
    return near_rows, far_rows


def weigh_table(table, weights, slot):
    tiles = table.shape[1]
    for channel in range(CHANNELS):
        high, low = split_two(table[channel])
        rows = slice(channel * tiles, (channel + 1) * tiles)
        weights[slot, rows, 0:TILE_PTS] = high
        weights[slot, rows, TILE_PTS : 2 * TILE_PTS] = low


def process(packed, near_rows, far_rows, weights, totals_ref, work):
    target, terms_ref = work
    tiles = weights.shape[1] // CHANNELS
    room = packed.shape[0] // POINT_ROWS
    member = lax.axis_index("tile")
    near_blocks = lax.shift_right_logical(near_rows + BLOCK_TILES - 1, 2)
    far_blocks = lax.shift_right_logical(far_rows + BLOCK_TILES - 1, 2)
    blocks = near_blocks + far_blocks
    queries = BLOCK_TILES * TILE_PTS

    def one_block(block):
        block = jnp.minimum(block, blocks - 1)
        far = block >= near_blocks
        slot = far.astype(jnp.int32)
        base = jnp.where(far, room - BLOCK_TILES * (block - near_blocks + 1), block * BLOCK_TILES)
        ids = [base + j for j in range(BLOCK_TILES)]

        def channel(place):
            rows = [
                packed[pl.ds(base * POINT_ROWS + j * POINT_ROWS + place, 1), :]
                for j in range(BLOCK_TILES)
            ]
            return jnp.concatenate(rows, axis=1)

        index = channel(PARTNER).astype(jnp.int32)
        keys = index & (TILE_PTS - 1)
        rows = lax.shift_right_logical(index, 7) - member * tiles
        rows = jnp.where(channel(VALID) > 0.0, rows, -1)
        hot = jnp.where(
            lax.broadcasted_iota(jnp.int32, (TILE_PTS, queries), 0) == keys, 1.0, 0.0
        ).astype(jnp.bfloat16)
        picked = jnp.dot(
            weights[slot], jnp.concatenate([hot, hot], axis=0), preferred_element_type=jnp.float32
        )
        spread_rows = jnp.broadcast_to(rows, (8, queries))
        eight = lax.broadcasted_iota(jnp.int32, (8, queries), 0)
        found = [jnp.zeros((8, queries), jnp.float32) for _ in range(CHANNELS)]
        for step in range(tiles // 8):
            here = spread_rows == eight + 8 * step
            for channel in range(CHANNELS):
                begin = channel * tiles + 8 * step
                found[channel] = jnp.where(here, picked[begin : begin + 8], found[channel])
        return ids, [jnp.sum(entry, axis=0, keepdims=True) for entry in found]

    def body(step, carry):
        results = [one_block(2 * step), one_block(2 * step + 1)]
        for ids, flat in results:
            for channel in range(CHANNELS):
                for j in range(BLOCK_TILES):
                    piece = flat[channel][:, j * TILE_PTS : (j + 1) * TILE_PTS]
                    target[channel, pl.ds(ids[j], 1), :] = piece
        return carry

    lax.fori_loop(0, lax.shift_right_logical(blocks + 1, 1), body, 0)

    totals_ref[...] = jnp.zeros_like(totals_ref)
    terms_ref[75 * ROW_GROUP :, :] = jnp.zeros((5 * ROW_GROUP, TILE_PTS), jnp.float32)
    near_groups = lax.shift_right_logical(near_rows + ROW_GROUP - 1, 4)
    far_groups = lax.shift_right_logical(far_rows + ROW_GROUP - 1, 4)

    def add(step, carry):
        far = step >= near_groups
        base = jnp.where(far, room - ROW_GROUP * (step - near_groups + 1), step * ROW_GROUP)
        add_rows(pl.multiple_of(base, ROW_GROUP), packed, target, totals_ref, terms_ref)
        return carry

    lax.fori_loop(0, near_groups + far_groups, add, 0)


def add_rows(base, packed, target, totals_ref, terms_ref):
    group = ROW_GROUP
    span = pl.ds(base, group)

    def own(channel):
        return packed[pl.ds(base * POINT_ROWS + channel, group, stride=POINT_ROWS), :]

    valid = own(VALID) > 0.0
    m = [own(3 + c) + target[3 + c, span, :] for c in range(6)]
    residual = [jnp.where(valid, own(c) - target[c, span, :], 0.0) for c in range(3)]
    lever = [own(9 + c) for c in range(3)]
    later = own(12)
    early = 1.0 - later
    adjunct = [
        m[1] * m[2] - m[5] * m[5],
        m[0] * m[2] - m[4] * m[4],
        m[0] * m[1] - m[3] * m[3],
        m[4] * m[5] - m[3] * m[2],
        m[3] * m[5] - m[4] * m[1],
        m[3] * m[4] - m[0] * m[5],
    ]
    determinant = m[0] * adjunct[0] + m[3] * adjunct[3] + m[4] * adjunct[4]
    inv = [jnp.where(valid, entry / determinant, 0.0) for entry in adjunct]
    info = [[inv[0], inv[3], inv[4]], [inv[3], inv[1], inv[5]], [inv[4], inv[5], inv[2]]]

    def turned(column):
        return [
            lever[1] * column[2] - lever[2] * column[1],
            lever[2] * column[0] - lever[0] * column[2],
            lever[0] * column[1] - lever[1] * column[0],
        ] + list(column)

    weighted = [turned(info[i]) for i in range(3)]
    pulled = [
        info[i][0] * residual[0] + info[i][1] * residual[1] + info[i][2] * residual[2]
        for i in range(3)
    ]
    gradient = turned(pulled)
    gram = {}
    for b in range(6):
        column = turned([weighted[i][b] for i in range(3)])
        for a in range(b + 1):
            gram[a, b] = column[a]
    both = early * later
    terms = []
    for weight in (early * early, both, later * later):
        terms += [gram[pair] * weight for pair in PAIRS]
    for weight in (early, later):
        terms += [entry * weight for entry in gradient]
    for place, term in enumerate(terms):
        terms_ref[place * group : (place + 1) * group, :] = term
    knots = own(KNOT).astype(jnp.int32)
    stacked = lax.broadcasted_iota(jnp.int32, (KNOT_DEV, TILE_PTS), 0)
    total = totals_ref[...]
    for row in range(0, group, 2):
        parts, hots = [], []
        for r in (row, row + 1):
            high, low = split_two(terms_ref[pl.ds(r, SUM_ROWS, stride=group), :])
            parts.append(jnp.concatenate([high, low], axis=0))
            hots.append(jnp.where(stacked == knots[r : r + 1], 1.0, 0.0).astype(jnp.bfloat16))
        sums = lax.dot_general(
            jnp.concatenate(parts, axis=1),
            jnp.concatenate(hots, axis=1),
            (((1,), (1,)), ((), ())),
            preferred_element_type=jnp.float32,
        )
        total = total + sums[0:SUM_ROWS] + sums[SUM_ROWS:]
    totals_ref[...] = total


def early_kernel(groups, *refs):
    points = refs[:groups]
    packed, rows_ref = refs[groups : groups + 2]
    near_rows, far_rows = arrange(points, packed, refs[groups + 2 :])
    rows_ref[0:4, :] = jnp.full((4, TILE_PTS), near_rows, jnp.int32)
    rows_ref[4:8, :] = jnp.full((4, TILE_PTS), far_rows, jnp.int32)


def own_kernel(packed, rows_ref, near, far, weights, totals_ref, rows_here, sem, *work):
    copy = pltpu.make_async_copy(rows_ref, rows_here, sem.at[0])
    copy.start()
    weigh_table(near, weights, 0)
    weigh_table(far, weights, 1)
    copy.wait()
    process(packed, rows_here[0, 0], rows_here[4, 0], weights, totals_ref, work)


def other_kernel(groups, *refs):
    points = refs[:groups]
    weights, before_ref, totals_ref, packed = refs[groups : groups + 4]
    arranging, work = refs[groups + 4 : groups + 8], refs[groups + 8 :]
    near_rows, far_rows = arrange(points, packed, arranging)
    process(packed, near_rows, far_rows, weights, totals_ref, work)
    totals_ref[...] = totals_ref[...] + before_ref[...]


def arrange_shapes(groups, tiles):
    count = groups * tiles
    return [
        pltpu.VMEM((count * POINT_ROWS, TILE_PTS), jnp.float32),
        pltpu.VMEM((8, count), jnp.int32),
        pltpu.SMEM((8, count), jnp.int32),
        pltpu.SemaphoreType.DMA((1,)),
    ]


def process_shapes(groups, tiles):
    return [
        pltpu.VMEM((CHANNELS, row_room(groups, tiles), TILE_PTS), jnp.float32),
        pltpu.VMEM((SUM_ROWS * ROW_GROUP, TILE_PTS), jnp.float32),
    ]


def packed_shape(groups, tiles):
    return (row_room(groups, tiles) * POINT_ROWS, TILE_PTS)


def early_rows(points):
    groups, tiles = len(points), (points[0].shape[0] - 8) // TILE_ROW
    return pl.pallas_call(
        functools.partial(early_kernel, groups),
        out_shape=(
            jax.ShapeDtypeStruct(packed_shape(groups, tiles), jnp.float32),
            jax.ShapeDtypeStruct((8, TILE_PTS), jnp.int32),
        ),
        in_specs=vmem(groups),
        out_specs=(pl.BlockSpec(memory_space=pltpu.VMEM),) * 2,
        scratch_shapes=arrange_shapes(groups, tiles),
        compiler_params=params(14),
    )(*points)


def own_totals(groups, packed, rows, near, far):
    tiles = near.shape[1]
    return pl.pallas_call(
        own_kernel,
        out_shape=(
            jax.ShapeDtypeStruct((2, CHANNELS * tiles, 2 * TILE_PTS), jnp.bfloat16),
            jax.ShapeDtypeStruct((SUM_ROWS, KNOT_DEV), jnp.float32),
        ),
        in_specs=vmem(4),
        out_specs=(pl.BlockSpec(memory_space=pltpu.VMEM),) * 2,
        scratch_shapes=[pltpu.SMEM((8, TILE_PTS), jnp.int32), pltpu.SemaphoreType.DMA((1,))]
        + process_shapes(groups, tiles),
        compiler_params=params(14),
    )(packed, rows, near, far)


def all_totals(points, weights, totals):
    groups, tiles = len(points), (points[0].shape[0] - 8) // TILE_ROW
    return pl.pallas_call(
        functools.partial(other_kernel, groups),
        out_shape=jax.ShapeDtypeStruct((SUM_ROWS, KNOT_DEV), jnp.float32),
        in_specs=vmem(groups + 2),
        out_specs=pl.BlockSpec(memory_space=pltpu.VMEM),
        scratch_shapes=[pltpu.VMEM(packed_shape(groups, tiles), jnp.float32)]
        + arrange_shapes(groups, tiles)
        + process_shapes(groups, tiles),
        compiler_params=params(24),
    )(*points, weights, totals)


def cholesky(matrix):
    factor = {}
    inverse = []
    for column in range(6):
        pivot = matrix[column, column]
        for inner in range(column):
            pivot = pivot - factor[column, inner] * factor[column, inner]
        inverse.append(1.0 / jnp.sqrt(pivot))
        for row in range(column + 1, 6):
            entry = matrix[column, row]
            for inner in range(column):
                entry = entry - factor[row, inner] * factor[column, inner]
            factor[row, column] = entry * inverse[column]
    return factor, inverse


def solve(system, right_side):
    factor, inverse = system
    forward = []
    for row in range(6):
        entry = right_side[row]
        for inner in range(row):
            entry = entry - factor[row, inner] * forward[inner]
        forward.append(entry * inverse[row])
    answer = [None] * 6
    for row in reversed(range(6)):
        entry = forward[row]
        for inner in range(row + 1, 6):
            entry = entry - factor[inner, row] * answer[inner]
        answer[row] = entry * inverse[row]
    return answer


def step_kernel(segs, members, knot_ref, sums_ref, points_ref, adjusted_ref, out_ref, held, index_ref):
    tiles = knot_ref.shape[1]
    for tile in range(tiles):
        index_ref[tile : tile + 1, :] = jnp.full((1, KNOT_DEV), knot_ref[0, tile], jnp.int32)
    seg = lax.axis_index("seg")
    for place in range(3):
        wanted = seg + place - 1
        there = (wanted >= 0) & (wanted < segs)
        first = jnp.minimum(jnp.maximum(wanted, 0), segs - 1) * members
        total = sums_ref[first]
        for other in range(1, members):
            total = total + sums_ref[first + other]
        held[place * SUM_ROWS : (place + 1) * SUM_ROWS, :] = jnp.where(there, total, 0.0)
    for place in range(3, 8):
        held[place * SUM_ROWS : (place + 1) * SUM_ROWS, :] = jnp.zeros(
            (SUM_ROWS, KNOT_DEV), jnp.float32
        )
    shape = (8, KNOT_DEV)
    lanes = lax.broadcasted_iota(jnp.int32, shape, 1)
    rows = lax.broadcasted_iota(jnp.int32, shape, 0)

    def earlier(value):
        turned = pltpu.roll(value, 1, 1)
        return jnp.where(lanes == 0, pltpu.roll(turned, 1, 0), turned)

    def following(value):
        turned = pltpu.roll(value, KNOT_DEV - 1, 1)
        return jnp.where(lanes == KNOT_DEV - 1, pltpu.roll(turned, 7, 0), turned)

    def quantity(place):
        return held[pl.ds(place, 8, stride=SUM_ROWS), :]

    pair_place = {pair: place for place, pair in enumerate(PAIRS)}
    matrix, cross, cross_before = {}, {}, {}
    for pair, place in pair_place.items():
        value = quantity(place) + earlier(quantity(42 + place))
        matrix[pair] = value + damping if pair[0] == pair[1] else value
        cross[pair] = quantity(21 + place)
        cross_before[pair] = earlier(cross[pair])
    right_side = [quantity(63 + a) + earlier(quantity(69 + a)) for a in range(6)]
    system = cholesky(matrix)
    beyond = (rows >= 2) & (seg == segs - 1)
    first = [jnp.where(beyond, 0.0, -entry) for entry in solve(system, right_side)]
    before = [earlier(entry) for entry in first]
    after = [following(entry) for entry in first]
    corrected = []
    for a in range(6):
        total = right_side[a]
        for b in range(6):
            pair = (min(a, b), max(a, b))
            total = total + cross_before[pair] * before[b] + cross[pair] * after[b]
        corrected.append(total)
    second = [jnp.where(beyond, 0.0, -entry) for entry in solve(system, corrected)]
    upper = [following(entry) for entry in second]
    for a in range(6):
        out_ref[a] = second[a][1:2]
    low_rows = [jnp.broadcast_to(second[a][1:2], shape) for a in range(6)]
    high_rows = [jnp.broadcast_to(upper[a][1:2], shape) for a in range(6)]
    for begin in range(0, tiles, 8):
        span = slice(begin, begin + 8)
        knots = index_ref[span, :]

        def own(channel):
            return points_ref[channel * tiles + begin : channel * tiles + begin + 8, :]

        later = own(12)
        early = 1.0 - later
        pose = []
        for a in range(6):
            low = jnp.take_along_axis(low_rows[a], knots, axis=1, mode="promise_in_bounds")
            high = jnp.take_along_axis(high_rows[a], knots, axis=1, mode="promise_in_bounds")
            pose.append(early * low + later * high)
        lever = [own(c) for c in range(9, 12)]
        moved = [
            pose[1] * lever[2] - pose[2] * lever[1] + pose[3],
            pose[2] * lever[0] - pose[0] * lever[2] + pose[4],
            pose[0] * lever[1] - pose[1] * lever[0] + pose[5],
        ]
        for c in range(3):
            adjusted_ref[c, span, :] = own(c) + moved[c]


def local(positions, lever_arm, spline_time, covariance, partner, partner_side, tile_knot):
    tiles = positions.shape[2] // TILE_PTS
    strips = lax.axis_size("strip")
    members = lax.axis_size("tile")
    segs = lax.axis_size("seg")

    table, points = pl.pallas_call(
        pack_kernel,
        out_shape=(
            jax.ShapeDtypeStruct((CHANNELS, tiles, TILE_PTS), jnp.float32),
            jax.ShapeDtypeStruct((TILE_ROW * tiles + 8, TILE_PTS), jnp.float32),
        ),
        in_specs=[pl.BlockSpec(memory_space=pltpu.HBM)] * 7,
        out_specs=(pl.BlockSpec(memory_space=pltpu.VMEM),) * 2,
        scratch_shapes=[
            pltpu.VMEM((tiles, TILE_PTS), jnp.int32),
            pltpu.VMEM((2, 1, tiles), jnp.int32),
            pltpu.SemaphoreType.DMA((9,)),
        ],
        compiler_params=params(14),
    )(
        *[
            pltpu.with_memory_space_constraint(array, pltpu.HBM)
            for array in (
                positions.reshape(3, tiles, TILE_PTS),
                covariance.reshape(6, tiles, TILE_PTS),
                lever_arm.reshape(3, tiles, TILE_PTS),
                spline_time.reshape(tiles, TILE_PTS),
                partner.reshape(tiles, TILE_PTS),
                partner_side,
                tile_knot,
            )
        ]
    )

    def trade(first):
        pairs = []
        for strip in range(first, strips - 1, 2):
            pairs += [(strip, strip + 1), (strip + 1, strip)]
        return lax.ppermute(table, "strip", pairs)

    swap = [(member, member ^ 1) for member in range(members)]
    arrived = []
    for hop in range(2, members, 2):
        pairs = [((member + hop) % members, member) for member in range(members)]
        arrived.append(lax.ppermute(points, "tile", pairs))
    near, far = trade(0), trade(1)
    packed, rows = early_rows([points, lax.ppermute(points, "tile", swap)])
    weights, totals = own_totals(2, packed, rows, near, far)
    arrived = lax.optimization_barrier((arrived, near, far, packed))[0]
    others = arrived + [lax.ppermute(group, "tile", swap) for group in arrived]
    sums = all_totals(others, weights, totals)
    all_sums = lax.all_gather(sums, ("seg", "tile"), axis=0)
    adjusted, corrections = pl.pallas_call(
        functools.partial(step_kernel, segs, members),
        out_shape=(
            jax.ShapeDtypeStruct((3, tiles, TILE_PTS), jnp.float32),
            jax.ShapeDtypeStruct((6, 1, KNOT_DEV), jnp.float32),
        ),
        in_specs=smem(1) + vmem(2),
        out_specs=(pl.BlockSpec(memory_space=pltpu.VMEM),) * 2,
        scratch_shapes=[
            pltpu.VMEM((8 * SUM_ROWS, KNOT_DEV), jnp.float32),
            pltpu.VMEM((tiles, KNOT_DEV), jnp.int32),
        ],
        compiler_params=params(6),
    )(tile_knot, all_sums, points)
    return adjusted.reshape(positions.shape), corrections.reshape(1, 6, KNOT_DEV)


def solution(mesh):
    in_specs = (
        P("strip", None, ("seg", "tile")),
        P("strip", None, ("seg", "tile")),
        P("strip", ("seg", "tile")),
        P("strip", None, ("seg", "tile")),
        P("strip", ("seg", "tile")),
        P("strip", ("seg", "tile")),
        P("strip", ("seg", "tile")),
    )
    out_specs = (P("strip", None, ("seg", "tile")), P("strip", None, "seg"))
    return jax.shard_map(local, mesh=mesh, in_specs=in_specs, out_specs=out_specs, check_vma=False)
```

```python
import functools

import jax
import jax.numpy as jnp
from jax import lax
from jax.experimental import pallas as pl
from jax.experimental.pallas import tpu as pltpu
from jax.sharding import PartitionSpec as P

KNOT_DEV = 128
TILE_PTS = 128
CHANNELS = 9
BLOCK_TILES = 4
ROW_GROUP = 16
POINT_ROWS = 16
PARTNER = 13
KNOT = 14
VALID = 15
TILE_ROW = 14
SUM_ROWS = 80

damping = 1.0

PAIRS = [(a, b) for a in range(6) for b in range(a, 6)]


def params(mebibytes=48):
    return pltpu.CompilerParams(vmem_limit_bytes=mebibytes * 2**20)


def vmem(count):
    return [pl.BlockSpec(memory_space=pltpu.VMEM)] * count


def smem(count):
    return [pl.BlockSpec(memory_space=pltpu.SMEM)] * count


def pack_kernel(pos, cov, lever, time, partner, sides, knots, table_ref, points_ref, ints, small, sems):
    tiles = time.shape[0]
    base = TILE_ROW * tiles

    def span(first):
        return points_ref.at[pl.ds(first * tiles, tiles)]

    copies = [
        pltpu.make_async_copy(partner, ints, sems.at[0]),
        pltpu.make_async_copy(sides, small.at[0], sems.at[1]),
        pltpu.make_async_copy(knots, small.at[1], sems.at[2]),
        pltpu.make_async_copy(pos, table_ref.at[pl.ds(0, 3)], sems.at[3]),
        pltpu.make_async_copy(cov, table_ref.at[pl.ds(3, 6)], sems.at[4]),
        pltpu.make_async_copy(time, span(12), sems.at[5]),
    ]
    copies += [pltpu.make_async_copy(lever.at[c], span(9 + c), sems.at[6 + c]) for c in range(3)]
    for copy in copies:
        copy.start()
    for copy in copies:
        copy.wait()
    for channel in range(CHANNELS):
        points_ref[channel * tiles : (channel + 1) * tiles, :] = table_ref[channel]
    points_ref[PARTNER * tiles : (PARTNER + 1) * tiles, :] = ints[...].astype(jnp.float32)
    points_ref[base : base + 8, :] = jnp.zeros((8, TILE_PTS), jnp.float32)
    for place in range(2):
        points_ref[base + place : base + place + 1, 0:tiles] = small[place].astype(jnp.float32)


def split_two(value):
    high = value.astype(jnp.bfloat16)
    low = (value - high.astype(jnp.float32)).astype(jnp.bfloat16)
    return high, low


def row_room(groups, tiles):
    return groups * tiles + 4 * ROW_GROUP


def arrange(points, packed, work):
    compact, codes, places, sem = work
    tiles = (points[0].shape[0] - 8) // TILE_ROW
    total = len(points) * tiles
    room = packed.shape[0] // POINT_ROWS
    shape = (tiles, TILE_PTS)
    lanes = lax.broadcasted_iota(jnp.int32, shape, 1)
    own_tile = lax.broadcasted_iota(jnp.int32, shape, 0)

    def ordered(size, test):
        rows = lax.broadcasted_iota(jnp.int32, (size, size), 0)
        marks = test(rows, lax.broadcasted_iota(jnp.int32, (size, size), 1))
        return jnp.where(marks, 1.0, 0.0).astype(jnp.bfloat16)

    member = lax.axis_index("tile")
    near = jnp.where(lax.axis_index("strip") % 2 == 1, 0.0, 1.0)

    def tile_value(group, place):
        at = TILE_ROW * tiles + place
        return jnp.take_along_axis(
            jnp.broadcast_to(group[at : at + 1, :], shape), own_tile, axis=1, mode="promise_in_bounds"
        )

    marks = []
    for group in points:
        index = group[PARTNER * tiles : (PARTNER + 1) * tiles, :].astype(jnp.int32)
        offset = lax.shift_right_logical(index, 7) - member * tiles
        wanted = (offset >= 0) & (offset < tiles) & (tile_value(group, 0) != 2.0)
        marks.append(jnp.where(wanted, 1.0, 0.0).astype(jnp.bfloat16))
    marks = jnp.concatenate(marks, axis=0)
    number = lax.dot_general(
        jnp.ones((16, TILE_PTS), jnp.bfloat16),
        marks,
        (((1,), (1,)), ((), ())),
        preferred_element_type=jnp.float32,
    )
    base = TILE_ROW * tiles
    sides = jnp.concatenate([group[base : base + 1, 0:tiles] for group in points], axis=1)
    far = jnp.broadcast_to(jnp.where(sides == near, 0.0, 1.0), number.shape)
    upper_rows = lax.broadcasted_iota(jnp.int32, number.shape, 0) < 8
    chosen = jnp.where(upper_rows, number * (1.0 - far), number * far)
    before = jnp.dot(
        chosen.astype(jnp.bfloat16),
        ordered(total, lambda row, lane: row < lane),
        preferred_element_type=jnp.float32,
    )
    ends = (before + chosen).astype(jnp.int32)
    before = before.astype(jnp.int32)
    far = far[0:8] > 0.0
    start = jnp.where(far, before[8:16], before[0:8])
    row = lax.shift_right_logical(start, 7)
    first = jnp.where(far, room - 1 - row, row) * POINT_ROWS
    second = jnp.where(far, first - POINT_ROWS, first + POINT_ROWS)
    line = lax.broadcasted_iota(jnp.int32, (8, total), 0)
    code = jnp.where(line == 0, first, jnp.where(line == 1, second, start & (TILE_PTS - 1)))
    code = jnp.where(line == 3, ends[0:8], jnp.where(line == 4, ends[8:16], code))
    codes[...] = code
    copy = pltpu.make_async_copy(codes, places, sem.at[0])
    copy.start()
    ranks = jnp.dot(
        marks, ordered(TILE_PTS, lambda row, lane: row <= lane), preferred_element_type=jnp.float32
    ).astype(jnp.int32)
    for p, group in enumerate(points):
        rank = ranks[p * tiles : (p + 1) * tiles]
        source = jnp.zeros_like(lanes)
        for jump in (64, 32, 16, 8, 4, 2, 1):
            there = jnp.take_along_axis(
                rank, source + (jump - 1), axis=1, mode="promise_in_bounds"
            )
            source = jnp.where(there <= lanes, source + jump, source)
        for channel in range(POINT_ROWS):
            if channel == VALID:
                value = jnp.where(lanes < jnp.broadcast_to(rank[:, TILE_PTS - 1 :], shape), 1.0, 0.0)
            elif channel == KNOT:
                value = tile_value(group, 1)
            else:
                value = group[channel * tiles : (channel + 1) * tiles, :]
                value = jnp.take_along_axis(value, source, axis=1, mode="promise_in_bounds")
            at = p * tiles * POINT_ROWS + channel
            compact[pl.ds(at, tiles, stride=POINT_ROWS), :] = value
    copy.wait()

    wide = lax.broadcasted_iota(jnp.int32, (POINT_ROWS, TILE_PTS), 1)

    def span(first):
        return pl.ds(pl.multiple_of(first, POINT_ROWS), POINT_ROWS)

    def place(tile):
        shift = places[2, tile]
        value = pltpu.roll(compact[span(tile * POINT_ROWS), :], shift, 1)
        at = span(places[0, tile])
        packed[at, :] = jnp.where(wide >= shift, value, packed[at, :])
        packed[span(places[1, tile]), :] = jnp.where(wide < shift, value, 0.0)

    unroll = tiles

    def several(step, carry):
        for tile in range(unroll):
            place(step * unroll + tile)
        return carry

    lax.fori_loop(0, total // unroll, several, 0)
    near_rows = lax.shift_right_logical(places[3, total - 1] + TILE_PTS - 1, 7)
    far_rows = lax.shift_right_logical(places[4, total - 1] + TILE_PTS - 1, 7)
    blank = jnp.zeros((POINT_ROWS, TILE_PTS), jnp.float32)
    for extra in range(ROW_GROUP):
        packed[span((near_rows + extra) * POINT_ROWS), :] = blank
        packed[span((room - 1 - far_rows - extra) * POINT_ROWS), :] = blank
    return near_rows, far_rows


def weigh_table(table, weights, slot):
    tiles = table.shape[1]
    for channel in range(CHANNELS):
        high, low = split_two(table[channel])
        rows = slice(channel * tiles, (channel + 1) * tiles)
        weights[slot, rows, 0:TILE_PTS] = high
        weights[slot, rows, TILE_PTS : 2 * TILE_PTS] = low


def process(packed, near_rows, far_rows, weights, totals_ref, work):
    target, terms_ref = work
    tiles = weights.shape[1] // CHANNELS
    room = packed.shape[0] // POINT_ROWS
    member = lax.axis_index("tile")
    near_blocks = lax.shift_right_logical(near_rows + BLOCK_TILES - 1, 2)
    far_blocks = lax.shift_right_logical(far_rows + BLOCK_TILES - 1, 2)
    blocks = near_blocks + far_blocks
    queries = BLOCK_TILES * TILE_PTS

    def one_block(block):
        block = jnp.minimum(block, blocks - 1)
        far = block >= near_blocks
        slot = far.astype(jnp.int32)
        base = jnp.where(far, room - BLOCK_TILES * (block - near_blocks + 1), block * BLOCK_TILES)
        ids = [base + j for j in range(BLOCK_TILES)]

        def channel(place):
            rows = [
                packed[pl.ds(base * POINT_ROWS + j * POINT_ROWS + place, 1), :]
                for j in range(BLOCK_TILES)
            ]
            return jnp.concatenate(rows, axis=1)

        index = channel(PARTNER).astype(jnp.int32)
        keys = index & (TILE_PTS - 1)
        rows = lax.shift_right_logical(index, 7) - member * tiles
        rows = jnp.where(channel(VALID) > 0.0, rows, -1)
        hot = jnp.where(
            lax.broadcasted_iota(jnp.int32, (TILE_PTS, queries), 0) == keys, 1.0, 0.0
        ).astype(jnp.bfloat16)
        picked = jnp.dot(
            weights[slot], jnp.concatenate([hot, hot], axis=0), preferred_element_type=jnp.float32
        )
        spread_rows = jnp.broadcast_to(rows, (8, queries))
        eight = lax.broadcasted_iota(jnp.int32, (8, queries), 0)
        found = [jnp.zeros((8, queries), jnp.float32) for _ in range(CHANNELS)]
        for step in range(tiles // 8):
            here = spread_rows == eight + 8 * step
            for channel in range(CHANNELS):
                begin = channel * tiles + 8 * step
                found[channel] = jnp.where(here, picked[begin : begin + 8], found[channel])
        return ids, [jnp.sum(entry, axis=0, keepdims=True) for entry in found]

    def body(step, carry):
        results = [one_block(2 * step), one_block(2 * step + 1)]
        for ids, flat in results:
            for channel in range(CHANNELS):
                for j in range(BLOCK_TILES):
                    piece = flat[channel][:, j * TILE_PTS : (j + 1) * TILE_PTS]
                    target[channel, pl.ds(ids[j], 1), :] = piece
        return carry

    lax.fori_loop(0, lax.shift_right_logical(blocks + 1, 1), body, 0)

    totals_ref[...] = jnp.zeros_like(totals_ref)
    terms_ref[75 * ROW_GROUP :, :] = jnp.zeros((5 * ROW_GROUP, TILE_PTS), jnp.float32)
    near_groups = lax.shift_right_logical(near_rows + ROW_GROUP - 1, 4)
    far_groups = lax.shift_right_logical(far_rows + ROW_GROUP - 1, 4)

    def add(step, carry):
        far = step >= near_groups
        base = jnp.where(far, room - ROW_GROUP * (step - near_groups + 1), step * ROW_GROUP)
        add_rows(pl.multiple_of(base, ROW_GROUP), packed, target, totals_ref, terms_ref)
        return carry

    lax.fori_loop(0, near_groups + far_groups, add, 0)


def add_rows(base, packed, target, totals_ref, terms_ref):
    group = ROW_GROUP
    span = pl.ds(base, group)

    def own(channel):
        return packed[pl.ds(base * POINT_ROWS + channel, group, stride=POINT_ROWS), :]

    valid = own(VALID) > 0.0
    m = [own(3 + c) + target[3 + c, span, :] for c in range(6)]
    residual = [jnp.where(valid, own(c) - target[c, span, :], 0.0) for c in range(3)]
    lever = [own(9 + c) for c in range(3)]
    later = own(12)
    early = 1.0 - later
    adjunct = [
        m[1] * m[2] - m[5] * m[5],
        m[0] * m[2] - m[4] * m[4],
        m[0] * m[1] - m[3] * m[3],
        m[4] * m[5] - m[3] * m[2],
        m[3] * m[5] - m[4] * m[1],
        m[3] * m[4] - m[0] * m[5],
    ]
    determinant = m[0] * adjunct[0] + m[3] * adjunct[3] + m[4] * adjunct[4]
    inv = [jnp.where(valid, entry / determinant, 0.0) for entry in adjunct]
    info = [[inv[0], inv[3], inv[4]], [inv[3], inv[1], inv[5]], [inv[4], inv[5], inv[2]]]

    def turned(column):
        return [
            lever[1] * column[2] - lever[2] * column[1],
            lever[2] * column[0] - lever[0] * column[2],
            lever[0] * column[1] - lever[1] * column[0],
        ] + list(column)

    weighted = [turned(info[i]) for i in range(3)]
    pulled = [
        info[i][0] * residual[0] + info[i][1] * residual[1] + info[i][2] * residual[2]
        for i in range(3)
    ]
    gradient = turned(pulled)
    gram = {}
    for b in range(6):
        column = turned([weighted[i][b] for i in range(3)])
        for a in range(b + 1):
            gram[a, b] = column[a]
    both = early * later
    terms = []
    for weight in (early * early, both, later * later):
        terms += [gram[pair] * weight for pair in PAIRS]
    for weight in (early, later):
        terms += [entry * weight for entry in gradient]
    for place, term in enumerate(terms):
        terms_ref[place * group : (place + 1) * group, :] = term
    knots = own(KNOT).astype(jnp.int32)
    stacked = lax.broadcasted_iota(jnp.int32, (KNOT_DEV, TILE_PTS), 0)
    total = totals_ref[...]
    for row in range(0, group, 2):
        parts, hots = [], []
        for r in (row, row + 1):
            high, low = split_two(terms_ref[pl.ds(r, SUM_ROWS, stride=group), :])
            parts.append(jnp.concatenate([high, low], axis=0))
            hots.append(jnp.where(stacked == knots[r : r + 1], 1.0, 0.0).astype(jnp.bfloat16))
        sums = lax.dot_general(
            jnp.concatenate(parts, axis=1),
            jnp.concatenate(hots, axis=1),
            (((1,), (1,)), ((), ())),
            preferred_element_type=jnp.float32,
        )
        total = total + sums[0:SUM_ROWS] + sums[SUM_ROWS:]
    totals_ref[...] = total


def early_kernel(groups, *refs):
    points = refs[:groups]
    packed, rows_ref = refs[groups : groups + 2]
    near_rows, far_rows = arrange(points, packed, refs[groups + 2 :])
    rows_ref[0:4, :] = jnp.full((4, TILE_PTS), near_rows, jnp.int32)
    rows_ref[4:8, :] = jnp.full((4, TILE_PTS), far_rows, jnp.int32)


def near_kernel(packed, rows_ref, near, weights, totals_ref, rows_here, sem, *work):
    copy = pltpu.make_async_copy(rows_ref, rows_here, sem.at[0])
    copy.start()
    weigh_table(near, weights, 0)
    copy.wait()
    process(packed, rows_here[0, 0], jnp.int32(0), weights, totals_ref, work)


def far_kernel(packed, rows_ref, far, before, before_ref, weights, totals_ref, rows_here, sem, *work):
    copy = pltpu.make_async_copy(rows_ref, rows_here, sem.at[0])
    copy.start()
    weights[0] = before[0]
    weigh_table(far, weights, 1)
    copy.wait()
    process(packed, jnp.int32(0), rows_here[4, 0], weights, totals_ref, work)
    totals_ref[...] = totals_ref[...] + before_ref[...]


def other_kernel(groups, *refs):
    points = refs[:groups]
    weights, before_ref, totals_ref, packed = refs[groups : groups + 4]
    arranging, work = refs[groups + 4 : groups + 8], refs[groups + 8 :]
    near_rows, far_rows = arrange(points, packed, arranging)
    process(packed, near_rows, far_rows, weights, totals_ref, work)
    totals_ref[...] = totals_ref[...] + before_ref[...]


def arrange_shapes(groups, tiles):
    count = groups * tiles
    return [
        pltpu.VMEM((count * POINT_ROWS, TILE_PTS), jnp.float32),
        pltpu.VMEM((8, count), jnp.int32),
        pltpu.SMEM((8, count), jnp.int32),
        pltpu.SemaphoreType.DMA((1,)),
    ]


def process_shapes(groups, tiles):
    return [
        pltpu.VMEM((CHANNELS, row_room(groups, tiles), TILE_PTS), jnp.float32),
        pltpu.VMEM((SUM_ROWS * ROW_GROUP, TILE_PTS), jnp.float32),
    ]


def packed_shape(groups, tiles):
    return (row_room(groups, tiles) * POINT_ROWS, TILE_PTS)


def early_rows(points):
    groups, tiles = len(points), (points[0].shape[0] - 8) // TILE_ROW
    return pl.pallas_call(
        functools.partial(early_kernel, groups),
        out_shape=(
            jax.ShapeDtypeStruct(packed_shape(groups, tiles), jnp.float32),
            jax.ShapeDtypeStruct((8, TILE_PTS), jnp.int32),
        ),
        in_specs=vmem(groups),
        out_specs=(pl.BlockSpec(memory_space=pltpu.VMEM),) * 2,
        scratch_shapes=arrange_shapes(groups, tiles),
        compiler_params=params(14),
    )(*points)


def own_totals(kernel, slots, packed, rows, table, *before):
    tiles = table.shape[1]
    return pl.pallas_call(
        kernel,
        out_shape=(
            jax.ShapeDtypeStruct((slots, CHANNELS * tiles, 2 * TILE_PTS), jnp.bfloat16),
            jax.ShapeDtypeStruct((SUM_ROWS, KNOT_DEV), jnp.float32),
        ),
        in_specs=vmem(3 + len(before)),
        out_specs=(pl.BlockSpec(memory_space=pltpu.VMEM),) * 2,
        scratch_shapes=[pltpu.SMEM((8, TILE_PTS), jnp.int32), pltpu.SemaphoreType.DMA((1,))]
        + process_shapes(2, tiles),
        compiler_params=params(14),
    )(packed, rows, table, *before)


def all_totals(points, weights, totals):
    groups, tiles = len(points), (points[0].shape[0] - 8) // TILE_ROW
    return pl.pallas_call(
        functools.partial(other_kernel, groups),
        out_shape=jax.ShapeDtypeStruct((SUM_ROWS, KNOT_DEV), jnp.float32),
        in_specs=vmem(groups + 2),
        out_specs=pl.BlockSpec(memory_space=pltpu.VMEM),
        scratch_shapes=[pltpu.VMEM(packed_shape(groups, tiles), jnp.float32)]
        + arrange_shapes(groups, tiles)
        + process_shapes(groups, tiles),
        compiler_params=params(24),
    )(*points, weights, totals)


def cholesky(matrix):
    factor = {}
    inverse = []
    for column in range(6):
        pivot = matrix[column, column]
        for inner in range(column):
            pivot = pivot - factor[column, inner] * factor[column, inner]
        inverse.append(1.0 / jnp.sqrt(pivot))
        for row in range(column + 1, 6):
            entry = matrix[column, row]
            for inner in range(column):
                entry = entry - factor[row, inner] * factor[column, inner]
            factor[row, column] = entry * inverse[column]
    return factor, inverse


def solve(system, right_side):
    factor, inverse = system
    forward = []
    for row in range(6):
        entry = right_side[row]
        for inner in range(row):
            entry = entry - factor[row, inner] * forward[inner]
        forward.append(entry * inverse[row])
    answer = [None] * 6
    for row in reversed(range(6)):
        entry = forward[row]
        for inner in range(row + 1, 6):
            entry = entry - factor[inner, row] * answer[inner]
        answer[row] = entry * inverse[row]
    return answer


def step_kernel(segs, members, knot_ref, sums_ref, points_ref, adjusted_ref, out_ref, held, index_ref):
    tiles = knot_ref.shape[1]
    for tile in range(tiles):
        index_ref[tile : tile + 1, :] = jnp.full((1, KNOT_DEV), knot_ref[0, tile], jnp.int32)
    seg = lax.axis_index("seg")
    for place in range(3):
        wanted = seg + place - 1
        there = (wanted >= 0) & (wanted < segs)
        first = jnp.minimum(jnp.maximum(wanted, 0), segs - 1) * members
        total = sums_ref[first]
        for other in range(1, members):
            total = total + sums_ref[first + other]
        held[place * SUM_ROWS : (place + 1) * SUM_ROWS, :] = jnp.where(there, total, 0.0)
    for place in range(3, 8):
        held[place * SUM_ROWS : (place + 1) * SUM_ROWS, :] = jnp.zeros(
            (SUM_ROWS, KNOT_DEV), jnp.float32
        )
    shape = (8, KNOT_DEV)
    lanes = lax.broadcasted_iota(jnp.int32, shape, 1)
    rows = lax.broadcasted_iota(jnp.int32, shape, 0)

    def earlier(value):
        turned = pltpu.roll(value, 1, 1)
        return jnp.where(lanes == 0, pltpu.roll(turned, 1, 0), turned)

    def following(value):
        turned = pltpu.roll(value, KNOT_DEV - 1, 1)
        return jnp.where(lanes == KNOT_DEV - 1, pltpu.roll(turned, 7, 0), turned)

    def quantity(place):
        return held[pl.ds(place, 8, stride=SUM_ROWS), :]

    pair_place = {pair: place for place, pair in enumerate(PAIRS)}
    matrix, cross, cross_before = {}, {}, {}
    for pair, place in pair_place.items():
        value = quantity(place) + earlier(quantity(42 + place))
        matrix[pair] = value + damping if pair[0] == pair[1] else value
        cross[pair] = quantity(21 + place)
        cross_before[pair] = earlier(cross[pair])
    right_side = [quantity(63 + a) + earlier(quantity(69 + a)) for a in range(6)]
    system = cholesky(matrix)
    beyond = (rows >= 2) & (seg == segs - 1)
    first = [jnp.where(beyond, 0.0, -entry) for entry in solve(system, right_side)]
    before = [earlier(entry) for entry in first]
    after = [following(entry) for entry in first]
    corrected = []
    for a in range(6):
        total = right_side[a]
        for b in range(6):
            pair = (min(a, b), max(a, b))
            total = total + cross_before[pair] * before[b] + cross[pair] * after[b]
        corrected.append(total)
    second = [jnp.where(beyond, 0.0, -entry) for entry in solve(system, corrected)]
    upper = [following(entry) for entry in second]
    for a in range(6):
        out_ref[a] = second[a][1:2]
    low_rows = [jnp.broadcast_to(second[a][1:2], shape) for a in range(6)]
    high_rows = [jnp.broadcast_to(upper[a][1:2], shape) for a in range(6)]
    for begin in range(0, tiles, 8):
        span = slice(begin, begin + 8)
        knots = index_ref[span, :]

        def own(channel):
            return points_ref[channel * tiles + begin : channel * tiles + begin + 8, :]

        later = own(12)
        early = 1.0 - later
        pose = []
        for a in range(6):
            low = jnp.take_along_axis(low_rows[a], knots, axis=1, mode="promise_in_bounds")
            high = jnp.take_along_axis(high_rows[a], knots, axis=1, mode="promise_in_bounds")
            pose.append(early * low + later * high)
        lever = [own(c) for c in range(9, 12)]
        moved = [
            pose[1] * lever[2] - pose[2] * lever[1] + pose[3],
            pose[2] * lever[0] - pose[0] * lever[2] + pose[4],
            pose[0] * lever[1] - pose[1] * lever[0] + pose[5],
        ]
        for c in range(3):
            adjusted_ref[c, span, :] = own(c) + moved[c]


def local(positions, lever_arm, spline_time, covariance, partner, partner_side, tile_knot):
    tiles = positions.shape[2] // TILE_PTS
    strips = lax.axis_size("strip")
    members = lax.axis_size("tile")
    segs = lax.axis_size("seg")

    table, points = pl.pallas_call(
        pack_kernel,
        out_shape=(
            jax.ShapeDtypeStruct((CHANNELS, tiles, TILE_PTS), jnp.float32),
            jax.ShapeDtypeStruct((TILE_ROW * tiles + 8, TILE_PTS), jnp.float32),
        ),
        in_specs=[pl.BlockSpec(memory_space=pltpu.HBM)] * 7,
        out_specs=(pl.BlockSpec(memory_space=pltpu.VMEM),) * 2,
        scratch_shapes=[
            pltpu.VMEM((tiles, TILE_PTS), jnp.int32),
            pltpu.VMEM((2, 1, tiles), jnp.int32),
            pltpu.SemaphoreType.DMA((9,)),
        ],
        compiler_params=params(14),
    )(
        *[
            pltpu.with_memory_space_constraint(array, pltpu.HBM)
            for array in (
                positions.reshape(3, tiles, TILE_PTS),
                covariance.reshape(6, tiles, TILE_PTS),
                lever_arm.reshape(3, tiles, TILE_PTS),
                spline_time.reshape(tiles, TILE_PTS),
                partner.reshape(tiles, TILE_PTS),
                partner_side,
                tile_knot,
            )
        ]
    )

    def trade(first):
        pairs = []
        for strip in range(first, strips - 1, 2):
            pairs += [(strip, strip + 1), (strip + 1, strip)]
        return lax.ppermute(table, "strip", pairs)

    swap = [(member, member ^ 1) for member in range(members)]
    arrived = []
    for hop in range(2, members, 2):
        pairs = [((member + hop) % members, member) for member in range(members)]
        arrived.append(lax.ppermute(points, "tile", pairs))
    near, far = trade(0), trade(1)
    packed, rows = early_rows([points, lax.ppermute(points, "tile", swap)])
    weights, totals = own_totals(near_kernel, 1, packed, rows, near)
    arrived = lax.optimization_barrier((arrived, totals, far))[0]
    weights, totals = own_totals(far_kernel, 2, packed, rows, far, weights, totals)
    others = arrived + [lax.ppermute(group, "tile", swap) for group in arrived]
    sums = all_totals(others, weights, totals)
    all_sums = lax.all_gather(sums, ("seg", "tile"), axis=0)
    adjusted, corrections = pl.pallas_call(
        functools.partial(step_kernel, segs, members),
        out_shape=(
            jax.ShapeDtypeStruct((3, tiles, TILE_PTS), jnp.float32),
            jax.ShapeDtypeStruct((6, 1, KNOT_DEV), jnp.float32),
        ),
        in_specs=smem(1) + vmem(2),
        out_specs=(pl.BlockSpec(memory_space=pltpu.VMEM),) * 2,
        scratch_shapes=[
            pltpu.VMEM((8 * SUM_ROWS, KNOT_DEV), jnp.float32),
            pltpu.VMEM((tiles, KNOT_DEV), jnp.int32),
        ],
        compiler_params=params(6),
    )(tile_knot, all_sums, points)
    return adjusted.reshape(positions.shape), corrections.reshape(1, 6, KNOT_DEV)


def solution(mesh):
    in_specs = (
        P("strip", None, ("seg", "tile")),
        P("strip", None, ("seg", "tile")),
        P("strip", ("seg", "tile")),
        P("strip", None, ("seg", "tile")),
        P("strip", ("seg", "tile")),
        P("strip", ("seg", "tile")),
        P("strip", ("seg", "tile")),
    )
    out_specs = (P("strip", None, ("seg", "tile")), P("strip", None, "seg"))
    return jax.shard_map(local, mesh=mesh, in_specs=in_specs, out_specs=out_specs, check_vma=False)
```

```python
import functools

import jax
import jax.numpy as jnp
from jax import lax
from jax.experimental import pallas as pl
from jax.experimental.pallas import tpu as pltpu
from jax.sharding import PartitionSpec as P

KNOT_DEV = 128
TILE_PTS = 128
CHANNELS = 9
BLOCK_TILES = 4
ROW_GROUP = 16
SPREAD = 17
POINT_ROWS = 16
PARTNER = 13
KNOT = 14
VALID = 15
TILE_ROW = 14
SUM_ROWS = 80

damping = 1.0

PAIRS = [(a, b) for a in range(6) for b in range(a, 6)]


def params(mebibytes=48):
    return pltpu.CompilerParams(vmem_limit_bytes=mebibytes * 2**20)


def vmem(count):
    return [pl.BlockSpec(memory_space=pltpu.VMEM)] * count


def smem(count):
    return [pl.BlockSpec(memory_space=pltpu.SMEM)] * count


def pack_kernel(pos, cov, lever, time, partner, sides, knots, table_ref, points_ref, ints, small, sems):
    tiles = time.shape[0]
    base = TILE_ROW * tiles

    def span(first):
        return points_ref.at[pl.ds(first * tiles, tiles)]

    copies = [
        pltpu.make_async_copy(partner, ints, sems.at[0]),
        pltpu.make_async_copy(sides, small.at[0], sems.at[1]),
        pltpu.make_async_copy(knots, small.at[1], sems.at[2]),
        pltpu.make_async_copy(pos, table_ref.at[pl.ds(0, 3)], sems.at[3]),
        pltpu.make_async_copy(cov, table_ref.at[pl.ds(3, 6)], sems.at[4]),
        pltpu.make_async_copy(time, span(12), sems.at[5]),
    ]
    copies += [pltpu.make_async_copy(lever.at[c], span(9 + c), sems.at[6 + c]) for c in range(3)]
    for copy in copies:
        copy.start()
    for copy in copies:
        copy.wait()
    for channel in range(CHANNELS):
        points_ref[channel * tiles : (channel + 1) * tiles, :] = table_ref[channel]
    points_ref[PARTNER * tiles : (PARTNER + 1) * tiles, :] = ints[...].astype(jnp.float32)
    points_ref[base : base + 8, :] = jnp.zeros((8, TILE_PTS), jnp.float32)
    for place in range(2):
        points_ref[base + place : base + place + 1, 0:tiles] = small[place].astype(jnp.float32)


def split_two(value):
    high = value.astype(jnp.bfloat16)
    low = (value - high.astype(jnp.float32)).astype(jnp.bfloat16)
    return high, low


def row_room(groups, tiles):
    return groups * tiles + 4 * ROW_GROUP


def arrange(points, packed, work):
    compact, codes, places, sem = work
    tiles = (points[0].shape[0] - 8) // TILE_ROW
    total = len(points) * tiles
    room = packed.shape[0] // POINT_ROWS
    shape = (tiles, TILE_PTS)
    lanes = lax.broadcasted_iota(jnp.int32, shape, 1)
    own_tile = lax.broadcasted_iota(jnp.int32, shape, 0)

    def ordered(size, test):
        rows = lax.broadcasted_iota(jnp.int32, (size, size), 0)
        marks = test(rows, lax.broadcasted_iota(jnp.int32, (size, size), 1))
        return jnp.where(marks, 1.0, 0.0).astype(jnp.bfloat16)

    member = lax.axis_index("tile")
    near = jnp.where(lax.axis_index("strip") % 2 == 1, 0.0, 1.0)

    def tile_value(group, place):
        at = TILE_ROW * tiles + place
        return jnp.take_along_axis(
            jnp.broadcast_to(group[at : at + 1, :], shape), own_tile, axis=1, mode="promise_in_bounds"
        )

    marks = []
    for group in points:
        index = group[PARTNER * tiles : (PARTNER + 1) * tiles, :].astype(jnp.int32)
        offset = lax.shift_right_logical(index, 7) - member * tiles
        wanted = (offset >= 0) & (offset < tiles) & (tile_value(group, 0) != 2.0)
        marks.append(jnp.where(wanted, 1.0, 0.0).astype(jnp.bfloat16))
    marks = jnp.concatenate(marks, axis=0)
    number = lax.dot_general(
        jnp.ones((16, TILE_PTS), jnp.bfloat16),
        marks,
        (((1,), (1,)), ((), ())),
        preferred_element_type=jnp.float32,
    )
    base = TILE_ROW * tiles
    sides = jnp.concatenate([group[base : base + 1, 0:tiles] for group in points], axis=1)
    far = jnp.broadcast_to(jnp.where(sides == near, 0.0, 1.0), number.shape)
    upper_rows = lax.broadcasted_iota(jnp.int32, number.shape, 0) < 8
    chosen = jnp.where(upper_rows, number * (1.0 - far), number * far)
    before = jnp.dot(
        chosen.astype(jnp.bfloat16),
        ordered(total, lambda row, lane: row < lane),
        preferred_element_type=jnp.float32,
    )
    ends = (before + chosen).astype(jnp.int32)
    before = before.astype(jnp.int32)
    far = far[0:8] > 0.0
    start = jnp.where(far, before[8:16], before[0:8])
    row = lax.shift_right_logical(start, 7)
    first = jnp.where(far, room - 1 - row, row) * POINT_ROWS
    second = jnp.where(far, first - POINT_ROWS, first + POINT_ROWS)
    line = lax.broadcasted_iota(jnp.int32, (8, total), 0)
    code = jnp.where(line == 0, first, jnp.where(line == 1, second, start & (TILE_PTS - 1)))
    code = jnp.where(line == 3, ends[0:8], jnp.where(line == 4, ends[8:16], code))
    codes[...] = code
    copy = pltpu.make_async_copy(codes, places, sem.at[0])
    copy.start()
    ranks = jnp.dot(
        marks, ordered(TILE_PTS, lambda row, lane: row <= lane), preferred_element_type=jnp.float32
    ).astype(jnp.int32)
    for p, group in enumerate(points):
        rank = ranks[p * tiles : (p + 1) * tiles]
        source = jnp.zeros_like(lanes)
        for jump in (64, 32, 16, 8, 4, 2, 1):
            there = jnp.take_along_axis(
                rank, source + (jump - 1), axis=1, mode="promise_in_bounds"
            )
            source = jnp.where(there <= lanes, source + jump, source)
        for channel in range(POINT_ROWS):
            if channel == VALID:
                value = jnp.where(lanes < jnp.broadcast_to(rank[:, TILE_PTS - 1 :], shape), 1.0, 0.0)
            elif channel == KNOT:
                value = tile_value(group, 1)
            else:
                value = group[channel * tiles : (channel + 1) * tiles, :]
                value = jnp.take_along_axis(value, source, axis=1, mode="promise_in_bounds")
            at = p * tiles * POINT_ROWS + channel
            compact[pl.ds(at, tiles, stride=POINT_ROWS), :] = value
    copy.wait()

    wide = lax.broadcasted_iota(jnp.int32, (POINT_ROWS, TILE_PTS), 1)

    def span(first):
        return pl.ds(pl.multiple_of(first, POINT_ROWS), POINT_ROWS)

    def place(tile):
        shift = places[2, tile]
        value = pltpu.roll(compact[span(tile * POINT_ROWS), :], shift, 1)
        at = span(places[0, tile])
        packed[at, :] = jnp.where(wide >= shift, value, packed[at, :])
        packed[span(places[1, tile]), :] = jnp.where(wide < shift, value, 0.0)

    unroll = tiles

    def several(step, carry):
        for tile in range(unroll):
            place(step * unroll + tile)
        return carry

    lax.fori_loop(0, total // unroll, several, 0)
    near_rows = lax.shift_right_logical(places[3, total - 1] + TILE_PTS - 1, 7)
    far_rows = lax.shift_right_logical(places[4, total - 1] + TILE_PTS - 1, 7)
    blank = jnp.zeros((POINT_ROWS, TILE_PTS), jnp.float32)
    for extra in range(ROW_GROUP):
        packed[span((near_rows + extra) * POINT_ROWS), :] = blank
        packed[span((room - 1 - far_rows - extra) * POINT_ROWS), :] = blank
    return near_rows, far_rows


def weigh_table(table, weights, slot):
    tiles = table.shape[1]
    for channel in range(CHANNELS):
        high, low = split_two(table[channel])
        rows = slice(channel * tiles, (channel + 1) * tiles)
        weights[slot, rows, 0:TILE_PTS] = high
        weights[slot, rows, TILE_PTS : 2 * TILE_PTS] = low


def process(packed, near_rows, far_rows, weights, totals_ref, work):
    target, terms_ref = work
    tiles = weights.shape[1] // CHANNELS
    room = packed.shape[0] // POINT_ROWS
    member = lax.axis_index("tile")
    near_blocks = lax.shift_right_logical(near_rows + BLOCK_TILES - 1, 2)
    far_blocks = lax.shift_right_logical(far_rows + BLOCK_TILES - 1, 2)
    blocks = near_blocks + far_blocks
    queries = BLOCK_TILES * TILE_PTS

    def one_block(block):
        block = jnp.minimum(block, blocks - 1)
        far = block >= near_blocks
        slot = far.astype(jnp.int32)
        base = jnp.where(far, room - BLOCK_TILES * (block - near_blocks + 1), block * BLOCK_TILES)
        ids = [base + j for j in range(BLOCK_TILES)]

        def channel(place):
            rows = [
                packed[pl.ds(base * POINT_ROWS + j * POINT_ROWS + place, 1), :]
                for j in range(BLOCK_TILES)
            ]
            return jnp.concatenate(rows, axis=1)

        index = channel(PARTNER).astype(jnp.int32)
        keys = index & (TILE_PTS - 1)
        rows = lax.shift_right_logical(index, 7) - member * tiles
        rows = jnp.where(channel(VALID) > 0.0, rows, -1)
        hot = jnp.where(
            lax.broadcasted_iota(jnp.int32, (TILE_PTS, queries), 0) == keys, 1.0, 0.0
        ).astype(jnp.bfloat16)
        picked = jnp.dot(
            weights[slot], jnp.concatenate([hot, hot], axis=0), preferred_element_type=jnp.float32
        )
        spread_rows = jnp.broadcast_to(rows, (8, queries))
        eight = lax.broadcasted_iota(jnp.int32, (8, queries), 0)
        found = [jnp.zeros((8, queries), jnp.float32) for _ in range(CHANNELS)]
        for step in range(tiles // 8):
            here = spread_rows == eight + 8 * step
            for channel in range(CHANNELS):
                begin = channel * tiles + 8 * step
                found[channel] = jnp.where(here, picked[begin : begin + 8], found[channel])
        return ids, [jnp.sum(entry, axis=0, keepdims=True) for entry in found]

    def body(step, carry):
        results = [one_block(3 * step + i) for i in range(3)]
        for ids, flat in results:
            for channel in range(CHANNELS):
                for j in range(BLOCK_TILES):
                    piece = flat[channel][:, j * TILE_PTS : (j + 1) * TILE_PTS]
                    target[channel, pl.ds(ids[j], 1), :] = piece
        return carry

    lax.fori_loop(0, lax.div(blocks + 2, jnp.int32(3)), body, 0)

    totals_ref[...] = jnp.zeros_like(totals_ref)
    terms_ref[75 * SPREAD :, :] = jnp.zeros((5 * SPREAD, TILE_PTS), jnp.float32)
    near_groups = lax.shift_right_logical(near_rows + ROW_GROUP - 1, 4)
    far_groups = lax.shift_right_logical(far_rows + ROW_GROUP - 1, 4)

    def add(step, carry):
        far = step >= near_groups
        base = jnp.where(far, room - ROW_GROUP * (step - near_groups + 1), step * ROW_GROUP)
        add_rows(pl.multiple_of(base, ROW_GROUP), packed, target, totals_ref, terms_ref)
        return carry

    lax.fori_loop(0, near_groups + far_groups, add, 0)


def add_rows(base, packed, target, totals_ref, terms_ref):
    group = ROW_GROUP
    span = pl.ds(base, group)

    def own(channel):
        return packed[pl.ds(base * POINT_ROWS + channel, group, stride=POINT_ROWS), :]

    valid = own(VALID) > 0.0
    m = [own(3 + c) + target[3 + c, span, :] for c in range(6)]
    residual = [jnp.where(valid, own(c) - target[c, span, :], 0.0) for c in range(3)]
    lever = [own(9 + c) for c in range(3)]
    later = own(12)
    early = 1.0 - later
    adjunct = [
        m[1] * m[2] - m[5] * m[5],
        m[0] * m[2] - m[4] * m[4],
        m[0] * m[1] - m[3] * m[3],
        m[4] * m[5] - m[3] * m[2],
        m[3] * m[5] - m[4] * m[1],
        m[3] * m[4] - m[0] * m[5],
    ]
    determinant = m[0] * adjunct[0] + m[3] * adjunct[3] + m[4] * adjunct[4]
    inv = [jnp.where(valid, entry / determinant, 0.0) for entry in adjunct]
    info = [[inv[0], inv[3], inv[4]], [inv[3], inv[1], inv[5]], [inv[4], inv[5], inv[2]]]

    def turned(column):
        return [
            lever[1] * column[2] - lever[2] * column[1],
            lever[2] * column[0] - lever[0] * column[2],
            lever[0] * column[1] - lever[1] * column[0],
        ] + list(column)

    weighted = [turned(info[i]) for i in range(3)]
    pulled = [
        info[i][0] * residual[0] + info[i][1] * residual[1] + info[i][2] * residual[2]
        for i in range(3)
    ]
    gradient = turned(pulled)
    gram = {}
    for b in range(6):
        column = turned([weighted[i][b] for i in range(3)])
        for a in range(b + 1):
            gram[a, b] = column[a]
    both = early * later
    terms = []
    for weight in (early * early, both, later * later):
        terms += [gram[pair] * weight for pair in PAIRS]
    for weight in (early, later):
        terms += [entry * weight for entry in gradient]
    for place, term in enumerate(terms):
        terms_ref[place * SPREAD : place * SPREAD + group, :] = term
    knots = own(KNOT).astype(jnp.int32)
    stacked = lax.broadcasted_iota(jnp.int32, (KNOT_DEV, TILE_PTS), 0)
    total = totals_ref[...]
    for row in range(0, group, 2):
        parts, hots = [], []
        for r in (row, row + 1):
            high, low = split_two(terms_ref[pl.ds(r, SUM_ROWS, stride=SPREAD), :])
            parts.append(jnp.concatenate([high, low], axis=0))
            hots.append(jnp.where(stacked == knots[r : r + 1], 1.0, 0.0).astype(jnp.bfloat16))
        sums = lax.dot_general(
            jnp.concatenate(parts, axis=1),
            jnp.concatenate(hots, axis=1),
            (((1,), (1,)), ((), ())),
            preferred_element_type=jnp.float32,
        )
        total = total + sums[0:SUM_ROWS] + sums[SUM_ROWS:]
    totals_ref[...] = total


def early_kernel(groups, *refs):
    points = refs[:groups]
    packed, rows_ref = refs[groups : groups + 2]
    near_rows, far_rows = arrange(points, packed, refs[groups + 2 :])
    rows_ref[0:4, :] = jnp.full((4, TILE_PTS), near_rows, jnp.int32)
    rows_ref[4:8, :] = jnp.full((4, TILE_PTS), far_rows, jnp.int32)


def near_kernel(packed, rows_ref, near, weights, totals_ref, rows_here, sem, *work):
    copy = pltpu.make_async_copy(rows_ref, rows_here, sem.at[0])
    copy.start()
    weigh_table(near, weights, 0)
    copy.wait()
    process(packed, rows_here[0, 0], jnp.int32(0), weights, totals_ref, work)


def far_kernel(packed, rows_ref, far, before, before_ref, weights, totals_ref, rows_here, sem, *work):
    copy = pltpu.make_async_copy(rows_ref, rows_here, sem.at[0])
    copy.start()
    weights[0] = before[0]
    weigh_table(far, weights, 1)
    copy.wait()
    process(packed, jnp.int32(0), rows_here[4, 0], weights, totals_ref, work)
    totals_ref[...] = totals_ref[...] + before_ref[...]


def other_kernel(groups, *refs):
    points = refs[:groups]
    weights, before_ref, totals_ref, packed = refs[groups : groups + 4]
    arranging, work = refs[groups + 4 : groups + 8], refs[groups + 8 :]
    near_rows, far_rows = arrange(points, packed, arranging)
    process(packed, near_rows, far_rows, weights, totals_ref, work)
    totals_ref[...] = totals_ref[...] + before_ref[...]


def arrange_shapes(groups, tiles):
    count = groups * tiles
    return [
        pltpu.VMEM((count * POINT_ROWS, TILE_PTS), jnp.float32),
        pltpu.VMEM((8, count), jnp.int32),
        pltpu.SMEM((8, count), jnp.int32),
        pltpu.SemaphoreType.DMA((1,)),
    ]


def process_shapes(groups, tiles):
    return [
        pltpu.VMEM((CHANNELS, row_room(groups, tiles), TILE_PTS), jnp.float32),
        pltpu.VMEM((SUM_ROWS * SPREAD, TILE_PTS), jnp.float32),
    ]


def packed_shape(groups, tiles):
    return (row_room(groups, tiles) * POINT_ROWS, TILE_PTS)


def early_rows(points):
    groups, tiles = len(points), (points[0].shape[0] - 8) // TILE_ROW
    return pl.pallas_call(
        functools.partial(early_kernel, groups),
        out_shape=(
            jax.ShapeDtypeStruct(packed_shape(groups, tiles), jnp.float32),
            jax.ShapeDtypeStruct((8, TILE_PTS), jnp.int32),
        ),
        in_specs=vmem(groups),
        out_specs=(pl.BlockSpec(memory_space=pltpu.VMEM),) * 2,
        scratch_shapes=arrange_shapes(groups, tiles),
        compiler_params=params(14),
    )(*points)


def own_totals(kernel, slots, packed, rows, table, *before):
    tiles = table.shape[1]
    return pl.pallas_call(
        kernel,
        out_shape=(
            jax.ShapeDtypeStruct((slots, CHANNELS * tiles, 2 * TILE_PTS), jnp.bfloat16),
            jax.ShapeDtypeStruct((SUM_ROWS, KNOT_DEV), jnp.float32),
        ),
        in_specs=vmem(3 + len(before)),
        out_specs=(pl.BlockSpec(memory_space=pltpu.VMEM),) * 2,
        scratch_shapes=[pltpu.SMEM((8, TILE_PTS), jnp.int32), pltpu.SemaphoreType.DMA((1,))]
        + process_shapes(2, tiles),
        compiler_params=params(14),
    )(packed, rows, table, *before)


def all_totals(points, weights, totals):
    groups, tiles = len(points), (points[0].shape[0] - 8) // TILE_ROW
    return pl.pallas_call(
        functools.partial(other_kernel, groups),
        out_shape=jax.ShapeDtypeStruct((SUM_ROWS, KNOT_DEV), jnp.float32),
        in_specs=vmem(groups + 2),
        out_specs=pl.BlockSpec(memory_space=pltpu.VMEM),
        scratch_shapes=[pltpu.VMEM(packed_shape(groups, tiles), jnp.float32)]
        + arrange_shapes(groups, tiles)
        + process_shapes(groups, tiles),
        compiler_params=params(24),
    )(*points, weights, totals)


def cholesky(matrix):
    factor = {}
    inverse = []
    for column in range(6):
        pivot = matrix[column, column]
        for inner in range(column):
            pivot = pivot - factor[column, inner] * factor[column, inner]
        inverse.append(1.0 / jnp.sqrt(pivot))
        for row in range(column + 1, 6):
            entry = matrix[column, row]
            for inner in range(column):
                entry = entry - factor[row, inner] * factor[column, inner]
            factor[row, column] = entry * inverse[column]
    return factor, inverse


def solve(system, right_side):
    factor, inverse = system
    forward = []
    for row in range(6):
        entry = right_side[row]
        for inner in range(row):
            entry = entry - factor[row, inner] * forward[inner]
        forward.append(entry * inverse[row])
    answer = [None] * 6
    for row in reversed(range(6)):
        entry = forward[row]
        for inner in range(row + 1, 6):
            entry = entry - factor[inner, row] * answer[inner]
        answer[row] = entry * inverse[row]
    return answer


def step_kernel(segs, members, knot_ref, sums_ref, points_ref, adjusted_ref, out_ref, held, index_ref):
    tiles = knot_ref.shape[1]
    for tile in range(tiles):
        index_ref[tile : tile + 1, :] = jnp.full((1, KNOT_DEV), knot_ref[0, tile], jnp.int32)
    seg = lax.axis_index("seg")
    for place in range(3):
        wanted = seg + place - 1
        there = (wanted >= 0) & (wanted < segs)
        first = jnp.minimum(jnp.maximum(wanted, 0), segs - 1) * members
        total = sums_ref[first]
        for other in range(1, members):
            total = total + sums_ref[first + other]
        held[place * SUM_ROWS : (place + 1) * SUM_ROWS, :] = jnp.where(there, total, 0.0)
    for place in range(3, 8):
        held[place * SUM_ROWS : (place + 1) * SUM_ROWS, :] = jnp.zeros(
            (SUM_ROWS, KNOT_DEV), jnp.float32
        )
    shape = (8, KNOT_DEV)
    lanes = lax.broadcasted_iota(jnp.int32, shape, 1)
    rows = lax.broadcasted_iota(jnp.int32, shape, 0)

    def earlier(value):
        turned = pltpu.roll(value, 1, 1)
        return jnp.where(lanes == 0, pltpu.roll(turned, 1, 0), turned)

    def following(value):
        turned = pltpu.roll(value, KNOT_DEV - 1, 1)
        return jnp.where(lanes == KNOT_DEV - 1, pltpu.roll(turned, 7, 0), turned)

    def quantity(place):
        return held[pl.ds(place, 8, stride=SUM_ROWS), :]

    pair_place = {pair: place for place, pair in enumerate(PAIRS)}
    matrix, cross, cross_before = {}, {}, {}
    for pair, place in pair_place.items():
        value = quantity(place) + earlier(quantity(42 + place))
        matrix[pair] = value + damping if pair[0] == pair[1] else value
        cross[pair] = quantity(21 + place)
        cross_before[pair] = earlier(cross[pair])
    right_side = [quantity(63 + a) + earlier(quantity(69 + a)) for a in range(6)]
    system = cholesky(matrix)
    beyond = (rows >= 2) & (seg == segs - 1)
    first = [jnp.where(beyond, 0.0, -entry) for entry in solve(system, right_side)]
    before = [earlier(entry) for entry in first]
    after = [following(entry) for entry in first]
    corrected = []
    for a in range(6):
        total = right_side[a]
        for b in range(6):
            pair = (min(a, b), max(a, b))
            total = total + cross_before[pair] * before[b] + cross[pair] * after[b]
        corrected.append(total)
    second = [jnp.where(beyond, 0.0, -entry) for entry in solve(system, corrected)]
    upper = [following(entry) for entry in second]
    for a in range(6):
        out_ref[a] = second[a][1:2]
    low_rows = [jnp.broadcast_to(second[a][1:2], shape) for a in range(6)]
    high_rows = [jnp.broadcast_to(upper[a][1:2], shape) for a in range(6)]
    for begin in range(0, tiles, 8):
        span = slice(begin, begin + 8)
        knots = index_ref[span, :]

        def own(channel):
            return points_ref[channel * tiles + begin : channel * tiles + begin + 8, :]

        later = own(12)
        early = 1.0 - later
        pose = []
        for a in range(6):
            low = jnp.take_along_axis(low_rows[a], knots, axis=1, mode="promise_in_bounds")
            high = jnp.take_along_axis(high_rows[a], knots, axis=1, mode="promise_in_bounds")
            pose.append(early * low + later * high)
        lever = [own(c) for c in range(9, 12)]
        moved = [
            pose[1] * lever[2] - pose[2] * lever[1] + pose[3],
            pose[2] * lever[0] - pose[0] * lever[2] + pose[4],
            pose[0] * lever[1] - pose[1] * lever[0] + pose[5],
        ]
        for c in range(3):
            adjusted_ref[c, span, :] = own(c) + moved[c]


def local(positions, lever_arm, spline_time, covariance, partner, partner_side, tile_knot):
    tiles = positions.shape[2] // TILE_PTS
    strips = lax.axis_size("strip")
    members = lax.axis_size("tile")
    segs = lax.axis_size("seg")

    table, points = pl.pallas_call(
        pack_kernel,
        out_shape=(
            jax.ShapeDtypeStruct((CHANNELS, tiles, TILE_PTS), jnp.float32),
            jax.ShapeDtypeStruct((TILE_ROW * tiles + 8, TILE_PTS), jnp.float32),
        ),
        in_specs=[pl.BlockSpec(memory_space=pltpu.HBM)] * 7,
        out_specs=(pl.BlockSpec(memory_space=pltpu.VMEM),) * 2,
        scratch_shapes=[
            pltpu.VMEM((tiles, TILE_PTS), jnp.int32),
            pltpu.VMEM((2, 1, tiles), jnp.int32),
            pltpu.SemaphoreType.DMA((9,)),
        ],
        compiler_params=params(14),
    )(
        *[
            pltpu.with_memory_space_constraint(array, pltpu.HBM)
            for array in (
                positions.reshape(3, tiles, TILE_PTS),
                covariance.reshape(6, tiles, TILE_PTS),
                lever_arm.reshape(3, tiles, TILE_PTS),
                spline_time.reshape(tiles, TILE_PTS),
                partner.reshape(tiles, TILE_PTS),
                partner_side,
                tile_knot,
            )
        ]
    )

    def trade(first):
        pairs = []
        for strip in range(first, strips - 1, 2):
            pairs += [(strip, strip + 1), (strip + 1, strip)]
        return lax.ppermute(table, "strip", pairs)

    swap = [(member, member ^ 1) for member in range(members)]
    arrived = []
    for hop in range(2, members, 2):
        pairs = [((member + hop) % members, member) for member in range(members)]
        arrived.append(lax.ppermute(points, "tile", pairs))
    near, far = trade(0), trade(1)
    packed, rows = early_rows([points, lax.ppermute(points, "tile", swap)])
    weights, totals = own_totals(near_kernel, 1, packed, rows, near)
    arrived = lax.optimization_barrier((arrived, totals, far))[0]
    weights, totals = own_totals(far_kernel, 2, packed, rows, far, weights, totals)
    others = arrived + [lax.ppermute(group, "tile", swap) for group in arrived]
    sums = all_totals(others, weights, totals)
    all_sums = lax.all_gather(sums, ("seg", "tile"), axis=0)
    adjusted, corrections = pl.pallas_call(
        functools.partial(step_kernel, segs, members),
        out_shape=(
            jax.ShapeDtypeStruct((3, tiles, TILE_PTS), jnp.float32),
            jax.ShapeDtypeStruct((6, 1, KNOT_DEV), jnp.float32),
        ),
        in_specs=smem(1) + vmem(2),
        out_specs=(pl.BlockSpec(memory_space=pltpu.VMEM),) * 2,
        scratch_shapes=[
            pltpu.VMEM((8 * SUM_ROWS, KNOT_DEV), jnp.float32),
            pltpu.VMEM((tiles, KNOT_DEV), jnp.int32),
        ],
        compiler_params=params(6),
    )(tile_knot, all_sums, points)
    return adjusted.reshape(positions.shape), corrections.reshape(1, 6, KNOT_DEV)


def solution(mesh):
    in_specs = (
        P("strip", None, ("seg", "tile")),
        P("strip", None, ("seg", "tile")),
        P("strip", ("seg", "tile")),
        P("strip", None, ("seg", "tile")),
        P("strip", ("seg", "tile")),
        P("strip", ("seg", "tile")),
        P("strip", ("seg", "tile")),
    )
    out_specs = (P("strip", None, ("seg", "tile")), P("strip", None, "seg"))
    return jax.shard_map(local, mesh=mesh, in_specs=in_specs, out_specs=out_specs, check_vma=False)
```

```python
import functools

import jax
import jax.numpy as jnp
from jax import lax
from jax.experimental import pallas as pl
from jax.experimental.pallas import tpu as pltpu
from jax.sharding import PartitionSpec as P

KNOT_DEV = 128
TILE_PTS = 128
CHANNELS = 9
BLOCK_TILES = 4
ROW_GROUP = 16
SPREAD = 17
POINT_ROWS = 16
PARTNER = 13
KNOT = 14
VALID = 15
TILE_ROW = 14
SUM_ROWS = 80

damping = 1.0

PAIRS = [(a, b) for a in range(6) for b in range(a, 6)]


def params(mebibytes=48):
    return pltpu.CompilerParams(vmem_limit_bytes=mebibytes * 2**20)


def vmem(count):
    return [pl.BlockSpec(memory_space=pltpu.VMEM)] * count


def pack_kernel(pos, cov, lever, time, partner, sides, knots, table_ref, points_ref, ints, small, sems):
    tiles = time.shape[0]
    base = TILE_ROW * tiles

    def span(first):
        return points_ref.at[pl.ds(first * tiles, tiles)]

    copies = [
        pltpu.make_async_copy(partner, ints, sems.at[0]),
        pltpu.make_async_copy(sides, small.at[0], sems.at[1]),
        pltpu.make_async_copy(knots, small.at[1], sems.at[2]),
        pltpu.make_async_copy(pos, table_ref.at[pl.ds(0, 3)], sems.at[3]),
        pltpu.make_async_copy(cov, table_ref.at[pl.ds(3, 6)], sems.at[4]),
        pltpu.make_async_copy(time, span(12), sems.at[5]),
    ]
    copies += [pltpu.make_async_copy(lever.at[c], span(9 + c), sems.at[6 + c]) for c in range(3)]
    for copy in copies:
        copy.start()
    for copy in copies:
        copy.wait()
    for channel in range(CHANNELS):
        points_ref[channel * tiles : (channel + 1) * tiles, :] = table_ref[channel]
    points_ref[PARTNER * tiles : (PARTNER + 1) * tiles, :] = ints[...].astype(jnp.float32)
    points_ref[base : base + 8, :] = jnp.zeros((8, TILE_PTS), jnp.float32)
    for place in range(2):
        points_ref[base + place : base + place + 1, 0:tiles] = small[place].astype(jnp.float32)


def split_two(value):
    high = value.astype(jnp.bfloat16)
    low = (value - high.astype(jnp.float32)).astype(jnp.bfloat16)
    return high, low


def row_room(groups, tiles):
    return groups * tiles + 4 * ROW_GROUP


def arrange(points, packed, work):
    compact, codes, places, sem = work
    tiles = (points[0].shape[0] - 8) // TILE_ROW
    total = len(points) * tiles
    room = packed.shape[0] // POINT_ROWS
    shape = (tiles, TILE_PTS)
    lanes = lax.broadcasted_iota(jnp.int32, shape, 1)
    own_tile = lax.broadcasted_iota(jnp.int32, shape, 0)

    def ordered(size, test):
        rows = lax.broadcasted_iota(jnp.int32, (size, size), 0)
        marks = test(rows, lax.broadcasted_iota(jnp.int32, (size, size), 1))
        return jnp.where(marks, 1.0, 0.0).astype(jnp.bfloat16)

    member = lax.axis_index("tile")
    near = jnp.where(lax.axis_index("strip") % 2 == 1, 0.0, 1.0)

    def tile_value(group, place):
        at = TILE_ROW * tiles + place
        return jnp.take_along_axis(
            jnp.broadcast_to(group[at : at + 1, :], shape), own_tile, axis=1, mode="promise_in_bounds"
        )

    marks = []
    for group in points:
        index = group[PARTNER * tiles : (PARTNER + 1) * tiles, :].astype(jnp.int32)
        offset = lax.shift_right_logical(index, 7) - member * tiles
        wanted = (offset >= 0) & (offset < tiles) & (tile_value(group, 0) != 2.0)
        marks.append(jnp.where(wanted, 1.0, 0.0).astype(jnp.bfloat16))
    marks = jnp.concatenate(marks, axis=0)
    number = lax.dot_general(
        jnp.ones((16, TILE_PTS), jnp.bfloat16),
        marks,
        (((1,), (1,)), ((), ())),
        preferred_element_type=jnp.float32,
    )
    base = TILE_ROW * tiles
    sides = jnp.concatenate([group[base : base + 1, 0:tiles] for group in points], axis=1)
    far = jnp.broadcast_to(jnp.where(sides == near, 0.0, 1.0), number.shape)
    upper_rows = lax.broadcasted_iota(jnp.int32, number.shape, 0) < 8
    chosen = jnp.where(upper_rows, number * (1.0 - far), number * far)
    before = jnp.dot(
        chosen.astype(jnp.bfloat16),
        ordered(total, lambda row, lane: row < lane),
        preferred_element_type=jnp.float32,
    )
    ends = (before + chosen).astype(jnp.int32)
    before = before.astype(jnp.int32)
    far = far[0:8] > 0.0
    start = jnp.where(far, before[8:16], before[0:8])
    row = lax.shift_right_logical(start, 7)
    first = jnp.where(far, room - 1 - row, row) * POINT_ROWS
    second = jnp.where(far, first - POINT_ROWS, first + POINT_ROWS)
    line = lax.broadcasted_iota(jnp.int32, (8, total), 0)
    code = jnp.where(line == 0, first, jnp.where(line == 1, second, start & (TILE_PTS - 1)))
    code = jnp.where(line == 3, ends[0:8], jnp.where(line == 4, ends[8:16], code))
    codes[...] = code
    copy = pltpu.make_async_copy(codes, places, sem.at[0])
    copy.start()
    ranks = jnp.dot(
        marks, ordered(TILE_PTS, lambda row, lane: row <= lane), preferred_element_type=jnp.float32
    ).astype(jnp.int32)
    for p, group in enumerate(points):
        rank = ranks[p * tiles : (p + 1) * tiles]
        source = jnp.zeros_like(lanes)
        for jump in (64, 32, 16, 8, 4, 2, 1):
            there = jnp.take_along_axis(
                rank, source + (jump - 1), axis=1, mode="promise_in_bounds"
            )
            source = jnp.where(there <= lanes, source + jump, source)
        for channel in range(POINT_ROWS):
            if channel == VALID:
                value = jnp.where(lanes < jnp.broadcast_to(rank[:, TILE_PTS - 1 :], shape), 1.0, 0.0)
            elif channel == KNOT:
                value = tile_value(group, 1)
            else:
                value = group[channel * tiles : (channel + 1) * tiles, :]
                value = jnp.take_along_axis(value, source, axis=1, mode="promise_in_bounds")
            at = p * tiles * POINT_ROWS + channel
            compact[pl.ds(at, tiles, stride=POINT_ROWS), :] = value
    copy.wait()

    wide = lax.broadcasted_iota(jnp.int32, (POINT_ROWS, TILE_PTS), 1)

    def span(first):
        return pl.ds(pl.multiple_of(first, POINT_ROWS), POINT_ROWS)

    def place(tile):
        shift = places[2, tile]
        value = pltpu.roll(compact[span(tile * POINT_ROWS), :], shift, 1)
        at = span(places[0, tile])
        packed[at, :] = jnp.where(wide >= shift, value, packed[at, :])
        packed[span(places[1, tile]), :] = jnp.where(wide < shift, value, 0.0)

    unroll = tiles

    def several(step, carry):
        for tile in range(unroll):
            place(step * unroll + tile)
        return carry

    lax.fori_loop(0, total // unroll, several, 0)
    near_rows = lax.shift_right_logical(places[3, total - 1] + TILE_PTS - 1, 7)
    far_rows = lax.shift_right_logical(places[4, total - 1] + TILE_PTS - 1, 7)
    blank = jnp.zeros((POINT_ROWS, TILE_PTS), jnp.float32)
    for extra in range(ROW_GROUP):
        packed[span((near_rows + extra) * POINT_ROWS), :] = blank
        packed[span((room - 1 - far_rows - extra) * POINT_ROWS), :] = blank
    return near_rows, far_rows


def weigh_table(table, weights, slot):
    tiles = table.shape[1]
    for channel in range(CHANNELS):
        high, low = split_two(table[channel])
        rows = slice(channel * tiles, (channel + 1) * tiles)
        weights[slot, rows, 0:TILE_PTS] = high
        weights[slot, rows, TILE_PTS : 2 * TILE_PTS] = low


def process(packed, near_rows, far_rows, weights, totals_ref, work):
    target, terms_ref = work
    tiles = weights.shape[1] // CHANNELS
    room = packed.shape[0] // POINT_ROWS
    member = lax.axis_index("tile")
    near_blocks = lax.shift_right_logical(near_rows + BLOCK_TILES - 1, 2)
    far_blocks = lax.shift_right_logical(far_rows + BLOCK_TILES - 1, 2)
    blocks = near_blocks + far_blocks
    queries = BLOCK_TILES * TILE_PTS

    def one_block(block):
        block = jnp.minimum(block, blocks - 1)
        far = block >= near_blocks
        slot = far.astype(jnp.int32)
        base = jnp.where(far, room - BLOCK_TILES * (block - near_blocks + 1), block * BLOCK_TILES)
        ids = [base + j for j in range(BLOCK_TILES)]

        def channel(place):
            rows = [
                packed[pl.ds(base * POINT_ROWS + j * POINT_ROWS + place, 1), :]
                for j in range(BLOCK_TILES)
            ]
            return jnp.concatenate(rows, axis=1)

        index = channel(PARTNER).astype(jnp.int32)
        keys = index & (TILE_PTS - 1)
        rows = lax.shift_right_logical(index, 7) - member * tiles
        rows = jnp.where(channel(VALID) > 0.0, rows, -1)
        hot = jnp.where(
            lax.broadcasted_iota(jnp.int32, (TILE_PTS, queries), 0) == keys, 1.0, 0.0
        ).astype(jnp.bfloat16)
        picked = jnp.dot(
            weights[slot], jnp.concatenate([hot, hot], axis=0), preferred_element_type=jnp.float32
        )
        spread_rows = jnp.broadcast_to(rows, (8, queries))
        eight = lax.broadcasted_iota(jnp.int32, (8, queries), 0)
        found = [jnp.zeros((8, queries), jnp.float32) for _ in range(CHANNELS)]
        for step in range(tiles // 8):
            here = spread_rows == eight + 8 * step
            for channel in range(CHANNELS):
                begin = channel * tiles + 8 * step
                found[channel] = jnp.where(here, picked[begin : begin + 8], found[channel])
        return ids, [jnp.sum(entry, axis=0, keepdims=True) for entry in found]

    def body(step, carry):
        results = [one_block(3 * step + i) for i in range(3)]
        for ids, flat in results:
            for channel in range(CHANNELS):
                for j in range(BLOCK_TILES):
                    piece = flat[channel][:, j * TILE_PTS : (j + 1) * TILE_PTS]
                    target[channel, pl.ds(ids[j], 1), :] = piece
        return carry

    lax.fori_loop(0, lax.div(blocks + 2, jnp.int32(3)), body, 0)

    totals_ref[...] = jnp.zeros_like(totals_ref)
    terms_ref[75 * SPREAD :, :] = jnp.zeros((5 * SPREAD, TILE_PTS), jnp.float32)
    near_groups = lax.shift_right_logical(near_rows + ROW_GROUP - 1, 4)
    far_groups = lax.shift_right_logical(far_rows + ROW_GROUP - 1, 4)

    def add(step, carry):
        far = step >= near_groups
        base = jnp.where(far, room - ROW_GROUP * (step - near_groups + 1), step * ROW_GROUP)
        add_rows(pl.multiple_of(base, ROW_GROUP), packed, target, totals_ref, terms_ref)
        return carry

    lax.fori_loop(0, near_groups + far_groups, add, 0)


def add_rows(base, packed, target, totals_ref, terms_ref):
    group = ROW_GROUP
    span = pl.ds(base, group)

    def own(channel):
        return packed[pl.ds(base * POINT_ROWS + channel, group, stride=POINT_ROWS), :]

    valid = own(VALID) > 0.0
    m = [own(3 + c) + target[3 + c, span, :] for c in range(6)]
    residual = [jnp.where(valid, own(c) - target[c, span, :], 0.0) for c in range(3)]
    lever = [own(9 + c) for c in range(3)]
    later = own(12)
    early = 1.0 - later
    adjunct = [
        m[1] * m[2] - m[5] * m[5],
        m[0] * m[2] - m[4] * m[4],
        m[0] * m[1] - m[3] * m[3],
        m[4] * m[5] - m[3] * m[2],
        m[3] * m[5] - m[4] * m[1],
        m[3] * m[4] - m[0] * m[5],
    ]
    determinant = m[0] * adjunct[0] + m[3] * adjunct[3] + m[4] * adjunct[4]
    inv = [jnp.where(valid, entry / determinant, 0.0) for entry in adjunct]
    info = [[inv[0], inv[3], inv[4]], [inv[3], inv[1], inv[5]], [inv[4], inv[5], inv[2]]]

    def turned(column):
        return [
            lever[1] * column[2] - lever[2] * column[1],
            lever[2] * column[0] - lever[0] * column[2],
            lever[0] * column[1] - lever[1] * column[0],
        ] + list(column)

    weighted = [turned(info[i]) for i in range(3)]
    pulled = [
        info[i][0] * residual[0] + info[i][1] * residual[1] + info[i][2] * residual[2]
        for i in range(3)
    ]
    gradient = turned(pulled)
    gram = {}
    for b in range(6):
        column = turned([weighted[i][b] for i in range(3)])
        for a in range(b + 1):
            gram[a, b] = column[a]
    both = early * later
    terms = []
    for weight in (early * early, both, later * later):
        terms += [gram[pair] * weight for pair in PAIRS]
    for weight in (early, later):
        terms += [entry * weight for entry in gradient]
    for place, term in enumerate(terms):
        terms_ref[place * SPREAD : place * SPREAD + group, :] = term
    knots = own(KNOT).astype(jnp.int32)
    stacked = lax.broadcasted_iota(jnp.int32, (KNOT_DEV, TILE_PTS), 0)
    total = totals_ref[...]
    for row in range(0, group, 2):
        parts, hots = [], []
        for r in (row, row + 1):
            high, low = split_two(terms_ref[pl.ds(r, SUM_ROWS, stride=SPREAD), :])
            parts.append(jnp.concatenate([high, low], axis=0))
            hots.append(jnp.where(stacked == knots[r : r + 1], 1.0, 0.0).astype(jnp.bfloat16))
        sums = lax.dot_general(
            jnp.concatenate(parts, axis=1),
            jnp.concatenate(hots, axis=1),
            (((1,), (1,)), ((), ())),
            preferred_element_type=jnp.float32,
        )
        total = total + sums[0:SUM_ROWS] + sums[SUM_ROWS:]
    totals_ref[...] = total


def early_kernel(groups, *refs):
    points = refs[:groups]
    packed, rows_ref = refs[groups : groups + 2]
    near_rows, far_rows = arrange(points, packed, refs[groups + 2 :])
    rows_ref[0:8, :] = jnp.full((8, TILE_PTS), near_rows, jnp.int32)
    rows_ref[8:16, :] = jnp.full((8, TILE_PTS), far_rows, jnp.int32)


def near_kernel(packed, rows_ref, near, weights, totals_ref, *work):
    near_rows = jnp.max(rows_ref[0:8, :])
    weigh_table(near, weights, 0)
    process(packed, near_rows, jnp.int32(0), weights, totals_ref, work)


def far_kernel(packed, rows_ref, far, before, before_ref, weights, totals_ref, *work):
    far_rows = jnp.max(rows_ref[8:16, :])
    weights[0] = before[0]
    weigh_table(far, weights, 1)
    process(packed, jnp.int32(0), far_rows, weights, totals_ref, work)
    totals_ref[...] = totals_ref[...] + before_ref[...]


def other_kernel(groups, *refs):
    points = refs[:groups]
    weights, before_ref, totals_ref, packed = refs[groups : groups + 4]
    arranging, work = refs[groups + 4 : groups + 8], refs[groups + 8 :]
    near_rows, far_rows = arrange(points, packed, arranging)
    process(packed, near_rows, far_rows, weights, totals_ref, work)
    totals_ref[...] = totals_ref[...] + before_ref[...]


def arrange_shapes(groups, tiles):
    count = groups * tiles
    return [
        pltpu.VMEM((count * POINT_ROWS, TILE_PTS), jnp.float32),
        pltpu.VMEM((8, count), jnp.int32),
        pltpu.SMEM((8, count), jnp.int32),
        pltpu.SemaphoreType.DMA((1,)),
    ]


def process_shapes(groups, tiles):
    return [
        pltpu.VMEM((CHANNELS, row_room(groups, tiles), TILE_PTS), jnp.float32),
        pltpu.VMEM((SUM_ROWS * SPREAD, TILE_PTS), jnp.float32),
    ]


def packed_shape(groups, tiles):
    return (row_room(groups, tiles) * POINT_ROWS, TILE_PTS)


def early_rows(points):
    groups, tiles = len(points), (points[0].shape[0] - 8) // TILE_ROW
    return pl.pallas_call(
        functools.partial(early_kernel, groups),
        out_shape=(
            jax.ShapeDtypeStruct(packed_shape(groups, tiles), jnp.float32),
            jax.ShapeDtypeStruct((16, TILE_PTS), jnp.int32),
        ),
        in_specs=vmem(groups),
        out_specs=(pl.BlockSpec(memory_space=pltpu.VMEM),) * 2,
        scratch_shapes=arrange_shapes(groups, tiles),
        compiler_params=params(14),
    )(*points)


def own_totals(kernel, slots, packed, rows, table, *before):
    tiles = table.shape[1]
    return pl.pallas_call(
        kernel,
        out_shape=(
            jax.ShapeDtypeStruct((slots, CHANNELS * tiles, 2 * TILE_PTS), jnp.bfloat16),
            jax.ShapeDtypeStruct((SUM_ROWS, KNOT_DEV), jnp.float32),
        ),
        in_specs=vmem(3 + len(before)),
        out_specs=(pl.BlockSpec(memory_space=pltpu.VMEM),) * 2,
        scratch_shapes=process_shapes(2, tiles),
        compiler_params=params(14),
    )(packed, rows, table, *before)


def all_totals(points, weights, totals):
    groups, tiles = len(points), (points[0].shape[0] - 8) // TILE_ROW
    return pl.pallas_call(
        functools.partial(other_kernel, groups),
        out_shape=jax.ShapeDtypeStruct((SUM_ROWS, KNOT_DEV), jnp.float32),
        in_specs=vmem(groups + 2),
        out_specs=pl.BlockSpec(memory_space=pltpu.VMEM),
        scratch_shapes=[pltpu.VMEM(packed_shape(groups, tiles), jnp.float32)]
        + arrange_shapes(groups, tiles)
        + process_shapes(groups, tiles),
        compiler_params=params(24),
    )(*points, weights, totals)


def cholesky(matrix):
    factor = {}
    inverse = []
    for column in range(6):
        pivot = matrix[column, column]
        for inner in range(column):
            pivot = pivot - factor[column, inner] * factor[column, inner]
        inverse.append(1.0 / jnp.sqrt(pivot))
        for row in range(column + 1, 6):
            entry = matrix[column, row]
            for inner in range(column):
                entry = entry - factor[row, inner] * factor[column, inner]
            factor[row, column] = entry * inverse[column]
    return factor, inverse


def solve(system, right_side):
    factor, inverse = system
    forward = []
    for row in range(6):
        entry = right_side[row]
        for inner in range(row):
            entry = entry - factor[row, inner] * forward[inner]
        forward.append(entry * inverse[row])
    answer = [None] * 6
    for row in reversed(range(6)):
        entry = forward[row]
        for inner in range(row + 1, 6):
            entry = entry - factor[inner, row] * answer[inner]
        answer[row] = entry * inverse[row]
    return answer


def step_kernel(segs, members, sums, points_ref, adjusted_ref, out_ref, held, index_ref):
    tiles = index_ref.shape[0]
    seg = lax.axis_index("seg")
    at = TILE_ROW * tiles + 1
    index_ref[...] = jnp.take_along_axis(
        jnp.broadcast_to(points_ref[at : at + 1, :], index_ref.shape),
        lax.broadcasted_iota(jnp.int32, index_ref.shape, 0),
        axis=1,
        mode="promise_in_bounds",
    ).astype(jnp.int32)
    for place in range(3, 8):
        held[place * SUM_ROWS : (place + 1) * SUM_ROWS, :] = jnp.zeros(
            (SUM_ROWS, KNOT_DEV), jnp.float32
        )
    for place in range(3):
        wanted = seg + place - 1
        there = (wanted >= 0) & (wanted < segs)
        first = jnp.minimum(jnp.maximum(wanted, 0), segs - 1) * members
        total = sums[first]
        for other in range(1, members):
            total = total + sums[first + other]
        held[place * SUM_ROWS : (place + 1) * SUM_ROWS, :] = jnp.where(there, total, 0.0)
    shape = (8, KNOT_DEV)
    lanes = lax.broadcasted_iota(jnp.int32, shape, 1)
    rows = lax.broadcasted_iota(jnp.int32, shape, 0)

    def earlier(value):
        turned = pltpu.roll(value, 1, 1)
        return jnp.where(lanes == 0, pltpu.roll(turned, 1, 0), turned)

    def following(value):
        turned = pltpu.roll(value, KNOT_DEV - 1, 1)
        return jnp.where(lanes == KNOT_DEV - 1, pltpu.roll(turned, 7, 0), turned)

    def quantity(place):
        return held[pl.ds(place, 8, stride=SUM_ROWS), :]

    pair_place = {pair: place for place, pair in enumerate(PAIRS)}
    matrix, cross, cross_before = {}, {}, {}
    for pair, place in pair_place.items():
        value = quantity(place) + earlier(quantity(42 + place))
        matrix[pair] = value + damping if pair[0] == pair[1] else value
        cross[pair] = quantity(21 + place)
        cross_before[pair] = earlier(cross[pair])
    right_side = [quantity(63 + a) + earlier(quantity(69 + a)) for a in range(6)]
    system = cholesky(matrix)
    beyond = (rows >= 2) & (seg == segs - 1)
    first = [jnp.where(beyond, 0.0, -entry) for entry in solve(system, right_side)]
    before = [earlier(entry) for entry in first]
    after = [following(entry) for entry in first]
    corrected = []
    for a in range(6):
        total = right_side[a]
        for b in range(6):
            pair = (min(a, b), max(a, b))
            total = total + cross_before[pair] * before[b] + cross[pair] * after[b]
        corrected.append(total)
    second = [jnp.where(beyond, 0.0, -entry) for entry in solve(system, corrected)]
    upper = [following(entry) for entry in second]
    for a in range(6):
        out_ref[a] = second[a][1:2]
    low_rows = [jnp.broadcast_to(second[a][1:2], shape) for a in range(6)]
    high_rows = [jnp.broadcast_to(upper[a][1:2], shape) for a in range(6)]
    for begin in range(0, tiles, 8):
        span = slice(begin, begin + 8)
        knots = index_ref[span, :]

        def own(channel):
            return points_ref[channel * tiles + begin : channel * tiles + begin + 8, :]

        later = own(12)
        early = 1.0 - later
        pose = []
        for a in range(6):
            low = jnp.take_along_axis(low_rows[a], knots, axis=1, mode="promise_in_bounds")
            high = jnp.take_along_axis(high_rows[a], knots, axis=1, mode="promise_in_bounds")
            pose.append(early * low + later * high)
        lever = [own(c) for c in range(9, 12)]
        moved = [
            pose[1] * lever[2] - pose[2] * lever[1] + pose[3],
            pose[2] * lever[0] - pose[0] * lever[2] + pose[4],
            pose[0] * lever[1] - pose[1] * lever[0] + pose[5],
        ]
        for c in range(3):
            adjusted_ref[c, span, :] = own(c) + moved[c]


def local(positions, lever_arm, spline_time, covariance, partner, partner_side, tile_knot):
    tiles = positions.shape[2] // TILE_PTS
    strips = lax.axis_size("strip")
    members = lax.axis_size("tile")
    segs = lax.axis_size("seg")

    table, points = pl.pallas_call(
        pack_kernel,
        out_shape=(
            jax.ShapeDtypeStruct((CHANNELS, tiles, TILE_PTS), jnp.float32),
            jax.ShapeDtypeStruct((TILE_ROW * tiles + 8, TILE_PTS), jnp.float32),
        ),
        in_specs=[pl.BlockSpec(memory_space=pltpu.HBM)] * 7,
        out_specs=(pl.BlockSpec(memory_space=pltpu.VMEM),) * 2,
        scratch_shapes=[
            pltpu.VMEM((tiles, TILE_PTS), jnp.int32),
            pltpu.VMEM((2, 1, tiles), jnp.int32),
            pltpu.SemaphoreType.DMA((9,)),
        ],
        compiler_params=params(14),
    )(
        *[
            pltpu.with_memory_space_constraint(array, pltpu.HBM)
            for array in (
                positions.reshape(3, tiles, TILE_PTS),
                covariance.reshape(6, tiles, TILE_PTS),
                lever_arm.reshape(3, tiles, TILE_PTS),
                spline_time.reshape(tiles, TILE_PTS),
                partner.reshape(tiles, TILE_PTS),
                partner_side,
                tile_knot,
            )
        ]
    )

    def trade(first):
        pairs = []
        for strip in range(first, strips - 1, 2):
            pairs += [(strip, strip + 1), (strip + 1, strip)]
        return lax.ppermute(table, "strip", pairs)

    swap = [(member, member ^ 1) for member in range(members)]
    arrived = []
    for hop in range(2, members, 2):
        pairs = [((member + hop) % members, member) for member in range(members)]
        arrived.append(lax.ppermute(points, "tile", pairs))
    near, far = trade(0), trade(1)
    packed, rows = early_rows([points, lax.ppermute(points, "tile", swap)])
    weights, totals = own_totals(near_kernel, 1, packed, rows, near)
    arrived = lax.optimization_barrier((arrived, totals, far))[0]
    weights, totals = own_totals(far_kernel, 2, packed, rows, far, weights, totals)
    others = arrived + [lax.ppermute(group, "tile", swap) for group in arrived]
    sums = all_totals(others, weights, totals)
    all_sums = lax.all_gather(sums, ("seg", "tile"), axis=0)
    adjusted, corrections = pl.pallas_call(
        functools.partial(step_kernel, segs, members),
        out_shape=(
            jax.ShapeDtypeStruct((3, tiles, TILE_PTS), jnp.float32),
            jax.ShapeDtypeStruct((6, 1, KNOT_DEV), jnp.float32),
        ),
        in_specs=vmem(2),
        out_specs=(pl.BlockSpec(memory_space=pltpu.VMEM),) * 2,
        scratch_shapes=[
            pltpu.VMEM((8 * SUM_ROWS, KNOT_DEV), jnp.float32),
            pltpu.VMEM((tiles, KNOT_DEV), jnp.int32),
        ],
        compiler_params=params(6),
    )(all_sums, points)
    return adjusted.reshape(positions.shape), corrections.reshape(1, 6, KNOT_DEV)


def solution(mesh):
    in_specs = (
        P("strip", None, ("seg", "tile")),
        P("strip", None, ("seg", "tile")),
        P("strip", ("seg", "tile")),
        P("strip", None, ("seg", "tile")),
        P("strip", ("seg", "tile")),
        P("strip", ("seg", "tile")),
        P("strip", ("seg", "tile")),
    )
    out_specs = (P("strip", None, ("seg", "tile")), P("strip", None, "seg"))
    return jax.shard_map(local, mesh=mesh, in_specs=in_specs, out_specs=out_specs, check_vma=False)
```

```python
import functools

import jax
import jax.numpy as jnp
from jax import lax
from jax.experimental import pallas as pl
from jax.experimental.pallas import tpu as pltpu
from jax.sharding import PartitionSpec as P

KNOT_DEV = 128
TILE_PTS = 128
CHANNELS = 9
BLOCK_TILES = 4
ROW_GROUP = 16
SPREAD = 17
POINT_ROWS = 16
PARTNER = 13
KNOT = 14
VALID = 15
TILE_ROW = 14
SUM_ROWS = 80

damping = 1.0

PAIRS = [(a, b) for a in range(6) for b in range(a, 6)]


def params(mebibytes=48):
    return pltpu.CompilerParams(vmem_limit_bytes=mebibytes * 2**20)


def vmem(count):
    return [pl.BlockSpec(memory_space=pltpu.VMEM)] * count


def pack_kernel(pos, cov, lever, time, partner, sides, knots, table_ref, points_ref, ints, small, sems):
    tiles = time.shape[0]
    base = TILE_ROW * tiles

    def span(first):
        return points_ref.at[pl.ds(first * tiles, tiles)]

    copies = [
        pltpu.make_async_copy(partner, ints, sems.at[0]),
        pltpu.make_async_copy(sides, small.at[0], sems.at[1]),
        pltpu.make_async_copy(knots, small.at[1], sems.at[2]),
        pltpu.make_async_copy(pos, table_ref.at[pl.ds(0, 3)], sems.at[3]),
        pltpu.make_async_copy(cov, table_ref.at[pl.ds(3, 6)], sems.at[4]),
        pltpu.make_async_copy(time, span(12), sems.at[5]),
    ]
    copies += [pltpu.make_async_copy(lever.at[c], span(9 + c), sems.at[6 + c]) for c in range(3)]
    for copy in copies:
        copy.start()
    for copy in copies:
        copy.wait()
    for channel in range(CHANNELS):
        points_ref[channel * tiles : (channel + 1) * tiles, :] = table_ref[channel]
    points_ref[PARTNER * tiles : (PARTNER + 1) * tiles, :] = ints[...].astype(jnp.float32)
    points_ref[base : base + 8, :] = jnp.zeros((8, TILE_PTS), jnp.float32)
    for place in range(2):
        points_ref[base + place : base + place + 1, 0:tiles] = small[place].astype(jnp.float32)


def split_two(value):
    high = value.astype(jnp.bfloat16)
    low = (value - high.astype(jnp.float32)).astype(jnp.bfloat16)
    return high, low


def row_room(groups, tiles):
    return groups * tiles + 4 * ROW_GROUP


def arrange(points, packed, work):
    compact, codes, places, sem = work
    tiles = (points[0].shape[0] - 8) // TILE_ROW
    total = len(points) * tiles
    room = packed.shape[0] // POINT_ROWS
    shape = (tiles, TILE_PTS)
    lanes = lax.broadcasted_iota(jnp.int32, shape, 1)
    own_tile = lax.broadcasted_iota(jnp.int32, shape, 0)

    def ordered(size, test):
        rows = lax.broadcasted_iota(jnp.int32, (size, size), 0)
        marks = test(rows, lax.broadcasted_iota(jnp.int32, (size, size), 1))
        return jnp.where(marks, 1.0, 0.0).astype(jnp.bfloat16)

    member = lax.axis_index("tile")
    near = jnp.where(lax.axis_index("strip") % 2 == 1, 0.0, 1.0)

    def tile_value(group, place):
        at = TILE_ROW * tiles + place
        return jnp.take_along_axis(
            jnp.broadcast_to(group[at : at + 1, :], shape), own_tile, axis=1, mode="promise_in_bounds"
        )

    marks = []
    for group in points:
        index = group[PARTNER * tiles : (PARTNER + 1) * tiles, :].astype(jnp.int32)
        offset = lax.shift_right_logical(index, 7) - member * tiles
        wanted = (offset >= 0) & (offset < tiles) & (tile_value(group, 0) != 2.0)
        marks.append(jnp.where(wanted, 1.0, 0.0).astype(jnp.bfloat16))
    marks = jnp.concatenate(marks, axis=0)
    number = lax.dot_general(
        jnp.ones((16, TILE_PTS), jnp.bfloat16),
        marks,
        (((1,), (1,)), ((), ())),
        preferred_element_type=jnp.float32,
    )
    base = TILE_ROW * tiles
    sides = jnp.concatenate([group[base : base + 1, 0:tiles] for group in points], axis=1)
    far = jnp.broadcast_to(jnp.where(sides == near, 0.0, 1.0), number.shape)
    upper_rows = lax.broadcasted_iota(jnp.int32, number.shape, 0) < 8
    chosen = jnp.where(upper_rows, number * (1.0 - far), number * far)
    before = jnp.dot(
        chosen.astype(jnp.bfloat16),
        ordered(total, lambda row, lane: row < lane),
        preferred_element_type=jnp.float32,
    )
    ends = (before + chosen).astype(jnp.int32)
    before = before.astype(jnp.int32)
    far = far[0:8] > 0.0
    start = jnp.where(far, before[8:16], before[0:8])
    row = lax.shift_right_logical(start, 7)
    first = jnp.where(far, room - 1 - row, row) * POINT_ROWS
    second = jnp.where(far, first - POINT_ROWS, first + POINT_ROWS)
    line = lax.broadcasted_iota(jnp.int32, (8, total), 0)
    code = jnp.where(line == 0, first, jnp.where(line == 1, second, start & (TILE_PTS - 1)))
    code = jnp.where(line == 3, ends[0:8], jnp.where(line == 4, ends[8:16], code))
    codes[...] = code
    copy = pltpu.make_async_copy(codes, places, sem.at[0])
    copy.start()
    ranks = jnp.dot(
        marks, ordered(TILE_PTS, lambda row, lane: row <= lane), preferred_element_type=jnp.float32
    ).astype(jnp.int32)
    for p, group in enumerate(points):
        rank = ranks[p * tiles : (p + 1) * tiles]
        source = jnp.zeros_like(lanes)
        for jump in (64, 32, 16, 8, 4, 2, 1):
            there = jnp.take_along_axis(
                rank, source + (jump - 1), axis=1, mode="promise_in_bounds"
            )
            source = jnp.where(there <= lanes, source + jump, source)
        for channel in range(POINT_ROWS):
            if channel == VALID:
                value = jnp.where(lanes < jnp.broadcast_to(rank[:, TILE_PTS - 1 :], shape), 1.0, 0.0)
            elif channel == KNOT:
                value = tile_value(group, 1)
            else:
                value = group[channel * tiles : (channel + 1) * tiles, :]
                value = jnp.take_along_axis(value, source, axis=1, mode="promise_in_bounds")
            at = p * tiles * POINT_ROWS + channel
            compact[pl.ds(at, tiles, stride=POINT_ROWS), :] = value
    copy.wait()

    wide = lax.broadcasted_iota(jnp.int32, (POINT_ROWS, TILE_PTS), 1)

    def span(first):
        return pl.ds(pl.multiple_of(first, POINT_ROWS), POINT_ROWS)

    def place(tile):
        shift = places[2, tile]
        value = pltpu.roll(compact[span(tile * POINT_ROWS), :], shift, 1)
        at = span(places[0, tile])
        packed[at, :] = jnp.where(wide >= shift, value, packed[at, :])
        packed[span(places[1, tile]), :] = jnp.where(wide < shift, value, 0.0)

    unroll = total if total <= 2 * TILE_PTS else tiles

    def several(step, carry):
        for tile in range(unroll):
            place(step * unroll + tile)
        return carry

    if unroll == total:
        several(0, 0)
    else:
        lax.fori_loop(0, total // unroll, several, 0)
    near_rows = lax.shift_right_logical(places[3, total - 1] + TILE_PTS - 1, 7)
    far_rows = lax.shift_right_logical(places[4, total - 1] + TILE_PTS - 1, 7)
    blank = jnp.zeros((POINT_ROWS, TILE_PTS), jnp.float32)
    for extra in range(ROW_GROUP):
        packed[span((near_rows + extra) * POINT_ROWS), :] = blank
        packed[span((room - 1 - far_rows - extra) * POINT_ROWS), :] = blank
    return near_rows, far_rows


def weigh_table(table, weights, slot):
    tiles = table.shape[1]
    for channel in range(CHANNELS):
        high, low = split_two(table[channel])
        rows = slice(channel * tiles, (channel + 1) * tiles)
        weights[slot, rows, 0:TILE_PTS] = high
        weights[slot, rows, TILE_PTS : 2 * TILE_PTS] = low


def process(packed, near_rows, far_rows, weights, totals_ref, work):
    target, terms_ref = work
    tiles = weights.shape[1] // CHANNELS
    room = packed.shape[0] // POINT_ROWS
    member = lax.axis_index("tile")
    near_blocks = lax.shift_right_logical(near_rows + BLOCK_TILES - 1, 2)
    far_blocks = lax.shift_right_logical(far_rows + BLOCK_TILES - 1, 2)
    blocks = near_blocks + far_blocks
    queries = BLOCK_TILES * TILE_PTS

    def one_block(block):
        far = block >= near_blocks
        slot = far.astype(jnp.int32)
        base = jnp.where(far, room - BLOCK_TILES * (block - near_blocks + 1), block * BLOCK_TILES)
        ids = [base + j for j in range(BLOCK_TILES)]

        def channel(place):
            rows = [
                packed[pl.ds(base * POINT_ROWS + j * POINT_ROWS + place, 1), :]
                for j in range(BLOCK_TILES)
            ]
            return jnp.concatenate(rows, axis=1)

        index = channel(PARTNER).astype(jnp.int32)
        keys = index & (TILE_PTS - 1)
        rows = lax.shift_right_logical(index, 7) - member * tiles
        rows = jnp.where(channel(VALID) > 0.0, rows, -1)
        hot = jnp.where(
            lax.broadcasted_iota(jnp.int32, (TILE_PTS, queries), 0) == keys, 1.0, 0.0
        ).astype(jnp.bfloat16)
        picked = jnp.dot(
            weights[slot], jnp.concatenate([hot, hot], axis=0), preferred_element_type=jnp.float32
        )
        spread_rows = jnp.broadcast_to(rows, (8, queries))
        eight = lax.broadcasted_iota(jnp.int32, (8, queries), 0)
        found = [jnp.zeros((8, queries), jnp.float32) for _ in range(CHANNELS)]
        for step in range(tiles // 8):
            here = spread_rows == eight + 8 * step
            for channel in range(CHANNELS):
                begin = channel * tiles + 8 * step
                found[channel] = jnp.where(here, picked[begin : begin + 8], found[channel])
        return ids, [jnp.sum(entry, axis=0, keepdims=True) for entry in found]

    def pick(first, count):
        results = [one_block(first + i) for i in range(count)]
        for ids, flat in results:
            for channel in range(CHANNELS):
                for j in range(BLOCK_TILES):
                    piece = flat[channel][:, j * TILE_PTS : (j + 1) * TILE_PTS]
                    target[channel, pl.ds(ids[j], 1), :] = piece

    def three(step, carry):
        pick(3 * step, 3)
        return carry

    def one(block, carry):
        pick(block, 1)
        return carry

    threes = lax.div(blocks, jnp.int32(3))
    lax.fori_loop(0, threes, three, 0)
    rest = blocks - 3 * threes

    @pl.when(rest == 1)
    def _():
        pick(3 * threes, 1)

    @pl.when(rest == 2)
    def _():
        pick(3 * threes, 2)

    totals_ref[...] = jnp.zeros_like(totals_ref)
    terms_ref[75 * SPREAD :, :] = jnp.zeros((5 * SPREAD, TILE_PTS), jnp.float32)
    near_groups = lax.shift_right_logical(near_rows + ROW_GROUP - 1, 4)
    far_groups = lax.shift_right_logical(far_rows + ROW_GROUP - 1, 4)

    def add(step, carry):
        far = step >= near_groups
        base = jnp.where(far, room - ROW_GROUP * (step - near_groups + 1), step * ROW_GROUP)
        add_rows(pl.multiple_of(base, ROW_GROUP), packed, target, totals_ref, terms_ref)
        return carry

    lax.fori_loop(0, near_groups + far_groups, add, 0)


def add_rows(base, packed, target, totals_ref, terms_ref):
    group = ROW_GROUP
    span = pl.ds(base, group)

    def own(channel):
        return packed[pl.ds(base * POINT_ROWS + channel, group, stride=POINT_ROWS), :]

    valid = own(VALID) > 0.0
    m = [own(3 + c) + target[3 + c, span, :] for c in range(6)]
    residual = [jnp.where(valid, own(c) - target[c, span, :], 0.0) for c in range(3)]
    lever = [own(9 + c) for c in range(3)]
    later = own(12)
    early = 1.0 - later
    adjunct = [
        m[1] * m[2] - m[5] * m[5],
        m[0] * m[2] - m[4] * m[4],
        m[0] * m[1] - m[3] * m[3],
        m[4] * m[5] - m[3] * m[2],
        m[3] * m[5] - m[4] * m[1],
        m[3] * m[4] - m[0] * m[5],
    ]
    determinant = m[0] * adjunct[0] + m[3] * adjunct[3] + m[4] * adjunct[4]
    inv = [jnp.where(valid, entry / determinant, 0.0) for entry in adjunct]
    info = [[inv[0], inv[3], inv[4]], [inv[3], inv[1], inv[5]], [inv[4], inv[5], inv[2]]]

    def turned(column):
        return [
            lever[1] * column[2] - lever[2] * column[1],
            lever[2] * column[0] - lever[0] * column[2],
            lever[0] * column[1] - lever[1] * column[0],
        ] + list(column)

    weighted = [turned(info[i]) for i in range(3)]
    pulled = [
        info[i][0] * residual[0] + info[i][1] * residual[1] + info[i][2] * residual[2]
        for i in range(3)
    ]
    gradient = turned(pulled)
    gram = {}
    for b in range(6):
        column = turned([weighted[i][b] for i in range(3)])
        for a in range(b + 1):
            gram[a, b] = column[a]
    both = early * later
    terms = []
    for weight in (early * early, both, later * later):
        terms += [gram[pair] * weight for pair in PAIRS]
    for weight in (early, later):
        terms += [entry * weight for entry in gradient]
    for place, term in enumerate(terms):
        terms_ref[place * SPREAD : place * SPREAD + group, :] = term
    knots = own(KNOT).astype(jnp.int32)
    stacked = lax.broadcasted_iota(jnp.int32, (KNOT_DEV, TILE_PTS), 0)
    total = totals_ref[...]
    for row in range(0, group, 2):
        parts, hots = [], []
        for r in (row, row + 1):
            high, low = split_two(terms_ref[pl.ds(r, SUM_ROWS, stride=SPREAD), :])
            parts.append(jnp.concatenate([high, low], axis=0))
            hots.append(jnp.where(stacked == knots[r : r + 1], 1.0, 0.0).astype(jnp.bfloat16))
        sums = lax.dot_general(
            jnp.concatenate(parts, axis=1),
            jnp.concatenate(hots, axis=1),
            (((1,), (1,)), ((), ())),
            preferred_element_type=jnp.float32,
        )
        total = total + sums[0:SUM_ROWS] + sums[SUM_ROWS:]
    totals_ref[...] = total


def early_kernel(groups, *refs):
    points = refs[:groups]
    packed, rows_ref = refs[groups : groups + 2]
    near_rows, far_rows = arrange(points, packed, refs[groups + 2 :])
    rows_ref[0:8, :] = jnp.full((8, TILE_PTS), near_rows, jnp.int32)
    rows_ref[8:16, :] = jnp.full((8, TILE_PTS), far_rows, jnp.int32)


def near_kernel(packed, rows_ref, near, weights, totals_ref, *work):
    near_rows = jnp.max(rows_ref[0:8, :])
    weigh_table(near, weights, 0)
    process(packed, near_rows, jnp.int32(0), weights, totals_ref, work)


def far_kernel(packed, rows_ref, far, before, before_ref, weights, totals_ref, *work):
    far_rows = jnp.max(rows_ref[8:16, :])
    weights[0] = before[0]
    weigh_table(far, weights, 1)
    process(packed, jnp.int32(0), far_rows, weights, totals_ref, work)
    totals_ref[...] = totals_ref[...] + before_ref[...]


def other_kernel(groups, *refs):
    points = refs[:groups]
    weights, before_ref, totals_ref, packed = refs[groups : groups + 4]
    arranging, work = refs[groups + 4 : groups + 8], refs[groups + 8 :]
    near_rows, far_rows = arrange(points, packed, arranging)
    process(packed, near_rows, far_rows, weights, totals_ref, work)
    totals_ref[...] = totals_ref[...] + before_ref[...]


def arrange_shapes(groups, tiles):
    count = groups * tiles
    return [
        pltpu.VMEM((count * POINT_ROWS, TILE_PTS), jnp.float32),
        pltpu.VMEM((8, count), jnp.int32),
        pltpu.SMEM((8, count), jnp.int32),
        pltpu.SemaphoreType.DMA((1,)),
    ]


def process_shapes(groups, tiles):
    return [
        pltpu.VMEM((CHANNELS, row_room(groups, tiles), TILE_PTS), jnp.float32),
        pltpu.VMEM((SUM_ROWS * SPREAD, TILE_PTS), jnp.float32),
    ]


def packed_shape(groups, tiles):
    return (row_room(groups, tiles) * POINT_ROWS, TILE_PTS)


def early_rows(points):
    groups, tiles = len(points), (points[0].shape[0] - 8) // TILE_ROW
    return pl.pallas_call(
        functools.partial(early_kernel, groups),
        out_shape=(
            jax.ShapeDtypeStruct(packed_shape(groups, tiles), jnp.float32),
            jax.ShapeDtypeStruct((16, TILE_PTS), jnp.int32),
        ),
        in_specs=vmem(groups),
        out_specs=(pl.BlockSpec(memory_space=pltpu.VMEM),) * 2,
        scratch_shapes=arrange_shapes(groups, tiles),
        compiler_params=params(14),
    )(*points)


def own_totals(kernel, slots, packed, rows, table, *before):
    tiles = table.shape[1]
    return pl.pallas_call(
        kernel,
        out_shape=(
            jax.ShapeDtypeStruct((slots, CHANNELS * tiles, 2 * TILE_PTS), jnp.bfloat16),
            jax.ShapeDtypeStruct((SUM_ROWS, KNOT_DEV), jnp.float32),
        ),
        in_specs=vmem(3 + len(before)),
        out_specs=(pl.BlockSpec(memory_space=pltpu.VMEM),) * 2,
        scratch_shapes=process_shapes(2, tiles),
        compiler_params=params(14),
    )(packed, rows, table, *before)


def all_totals(points, weights, totals):
    groups, tiles = len(points), (points[0].shape[0] - 8) // TILE_ROW
    return pl.pallas_call(
        functools.partial(other_kernel, groups),
        out_shape=jax.ShapeDtypeStruct((SUM_ROWS, KNOT_DEV), jnp.float32),
        in_specs=vmem(groups + 2),
        out_specs=pl.BlockSpec(memory_space=pltpu.VMEM),
        scratch_shapes=[pltpu.VMEM(packed_shape(groups, tiles), jnp.float32)]
        + arrange_shapes(groups, tiles)
        + process_shapes(groups, tiles),
        compiler_params=params(24),
    )(*points, weights, totals)


def cholesky(matrix):
    factor = {}
    inverse = []
    for column in range(6):
        pivot = matrix[column, column]
        for inner in range(column):
            pivot = pivot - factor[column, inner] * factor[column, inner]
        inverse.append(1.0 / jnp.sqrt(pivot))
        for row in range(column + 1, 6):
            entry = matrix[column, row]
            for inner in range(column):
                entry = entry - factor[row, inner] * factor[column, inner]
            factor[row, column] = entry * inverse[column]
    return factor, inverse


def solve(system, right_side):
    factor, inverse = system
    forward = []
    for row in range(6):
        entry = right_side[row]
        for inner in range(row):
            entry = entry - factor[row, inner] * forward[inner]
        forward.append(entry * inverse[row])
    answer = [None] * 6
    for row in reversed(range(6)):
        entry = forward[row]
        for inner in range(row + 1, 6):
            entry = entry - factor[inner, row] * answer[inner]
        answer[row] = entry * inverse[row]
    return answer


def step_kernel(segs, members, sums, points_ref, adjusted_ref, out_ref, held, index_ref):
    tiles = index_ref.shape[0]
    seg = lax.axis_index("seg")
    at = TILE_ROW * tiles + 1
    index_ref[...] = jnp.take_along_axis(
        jnp.broadcast_to(points_ref[at : at + 1, :], index_ref.shape),
        lax.broadcasted_iota(jnp.int32, index_ref.shape, 0),
        axis=1,
        mode="promise_in_bounds",
    ).astype(jnp.int32)
    for place in range(3, 8):
        held[place * SUM_ROWS : (place + 1) * SUM_ROWS, :] = jnp.zeros(
            (SUM_ROWS, KNOT_DEV), jnp.float32
        )
    for place in range(3):
        wanted = seg + place - 1
        there = (wanted >= 0) & (wanted < segs)
        first = jnp.minimum(jnp.maximum(wanted, 0), segs - 1) * members
        total = sums[first]
        for other in range(1, members):
            total = total + sums[first + other]
        held[place * SUM_ROWS : (place + 1) * SUM_ROWS, :] = jnp.where(there, total, 0.0)
    shape = (8, KNOT_DEV)
    lanes = lax.broadcasted_iota(jnp.int32, shape, 1)
    rows = lax.broadcasted_iota(jnp.int32, shape, 0)

    def earlier(value):
        turned = pltpu.roll(value, 1, 1)
        return jnp.where(lanes == 0, pltpu.roll(turned, 1, 0), turned)

    def following(value):
        turned = pltpu.roll(value, KNOT_DEV - 1, 1)
        return jnp.where(lanes == KNOT_DEV - 1, pltpu.roll(turned, 7, 0), turned)

    def quantity(place):
        return held[pl.ds(place, 8, stride=SUM_ROWS), :]

    pair_place = {pair: place for place, pair in enumerate(PAIRS)}
    matrix, cross, cross_before = {}, {}, {}
    for pair, place in pair_place.items():
        value = quantity(place) + earlier(quantity(42 + place))
        matrix[pair] = value + damping if pair[0] == pair[1] else value
        cross[pair] = quantity(21 + place)
        cross_before[pair] = earlier(cross[pair])
    right_side = [quantity(63 + a) + earlier(quantity(69 + a)) for a in range(6)]
    system = cholesky(matrix)
    beyond = (rows >= 2) & (seg == segs - 1)
    first = [jnp.where(beyond, 0.0, -entry) for entry in solve(system, right_side)]
    before = [earlier(entry) for entry in first]
    after = [following(entry) for entry in first]
    corrected = []
    for a in range(6):
        total = right_side[a]
        for b in range(6):
            pair = (min(a, b), max(a, b))
            total = total + cross_before[pair] * before[b] + cross[pair] * after[b]
        corrected.append(total)
    second = [jnp.where(beyond, 0.0, -entry) for entry in solve(system, corrected)]
    upper = [following(entry) for entry in second]
    for a in range(6):
        out_ref[a] = second[a][1:2]
    low_rows = [jnp.broadcast_to(second[a][1:2], shape) for a in range(6)]
    high_rows = [jnp.broadcast_to(upper[a][1:2], shape) for a in range(6)]
    for begin in range(0, tiles, 8):
        span = slice(begin, begin + 8)
        knots = index_ref[span, :]

        def own(channel):
            return points_ref[channel * tiles + begin : channel * tiles + begin + 8, :]

        later = own(12)
        early = 1.0 - later
        pose = []
        for a in range(6):
            low = jnp.take_along_axis(low_rows[a], knots, axis=1, mode="promise_in_bounds")
            high = jnp.take_along_axis(high_rows[a], knots, axis=1, mode="promise_in_bounds")
            pose.append(early * low + later * high)
        lever = [own(c) for c in range(9, 12)]
        moved = [
            pose[1] * lever[2] - pose[2] * lever[1] + pose[3],
            pose[2] * lever[0] - pose[0] * lever[2] + pose[4],
            pose[0] * lever[1] - pose[1] * lever[0] + pose[5],
        ]
        for c in range(3):
            adjusted_ref[c, span, :] = own(c) + moved[c]


def local(positions, lever_arm, spline_time, covariance, partner, partner_side, tile_knot):
    tiles = positions.shape[2] // TILE_PTS
    strips = lax.axis_size("strip")
    members = lax.axis_size("tile")
    segs = lax.axis_size("seg")

    table, points = pl.pallas_call(
        pack_kernel,
        out_shape=(
            jax.ShapeDtypeStruct((CHANNELS, tiles, TILE_PTS), jnp.float32),
            jax.ShapeDtypeStruct((TILE_ROW * tiles + 8, TILE_PTS), jnp.float32),
        ),
        in_specs=[pl.BlockSpec(memory_space=pltpu.HBM)] * 7,
        out_specs=(pl.BlockSpec(memory_space=pltpu.VMEM),) * 2,
        scratch_shapes=[
            pltpu.VMEM((tiles, TILE_PTS), jnp.int32),
            pltpu.VMEM((2, 1, tiles), jnp.int32),
            pltpu.SemaphoreType.DMA((9,)),
        ],
        compiler_params=params(14),
    )(
        *[
            pltpu.with_memory_space_constraint(array, pltpu.HBM)
            for array in (
                positions.reshape(3, tiles, TILE_PTS),
                covariance.reshape(6, tiles, TILE_PTS),
                lever_arm.reshape(3, tiles, TILE_PTS),
                spline_time.reshape(tiles, TILE_PTS),
                partner.reshape(tiles, TILE_PTS),
                partner_side,
                tile_knot,
            )
        ]
    )

    def trade(first):
        pairs = []
        for strip in range(first, strips - 1, 2):
            pairs += [(strip, strip + 1), (strip + 1, strip)]
        return lax.ppermute(table, "strip", pairs)

    swap = [(member, member ^ 1) for member in range(members)]
    arrived = []
    for hop in range(2, members, 2):
        pairs = [((member + hop) % members, member) for member in range(members)]
        arrived.append(lax.ppermute(points, "tile", pairs))
    near, far = trade(0), trade(1)
    packed, rows = early_rows([points, lax.ppermute(points, "tile", swap)])
    weights, totals = own_totals(near_kernel, 1, packed, rows, near)
    arrived = lax.optimization_barrier((arrived, totals, far))[0]
    weights, totals = own_totals(far_kernel, 2, packed, rows, far, weights, totals)
    others = arrived + [lax.ppermute(group, "tile", swap) for group in arrived]
    sums = all_totals(others, weights, totals)
    all_sums = lax.all_gather(sums, ("seg", "tile"), axis=0)
    adjusted, corrections = pl.pallas_call(
        functools.partial(step_kernel, segs, members),
        out_shape=(
            jax.ShapeDtypeStruct((3, tiles, TILE_PTS), jnp.float32),
            jax.ShapeDtypeStruct((6, 1, KNOT_DEV), jnp.float32),
        ),
        in_specs=vmem(2),
        out_specs=(pl.BlockSpec(memory_space=pltpu.VMEM),) * 2,
        scratch_shapes=[
            pltpu.VMEM((8 * SUM_ROWS, KNOT_DEV), jnp.float32),
            pltpu.VMEM((tiles, KNOT_DEV), jnp.int32),
        ],
        compiler_params=params(6),
    )(all_sums, points)
    return adjusted.reshape(positions.shape), corrections.reshape(1, 6, KNOT_DEV)


def solution(mesh):
    in_specs = (
        P("strip", None, ("seg", "tile")),
        P("strip", None, ("seg", "tile")),
        P("strip", ("seg", "tile")),
        P("strip", None, ("seg", "tile")),
        P("strip", ("seg", "tile")),
        P("strip", ("seg", "tile")),
        P("strip", ("seg", "tile")),
    )
    out_specs = (P("strip", None, ("seg", "tile")), P("strip", None, "seg"))
    return jax.shard_map(local, mesh=mesh, in_specs=in_specs, out_specs=out_specs, check_vma=False)
```

```python
import functools

import jax
import jax.numpy as jnp
from jax import lax
from jax.experimental import pallas as pl
from jax.experimental.pallas import tpu as pltpu
from jax.sharding import PartitionSpec as P

KNOT_DEV = 128
TILE_PTS = 128
CHANNELS = 9
BLOCK_TILES = 4
ROW_GROUP = 16
SPREAD = 17
POINT_ROWS = 16
PARTNER = 13
KNOT = 14
VALID = 15
TILE_ROW = 14
SUM_ROWS = 80

damping = 1.0

PAIRS = [(a, b) for a in range(6) for b in range(a, 6)]


def params(mebibytes=48):
    return pltpu.CompilerParams(vmem_limit_bytes=mebibytes * 2**20)


def vmem(count):
    return [pl.BlockSpec(memory_space=pltpu.VMEM)] * count


def pack_kernel(pos, cov, lever, time, partner, sides, knots, table_ref, points_ref, ints, small, sems):
    tiles = time.shape[0]
    base = TILE_ROW * tiles

    def span(first):
        return points_ref.at[pl.ds(first * tiles, tiles)]

    copies = [
        pltpu.make_async_copy(partner, ints, sems.at[0]),
        pltpu.make_async_copy(sides, small.at[0], sems.at[1]),
        pltpu.make_async_copy(knots, small.at[1], sems.at[2]),
        pltpu.make_async_copy(pos, table_ref.at[pl.ds(0, 3)], sems.at[3]),
        pltpu.make_async_copy(cov, table_ref.at[pl.ds(3, 6)], sems.at[4]),
        pltpu.make_async_copy(time, span(12), sems.at[5]),
    ]
    copies += [pltpu.make_async_copy(lever.at[c], span(9 + c), sems.at[6 + c]) for c in range(3)]
    for copy in copies:
        copy.start()
    for copy in copies:
        copy.wait()
    for channel in range(CHANNELS):
        points_ref[channel * tiles : (channel + 1) * tiles, :] = table_ref[channel]
    points_ref[PARTNER * tiles : (PARTNER + 1) * tiles, :] = ints[...].astype(jnp.float32)
    points_ref[base : base + 8, :] = jnp.zeros((8, TILE_PTS), jnp.float32)
    for place in range(2):
        points_ref[base + place : base + place + 1, 0:tiles] = small[place].astype(jnp.float32)


def split_two(value):
    high = value.astype(jnp.bfloat16)
    low = (value - high.astype(jnp.float32)).astype(jnp.bfloat16)
    return high, low


def row_room(groups, tiles):
    return groups * tiles + 4 * ROW_GROUP


def arrange(points, packed, work):
    compact, codes, places, sem = work
    tiles = (points[0].shape[0] - 8) // TILE_ROW
    total = len(points) * tiles
    room = packed.shape[0] // POINT_ROWS
    shape = (tiles, TILE_PTS)
    lanes = lax.broadcasted_iota(jnp.int32, shape, 1)
    own_tile = lax.broadcasted_iota(jnp.int32, shape, 0)

    def ordered(size, test):
        rows = lax.broadcasted_iota(jnp.int32, (size, size), 0)
        marks = test(rows, lax.broadcasted_iota(jnp.int32, (size, size), 1))
        return jnp.where(marks, 1.0, 0.0).astype(jnp.bfloat16)

    member = lax.axis_index("tile")
    near = jnp.where(lax.axis_index("strip") % 2 == 1, 0.0, 1.0)

    def tile_value(group, place):
        at = TILE_ROW * tiles + place
        return jnp.take_along_axis(
            jnp.broadcast_to(group[at : at + 1, :], shape), own_tile, axis=1, mode="promise_in_bounds"
        )

    marks = []
    for group in points:
        index = group[PARTNER * tiles : (PARTNER + 1) * tiles, :].astype(jnp.int32)
        offset = lax.shift_right_logical(index, 7) - member * tiles
        wanted = (offset >= 0) & (offset < tiles) & (tile_value(group, 0) != 2.0)
        marks.append(jnp.where(wanted, 1.0, 0.0).astype(jnp.bfloat16))
    marks = jnp.concatenate(marks, axis=0)
    ranks = jnp.dot(
        marks, ordered(TILE_PTS, lambda row, lane: row <= lane), preferred_element_type=jnp.float32
    ).astype(jnp.int32)
    sources = []
    for p in range(len(points)):
        rank = ranks[p * tiles : (p + 1) * tiles]
        source = jnp.zeros_like(lanes)
        for jump in (64, 32, 16, 8, 4, 2, 1):
            there = jnp.take_along_axis(
                rank, source + (jump - 1), axis=1, mode="promise_in_bounds"
            )
            source = jnp.where(there <= lanes, source + jump, source)
        sources.append(source)
    number = lax.dot_general(
        jnp.ones((16, TILE_PTS), jnp.bfloat16),
        marks,
        (((1,), (1,)), ((), ())),
        preferred_element_type=jnp.float32,
    )
    base = TILE_ROW * tiles
    sides = jnp.concatenate([group[base : base + 1, 0:tiles] for group in points], axis=1)
    far = jnp.broadcast_to(jnp.where(sides == near, 0.0, 1.0), number.shape)
    upper_rows = lax.broadcasted_iota(jnp.int32, number.shape, 0) < 8
    chosen = jnp.where(upper_rows, number * (1.0 - far), number * far)
    before = jnp.dot(
        chosen.astype(jnp.bfloat16),
        ordered(total, lambda row, lane: row < lane),
        preferred_element_type=jnp.float32,
    )
    ends = (before + chosen).astype(jnp.int32)
    before = before.astype(jnp.int32)
    far = far[0:8] > 0.0
    start = jnp.where(far, before[8:16], before[0:8])
    row = lax.shift_right_logical(start, 7)
    first = jnp.where(far, room - 1 - row, row) * POINT_ROWS
    second = jnp.where(far, first - POINT_ROWS, first + POINT_ROWS)
    line = lax.broadcasted_iota(jnp.int32, (8, total), 0)
    code = jnp.where(line == 0, first, jnp.where(line == 1, second, start & (TILE_PTS - 1)))
    code = jnp.where(line == 3, ends[0:8], jnp.where(line == 4, ends[8:16], code))
    codes[...] = code
    copy = pltpu.make_async_copy(codes, places, sem.at[0])
    copy.start()
    for p, group in enumerate(points):
        rank, source = ranks[p * tiles : (p + 1) * tiles], sources[p]
        for channel in range(POINT_ROWS):
            if channel == VALID:
                value = jnp.where(lanes < jnp.broadcast_to(rank[:, TILE_PTS - 1 :], shape), 1.0, 0.0)
            elif channel == KNOT:
                value = tile_value(group, 1)
            else:
                value = group[channel * tiles : (channel + 1) * tiles, :]
                value = jnp.take_along_axis(value, source, axis=1, mode="promise_in_bounds")
            at = p * tiles * POINT_ROWS + channel
            compact[pl.ds(at, tiles, stride=POINT_ROWS), :] = value
    copy.wait()

    wide = lax.broadcasted_iota(jnp.int32, (POINT_ROWS, TILE_PTS), 1)

    def span(first):
        return pl.ds(pl.multiple_of(first, POINT_ROWS), POINT_ROWS)

    def place(tile):
        shift = places[2, tile]
        value = pltpu.roll(compact[span(tile * POINT_ROWS), :], shift, 1)
        at = span(places[0, tile])
        packed[at, :] = jnp.where(wide >= shift, value, packed[at, :])
        packed[span(places[1, tile]), :] = jnp.where(wide < shift, value, 0.0)

    unroll = total if total <= 2 * TILE_PTS else tiles

    def several(step, carry):
        for tile in range(unroll):
            place(step * unroll + tile)
        return carry

    if unroll == total:
        several(0, 0)
    else:
        lax.fori_loop(0, total // unroll, several, 0)
    near_rows = lax.shift_right_logical(places[3, total - 1] + TILE_PTS - 1, 7)
    far_rows = lax.shift_right_logical(places[4, total - 1] + TILE_PTS - 1, 7)
    blank = jnp.zeros((POINT_ROWS, TILE_PTS), jnp.float32)
    for extra in range(ROW_GROUP):
        packed[span((near_rows + extra) * POINT_ROWS), :] = blank
        packed[span((room - 1 - far_rows - extra) * POINT_ROWS), :] = blank
    return near_rows, far_rows


def weigh_table(table, weights, slot):
    tiles = table.shape[1]
    for channel in range(CHANNELS):
        high, low = split_two(table[channel])
        rows = slice(channel * tiles, (channel + 1) * tiles)
        weights[slot, rows, 0:TILE_PTS] = high
        weights[slot, rows, TILE_PTS : 2 * TILE_PTS] = low


def process(packed, near_rows, far_rows, weights, totals_ref, work):
    target, terms_ref = work
    tiles = weights.shape[1] // CHANNELS
    room = packed.shape[0] // POINT_ROWS
    member = lax.axis_index("tile")
    near_blocks = lax.shift_right_logical(near_rows + BLOCK_TILES - 1, 2)
    far_blocks = lax.shift_right_logical(far_rows + BLOCK_TILES - 1, 2)
    blocks = near_blocks + far_blocks
    queries = BLOCK_TILES * TILE_PTS

    def one_block(block):
        far = block >= near_blocks
        slot = far.astype(jnp.int32)
        base = jnp.where(far, room - BLOCK_TILES * (block - near_blocks + 1), block * BLOCK_TILES)
        ids = [base + j for j in range(BLOCK_TILES)]

        def channel(place):
            rows = [
                packed[pl.ds(base * POINT_ROWS + j * POINT_ROWS + place, 1), :]
                for j in range(BLOCK_TILES)
            ]
            return jnp.concatenate(rows, axis=1)

        index = channel(PARTNER).astype(jnp.int32)
        keys = index & (TILE_PTS - 1)
        rows = lax.shift_right_logical(index, 7) - member * tiles
        rows = jnp.where(channel(VALID) > 0.0, rows, -1)
        hot = jnp.where(
            lax.broadcasted_iota(jnp.int32, (TILE_PTS, queries), 0) == keys, 1.0, 0.0
        ).astype(jnp.bfloat16)
        picked = jnp.dot(
            weights[slot], jnp.concatenate([hot, hot], axis=0), preferred_element_type=jnp.float32
        )
        spread_rows = jnp.broadcast_to(rows, (8, queries))
        eight = lax.broadcasted_iota(jnp.int32, (8, queries), 0)
        found = [jnp.zeros((8, queries), jnp.float32) for _ in range(CHANNELS)]
        for step in range(tiles // 8):
            here = spread_rows == eight + 8 * step
            for channel in range(CHANNELS):
                begin = channel * tiles + 8 * step
                found[channel] = jnp.where(here, picked[begin : begin + 8], found[channel])
        return ids, [jnp.sum(entry, axis=0, keepdims=True) for entry in found]

    def pick(first, count):
        results = [one_block(first + i) for i in range(count)]
        for ids, flat in results:
            for channel in range(CHANNELS):
                for j in range(BLOCK_TILES):
                    piece = flat[channel][:, j * TILE_PTS : (j + 1) * TILE_PTS]
                    target[channel, pl.ds(ids[j], 1), :] = piece

    def three(step, carry):
        pick(3 * step, 3)
        return carry

    def one(block, carry):
        pick(block, 1)
        return carry

    threes = lax.div(blocks, jnp.int32(3))
    lax.fori_loop(0, threes, three, 0)
    rest = blocks - 3 * threes

    @pl.when(rest == 1)
    def _():
        pick(3 * threes, 1)

    @pl.when(rest == 2)
    def _():
        pick(3 * threes, 2)

    totals_ref[...] = jnp.zeros_like(totals_ref)
    terms_ref[75 * SPREAD :, :] = jnp.zeros((5 * SPREAD, TILE_PTS), jnp.float32)
    near_groups = lax.shift_right_logical(near_rows + ROW_GROUP - 1, 4)
    far_groups = lax.shift_right_logical(far_rows + ROW_GROUP - 1, 4)

    def add(step, carry):
        far = step >= near_groups
        base = jnp.where(far, room - ROW_GROUP * (step - near_groups + 1), step * ROW_GROUP)
        add_rows(pl.multiple_of(base, ROW_GROUP), packed, target, totals_ref, terms_ref)
        return carry

    lax.fori_loop(0, near_groups + far_groups, add, 0)


def add_rows(base, packed, target, totals_ref, terms_ref):
    group = ROW_GROUP
    span = pl.ds(base, group)

    def own(channel):
        return packed[pl.ds(base * POINT_ROWS + channel, group, stride=POINT_ROWS), :]

    valid = own(VALID) > 0.0
    m = [own(3 + c) + target[3 + c, span, :] for c in range(6)]
    residual = [jnp.where(valid, own(c) - target[c, span, :], 0.0) for c in range(3)]
    lever = [own(9 + c) for c in range(3)]
    later = own(12)
    early = 1.0 - later
    adjunct = [
        m[1] * m[2] - m[5] * m[5],
        m[0] * m[2] - m[4] * m[4],
        m[0] * m[1] - m[3] * m[3],
        m[4] * m[5] - m[3] * m[2],
        m[3] * m[5] - m[4] * m[1],
        m[3] * m[4] - m[0] * m[5],
    ]
    determinant = m[0] * adjunct[0] + m[3] * adjunct[3] + m[4] * adjunct[4]
    inv = [jnp.where(valid, entry / determinant, 0.0) for entry in adjunct]
    info = [[inv[0], inv[3], inv[4]], [inv[3], inv[1], inv[5]], [inv[4], inv[5], inv[2]]]

    def turned(column):
        return [
            lever[1] * column[2] - lever[2] * column[1],
            lever[2] * column[0] - lever[0] * column[2],
            lever[0] * column[1] - lever[1] * column[0],
        ] + list(column)

    weighted = [turned(info[i]) for i in range(3)]
    pulled = [
        info[i][0] * residual[0] + info[i][1] * residual[1] + info[i][2] * residual[2]
        for i in range(3)
    ]
    gradient = turned(pulled)
    gram = {}
    for b in range(6):
        column = turned([weighted[i][b] for i in range(3)])
        for a in range(b + 1):
            gram[a, b] = column[a]
    both = early * later
    terms = []
    for weight in (early * early, both, later * later):
        terms += [gram[pair] * weight for pair in PAIRS]
    for weight in (early, later):
        terms += [entry * weight for entry in gradient]
    for place, term in enumerate(terms):
        terms_ref[place * SPREAD : place * SPREAD + group, :] = term
    knots = own(KNOT).astype(jnp.int32)
    stacked = lax.broadcasted_iota(jnp.int32, (KNOT_DEV, TILE_PTS), 0)
    total = totals_ref[...]
    for row in range(0, group, 2):
        parts, hots = [], []
        for r in (row, row + 1):
            high, low = split_two(terms_ref[pl.ds(r, SUM_ROWS, stride=SPREAD), :])
            parts.append(jnp.concatenate([high, low], axis=0))
            hots.append(jnp.where(stacked == knots[r : r + 1], 1.0, 0.0).astype(jnp.bfloat16))
        sums = lax.dot_general(
            jnp.concatenate(parts, axis=1),
            jnp.concatenate(hots, axis=1),
            (((1,), (1,)), ((), ())),
            preferred_element_type=jnp.float32,
        )
        total = total + sums[0:SUM_ROWS] + sums[SUM_ROWS:]
    totals_ref[...] = total


def early_kernel(groups, *refs):
    points = refs[:groups]
    packed, rows_ref = refs[groups : groups + 2]
    near_rows, far_rows = arrange(points, packed, refs[groups + 2 :])
    rows_ref[0:8, :] = jnp.full((8, TILE_PTS), near_rows, jnp.int32)
    rows_ref[8:16, :] = jnp.full((8, TILE_PTS), far_rows, jnp.int32)


def near_kernel(packed, rows_ref, near, weights, totals_ref, *work):
    near_rows = jnp.max(rows_ref[0:8, :])
    weigh_table(near, weights, 0)
    process(packed, near_rows, jnp.int32(0), weights, totals_ref, work)


def far_kernel(packed, rows_ref, far, before, before_ref, weights, totals_ref, *work):
    far_rows = jnp.max(rows_ref[8:16, :])
    weights[0] = before[0]
    weigh_table(far, weights, 1)
    process(packed, jnp.int32(0), far_rows, weights, totals_ref, work)
    totals_ref[...] = totals_ref[...] + before_ref[...]


def other_kernel(groups, *refs):
    points = refs[:groups]
    weights, before_ref, totals_ref, packed = refs[groups : groups + 4]
    arranging, work = refs[groups + 4 : groups + 8], refs[groups + 8 :]
    near_rows, far_rows = arrange(points, packed, arranging)
    process(packed, near_rows, far_rows, weights, totals_ref, work)
    totals_ref[...] = totals_ref[...] + before_ref[...]


def arrange_shapes(groups, tiles):
    count = groups * tiles
    return [
        pltpu.VMEM((count * POINT_ROWS, TILE_PTS), jnp.float32),
        pltpu.VMEM((8, count), jnp.int32),
        pltpu.SMEM((8, count), jnp.int32),
        pltpu.SemaphoreType.DMA((1,)),
    ]


def process_shapes(groups, tiles):
    return [
        pltpu.VMEM((CHANNELS, row_room(groups, tiles), TILE_PTS), jnp.float32),
        pltpu.VMEM((SUM_ROWS * SPREAD, TILE_PTS), jnp.float32),
    ]


def packed_shape(groups, tiles):
    return (row_room(groups, tiles) * POINT_ROWS, TILE_PTS)


def early_rows(points):
    groups, tiles = len(points), (points[0].shape[0] - 8) // TILE_ROW
    return pl.pallas_call(
        functools.partial(early_kernel, groups),
        out_shape=(
            jax.ShapeDtypeStruct(packed_shape(groups, tiles), jnp.float32),
            jax.ShapeDtypeStruct((16, TILE_PTS), jnp.int32),
        ),
        in_specs=vmem(groups),
        out_specs=(pl.BlockSpec(memory_space=pltpu.VMEM),) * 2,
        scratch_shapes=arrange_shapes(groups, tiles),
        compiler_params=params(14),
    )(*points)


def own_totals(kernel, slots, packed, rows, table, *before):
    tiles = table.shape[1]
    return pl.pallas_call(
        kernel,
        out_shape=(
            jax.ShapeDtypeStruct((slots, CHANNELS * tiles, 2 * TILE_PTS), jnp.bfloat16),
            jax.ShapeDtypeStruct((SUM_ROWS, KNOT_DEV), jnp.float32),
        ),
        in_specs=vmem(3 + len(before)),
        out_specs=(pl.BlockSpec(memory_space=pltpu.VMEM),) * 2,
        scratch_shapes=process_shapes(2, tiles),
        compiler_params=params(14),
    )(packed, rows, table, *before)


def all_totals(points, weights, totals):
    groups, tiles = len(points), (points[0].shape[0] - 8) // TILE_ROW
    return pl.pallas_call(
        functools.partial(other_kernel, groups),
        out_shape=jax.ShapeDtypeStruct((SUM_ROWS, KNOT_DEV), jnp.float32),
        in_specs=vmem(groups + 2),
        out_specs=pl.BlockSpec(memory_space=pltpu.VMEM),
        scratch_shapes=[pltpu.VMEM(packed_shape(groups, tiles), jnp.float32)]
        + arrange_shapes(groups, tiles)
        + process_shapes(groups, tiles),
        compiler_params=params(24),
    )(*points, weights, totals)


def cholesky(matrix):
    factor = {}
    inverse = []
    for column in range(6):
        pivot = matrix[column, column]
        for inner in range(column):
            pivot = pivot - factor[column, inner] * factor[column, inner]
        inverse.append(1.0 / jnp.sqrt(pivot))
        for row in range(column + 1, 6):
            entry = matrix[column, row]
            for inner in range(column):
                entry = entry - factor[row, inner] * factor[column, inner]
            factor[row, column] = entry * inverse[column]
    return factor, inverse


def solve(system, right_side):
    factor, inverse = system
    forward = []
    for row in range(6):
        entry = right_side[row]
        for inner in range(row):
            entry = entry - factor[row, inner] * forward[inner]
        forward.append(entry * inverse[row])
    answer = [None] * 6
    for row in reversed(range(6)):
        entry = forward[row]
        for inner in range(row + 1, 6):
            entry = entry - factor[inner, row] * answer[inner]
        answer[row] = entry * inverse[row]
    return answer


def step_kernel(segs, members, sums, points_ref, adjusted_ref, out_ref, held, index_ref):
    tiles = index_ref.shape[0]
    seg = lax.axis_index("seg")
    at = TILE_ROW * tiles + 1
    index_ref[...] = jnp.take_along_axis(
        jnp.broadcast_to(points_ref[at : at + 1, :], index_ref.shape),
        lax.broadcasted_iota(jnp.int32, index_ref.shape, 0),
        axis=1,
        mode="promise_in_bounds",
    ).astype(jnp.int32)
    for place in range(3, 8):
        held[place * SUM_ROWS : (place + 1) * SUM_ROWS, :] = jnp.zeros(
            (SUM_ROWS, KNOT_DEV), jnp.float32
        )
    for place in range(3):
        wanted = seg + place - 1
        there = (wanted >= 0) & (wanted < segs)
        first = jnp.minimum(jnp.maximum(wanted, 0), segs - 1) * members
        total = sums[first]
        for other in range(1, members):
            total = total + sums[first + other]
        held[place * SUM_ROWS : (place + 1) * SUM_ROWS, :] = jnp.where(there, total, 0.0)
    shape = (8, KNOT_DEV)
    lanes = lax.broadcasted_iota(jnp.int32, shape, 1)
    rows = lax.broadcasted_iota(jnp.int32, shape, 0)

    def earlier(value):
        turned = pltpu.roll(value, 1, 1)
        return jnp.where(lanes == 0, pltpu.roll(turned, 1, 0), turned)

    def following(value):
        turned = pltpu.roll(value, KNOT_DEV - 1, 1)
        return jnp.where(lanes == KNOT_DEV - 1, pltpu.roll(turned, 7, 0), turned)

    def quantity(place):
        return held[pl.ds(place, 8, stride=SUM_ROWS), :]

    pair_place = {pair: place for place, pair in enumerate(PAIRS)}
    matrix, cross, cross_before = {}, {}, {}
    for pair, place in pair_place.items():
        value = quantity(place) + earlier(quantity(42 + place))
        matrix[pair] = value + damping if pair[0] == pair[1] else value
        cross[pair] = quantity(21 + place)
        cross_before[pair] = earlier(cross[pair])
    right_side = [quantity(63 + a) + earlier(quantity(69 + a)) for a in range(6)]
    system = cholesky(matrix)
    beyond = (rows >= 2) & (seg == segs - 1)
    first = [jnp.where(beyond, 0.0, -entry) for entry in solve(system, right_side)]
    before = [earlier(entry) for entry in first]
    after = [following(entry) for entry in first]
    corrected = []
    for a in range(6):
        total = right_side[a]
        for b in range(6):
            pair = (min(a, b), max(a, b))
            total = total + cross_before[pair] * before[b] + cross[pair] * after[b]
        corrected.append(total)
    second = [jnp.where(beyond, 0.0, -entry) for entry in solve(system, corrected)]
    upper = [following(entry) for entry in second]
    for a in range(6):
        out_ref[a] = second[a][1:2]
    low_rows = [jnp.broadcast_to(second[a][1:2], shape) for a in range(6)]
    high_rows = [jnp.broadcast_to(upper[a][1:2], shape) for a in range(6)]
    for begin in range(0, tiles, 8):
        span = slice(begin, begin + 8)
        knots = index_ref[span, :]

        def own(channel):
            return points_ref[channel * tiles + begin : channel * tiles + begin + 8, :]

        later = own(12)
        early = 1.0 - later
        pose = []
        for a in range(6):
            low = jnp.take_along_axis(low_rows[a], knots, axis=1, mode="promise_in_bounds")
            high = jnp.take_along_axis(high_rows[a], knots, axis=1, mode="promise_in_bounds")
            pose.append(early * low + later * high)
        lever = [own(c) for c in range(9, 12)]
        moved = [
            pose[1] * lever[2] - pose[2] * lever[1] + pose[3],
            pose[2] * lever[0] - pose[0] * lever[2] + pose[4],
            pose[0] * lever[1] - pose[1] * lever[0] + pose[5],
        ]
        for c in range(3):
            adjusted_ref[c, span, :] = own(c) + moved[c]


def local(positions, lever_arm, spline_time, covariance, partner, partner_side, tile_knot):
    tiles = positions.shape[2] // TILE_PTS
    strips = lax.axis_size("strip")
    members = lax.axis_size("tile")
    segs = lax.axis_size("seg")

    table, points = pl.pallas_call(
        pack_kernel,
        out_shape=(
            jax.ShapeDtypeStruct((CHANNELS, tiles, TILE_PTS), jnp.float32),
            jax.ShapeDtypeStruct((TILE_ROW * tiles + 8, TILE_PTS), jnp.float32),
        ),
        in_specs=[pl.BlockSpec(memory_space=pltpu.HBM)] * 7,
        out_specs=(pl.BlockSpec(memory_space=pltpu.VMEM),) * 2,
        scratch_shapes=[
            pltpu.VMEM((tiles, TILE_PTS), jnp.int32),
            pltpu.VMEM((2, 1, tiles), jnp.int32),
            pltpu.SemaphoreType.DMA((9,)),
        ],
        compiler_params=params(14),
    )(
        *[
            pltpu.with_memory_space_constraint(array, pltpu.HBM)
            for array in (
                positions.reshape(3, tiles, TILE_PTS),
                covariance.reshape(6, tiles, TILE_PTS),
                lever_arm.reshape(3, tiles, TILE_PTS),
                spline_time.reshape(tiles, TILE_PTS),
                partner.reshape(tiles, TILE_PTS),
                partner_side,
                tile_knot,
            )
        ]
    )

    def trade(first):
        pairs = []
        for strip in range(first, strips - 1, 2):
            pairs += [(strip, strip + 1), (strip + 1, strip)]
        return lax.ppermute(table, "strip", pairs)

    swap = [(member, member ^ 1) for member in range(members)]
    arrived = []
    for hop in range(2, members, 2):
        pairs = [((member + hop) % members, member) for member in range(members)]
        arrived.append(lax.ppermute(points, "tile", pairs))
    near, far = trade(0), trade(1)
    packed, rows = early_rows([points, lax.ppermute(points, "tile", swap)])
    weights, totals = own_totals(near_kernel, 1, packed, rows, near)
    arrived = lax.optimization_barrier((arrived, totals, far))[0]
    weights, totals = own_totals(far_kernel, 2, packed, rows, far, weights, totals)
    others = arrived + [lax.ppermute(group, "tile", swap) for group in arrived]
    sums = all_totals(others, weights, totals)
    all_sums = lax.all_gather(sums, ("seg", "tile"), axis=0)
    adjusted, corrections = pl.pallas_call(
        functools.partial(step_kernel, segs, members),
        out_shape=(
            jax.ShapeDtypeStruct((3, tiles, TILE_PTS), jnp.float32),
            jax.ShapeDtypeStruct((6, 1, KNOT_DEV), jnp.float32),
        ),
        in_specs=vmem(2),
        out_specs=(pl.BlockSpec(memory_space=pltpu.VMEM),) * 2,
        scratch_shapes=[
            pltpu.VMEM((8 * SUM_ROWS, KNOT_DEV), jnp.float32),
            pltpu.VMEM((tiles, KNOT_DEV), jnp.int32),
        ],
        compiler_params=params(6),
    )(all_sums, points)
    return adjusted.reshape(positions.shape), corrections.reshape(1, 6, KNOT_DEV)


def solution(mesh):
    in_specs = (
        P("strip", None, ("seg", "tile")),
        P("strip", None, ("seg", "tile")),
        P("strip", ("seg", "tile")),
        P("strip", None, ("seg", "tile")),
        P("strip", ("seg", "tile")),
        P("strip", ("seg", "tile")),
        P("strip", ("seg", "tile")),
    )
    out_specs = (P("strip", None, ("seg", "tile")), P("strip", None, "seg"))
    return jax.shard_map(local, mesh=mesh, in_specs=in_specs, out_specs=out_specs, check_vma=False)
```

```python
import functools

import jax
import jax.numpy as jnp
from jax import lax
from jax.experimental import pallas as pl
from jax.experimental.pallas import tpu as pltpu
from jax.sharding import PartitionSpec as P

KNOT_DEV = 128
TILE_PTS = 128
CHANNELS = 9
BLOCK_TILES = 4
ROW_GROUP = 16
SPREAD = 17
POINT_ROWS = 16
PARTNER = 13
KNOT = 14
VALID = 15
TILE_ROW = 14
SUM_ROWS = 80

damping = 1.0

PAIRS = [(a, b) for a in range(6) for b in range(a, 6)]


def params(mebibytes=48):
    return pltpu.CompilerParams(vmem_limit_bytes=mebibytes * 2**20)


def vmem(count):
    return [pl.BlockSpec(memory_space=pltpu.VMEM)] * count


def pack_kernel(pos, cov, lever, time, partner, sides, knots, table_ref, points_ref, ints, small, sems):
    tiles = time.shape[0]
    base = TILE_ROW * tiles

    def span(first):
        return points_ref.at[pl.ds(first * tiles, tiles)]

    copies = [
        pltpu.make_async_copy(partner, ints, sems.at[0]),
        pltpu.make_async_copy(sides, small.at[0], sems.at[1]),
        pltpu.make_async_copy(knots, small.at[1], sems.at[2]),
        pltpu.make_async_copy(pos, table_ref.at[pl.ds(0, 3)], sems.at[3]),
        pltpu.make_async_copy(cov, table_ref.at[pl.ds(3, 6)], sems.at[4]),
        pltpu.make_async_copy(time, span(12), sems.at[5]),
    ]
    copies += [pltpu.make_async_copy(lever.at[c], span(9 + c), sems.at[6 + c]) for c in range(3)]
    for copy in copies:
        copy.start()
    for copy in copies:
        copy.wait()
    for channel in range(CHANNELS):
        points_ref[channel * tiles : (channel + 1) * tiles, :] = table_ref[channel]
    points_ref[PARTNER * tiles : (PARTNER + 1) * tiles, :] = ints[...].astype(jnp.float32)
    points_ref[base : base + 8, :] = jnp.zeros((8, TILE_PTS), jnp.float32)
    for place in range(2):
        points_ref[base + place : base + place + 1, 0:tiles] = small[place].astype(jnp.float32)


def split_two(value):
    high = value.astype(jnp.bfloat16)
    low = (value - high.astype(jnp.float32)).astype(jnp.bfloat16)
    return high, low


def row_room(groups, tiles):
    return groups * tiles + 4 * ROW_GROUP


def arrange(points, packed, work):
    compact, codes, places, sem = work
    tiles = (points[0].shape[0] - 8) // TILE_ROW
    total = len(points) * tiles
    room = packed.shape[0] // POINT_ROWS
    shape = (tiles, TILE_PTS)
    lanes = lax.broadcasted_iota(jnp.int32, shape, 1)
    own_tile = lax.broadcasted_iota(jnp.int32, shape, 0)

    def ordered(size, test):
        rows = lax.broadcasted_iota(jnp.int32, (size, size), 0)
        marks = test(rows, lax.broadcasted_iota(jnp.int32, (size, size), 1))
        return jnp.where(marks, 1.0, 0.0).astype(jnp.bfloat16)

    member = lax.axis_index("tile")
    near = jnp.where(lax.axis_index("strip") % 2 == 1, 0.0, 1.0)

    def tile_value(group, place):
        at = TILE_ROW * tiles + place
        return jnp.take_along_axis(
            jnp.broadcast_to(group[at : at + 1, :], shape), own_tile, axis=1, mode="promise_in_bounds"
        )

    marks = []
    for group in points:
        index = group[PARTNER * tiles : (PARTNER + 1) * tiles, :].astype(jnp.int32)
        offset = lax.shift_right_logical(index, 7) - member * tiles
        wanted = (offset >= 0) & (offset < tiles) & (tile_value(group, 0) != 2.0)
        marks.append(jnp.where(wanted, 1.0, 0.0).astype(jnp.bfloat16))
    marks = jnp.concatenate(marks, axis=0)
    ranks = jnp.dot(
        marks, ordered(TILE_PTS, lambda row, lane: row <= lane), preferred_element_type=jnp.float32
    ).astype(jnp.int32)
    sources = []
    for p in range(len(points)):
        rank = ranks[p * tiles : (p + 1) * tiles]
        source = jnp.zeros_like(lanes)
        for jump in (64, 32, 16, 8, 4, 2, 1):
            there = jnp.take_along_axis(
                rank, source + (jump - 1), axis=1, mode="promise_in_bounds"
            )
            source = jnp.where(there <= lanes, source + jump, source)
        sources.append(source)
    number = lax.dot_general(
        jnp.ones((16, TILE_PTS), jnp.bfloat16),
        marks,
        (((1,), (1,)), ((), ())),
        preferred_element_type=jnp.float32,
    )
    base = TILE_ROW * tiles
    sides = jnp.concatenate([group[base : base + 1, 0:tiles] for group in points], axis=1)
    far = jnp.broadcast_to(jnp.where(sides == near, 0.0, 1.0), number.shape)
    upper_rows = lax.broadcasted_iota(jnp.int32, number.shape, 0) < 8
    chosen = jnp.where(upper_rows, number * (1.0 - far), number * far)
    before = jnp.dot(
        chosen.astype(jnp.bfloat16),
        ordered(total, lambda row, lane: row < lane),
        preferred_element_type=jnp.float32,
    )
    ends = (before + chosen).astype(jnp.int32)
    before = before.astype(jnp.int32)
    far = far[0:8] > 0.0
    start = jnp.where(far, before[8:16], before[0:8])
    row = lax.shift_right_logical(start, 7)
    first = jnp.where(far, room - 1 - row, row) * POINT_ROWS
    second = jnp.where(far, first - POINT_ROWS, first + POINT_ROWS)
    line = lax.broadcasted_iota(jnp.int32, (8, total), 0)
    code = jnp.where(line == 0, first, jnp.where(line == 1, second, start & (TILE_PTS - 1)))
    code = jnp.where(line == 3, ends[0:8], jnp.where(line == 4, ends[8:16], code))
    codes[...] = code
    copy = pltpu.make_async_copy(codes, places, sem.at[0])
    copy.start()
    for p, group in enumerate(points):
        rank, source = ranks[p * tiles : (p + 1) * tiles], sources[p]
        for channel in range(POINT_ROWS):
            if channel == VALID:
                value = jnp.where(lanes < jnp.broadcast_to(rank[:, TILE_PTS - 1 :], shape), 1.0, 0.0)
            elif channel == KNOT:
                value = tile_value(group, 1)
            else:
                value = group[channel * tiles : (channel + 1) * tiles, :]
                value = jnp.take_along_axis(value, source, axis=1, mode="promise_in_bounds")
            at = p * tiles * POINT_ROWS + channel
            compact[pl.ds(at, tiles, stride=POINT_ROWS), :] = value
    copy.wait()

    wide = lax.broadcasted_iota(jnp.int32, (POINT_ROWS, TILE_PTS), 1)

    def span(first):
        return pl.ds(pl.multiple_of(first, POINT_ROWS), POINT_ROWS)

    def place(tile):
        shift = places[2, tile]
        value = pltpu.roll(compact[span(tile * POINT_ROWS), :], shift, 1)
        at = span(places[0, tile])
        packed[at, :] = jnp.where(wide >= shift, value, packed[at, :])
        packed[span(places[1, tile]), :] = jnp.where(wide < shift, value, 0.0)

    unroll = total if total <= 2 * TILE_PTS else tiles

    def several(step, carry):
        for tile in range(unroll):
            place(step * unroll + tile)
        return carry

    if unroll == total:
        several(0, 0)
    else:
        lax.fori_loop(0, total // unroll, several, 0)
    near_rows = lax.shift_right_logical(places[3, total - 1] + TILE_PTS - 1, 7)
    far_rows = lax.shift_right_logical(places[4, total - 1] + TILE_PTS - 1, 7)
    blank = jnp.zeros((POINT_ROWS, TILE_PTS), jnp.float32)
    for extra in range(ROW_GROUP):
        packed[span((near_rows + extra) * POINT_ROWS), :] = blank
        packed[span((room - 1 - far_rows - extra) * POINT_ROWS), :] = blank
    return near_rows, far_rows


def weigh_table(table, weights, slot):
    tiles = table.shape[1]
    for channel in range(CHANNELS):
        high, low = split_two(table[channel])
        rows = slice(channel * tiles, (channel + 1) * tiles)
        weights[slot, rows, 0:TILE_PTS] = high
        weights[slot, rows, TILE_PTS : 2 * TILE_PTS] = low


def process(packed, near_rows, far_rows, weights, totals_ref, work):
    target, terms_ref = work
    tiles = weights.shape[1] // CHANNELS
    room = packed.shape[0] // POINT_ROWS
    member = lax.axis_index("tile")
    near_blocks = lax.shift_right_logical(near_rows + BLOCK_TILES - 1, 2)
    far_blocks = lax.shift_right_logical(far_rows + BLOCK_TILES - 1, 2)
    blocks = near_blocks + far_blocks
    queries = BLOCK_TILES * TILE_PTS

    def one_block(block):
        far = block >= near_blocks
        slot = far.astype(jnp.int32)
        base = jnp.where(far, room - BLOCK_TILES * (block - near_blocks + 1), block * BLOCK_TILES)
        ids = [base + j for j in range(BLOCK_TILES)]

        def channel(place):
            rows = [
                packed[pl.ds(base * POINT_ROWS + j * POINT_ROWS + place, 1), :]
                for j in range(BLOCK_TILES)
            ]
            return jnp.concatenate(rows, axis=1)

        index = channel(PARTNER).astype(jnp.int32)
        keys = index & (TILE_PTS - 1)
        rows = lax.shift_right_logical(index, 7) - member * tiles
        rows = jnp.where(channel(VALID) > 0.0, rows, -1)
        hot = jnp.where(
            lax.broadcasted_iota(jnp.int32, (TILE_PTS, queries), 0) == keys, 1.0, 0.0
        ).astype(jnp.bfloat16)
        picked = jnp.dot(
            weights[slot], jnp.concatenate([hot, hot], axis=0), preferred_element_type=jnp.float32
        )
        spread_rows = jnp.broadcast_to(rows, (8, queries))
        eight = lax.broadcasted_iota(jnp.int32, (8, queries), 0)
        found = [jnp.zeros((8, queries), jnp.float32) for _ in range(CHANNELS)]
        for step in range(tiles // 8):
            here = spread_rows == eight + 8 * step
            for channel in range(CHANNELS):
                begin = channel * tiles + 8 * step
                found[channel] = jnp.where(here, picked[begin : begin + 8], found[channel])
        return ids, [jnp.sum(entry, axis=0, keepdims=True) for entry in found]

    def pick(first, count):
        results = [one_block(first + i) for i in range(count)]
        for ids, flat in results:
            for channel in range(CHANNELS):
                for j in range(BLOCK_TILES):
                    piece = flat[channel][:, j * TILE_PTS : (j + 1) * TILE_PTS]
                    target[channel, pl.ds(ids[j], 1), :] = piece

    def three(step, carry):
        pick(3 * step, 3)
        return carry

    def one(block, carry):
        pick(block, 1)
        return carry

    threes = lax.div(blocks, jnp.int32(3))
    lax.fori_loop(0, threes, three, 0)
    rest = blocks - 3 * threes

    @pl.when(rest == 1)
    def _():
        pick(3 * threes, 1)

    @pl.when(rest == 2)
    def _():
        pick(3 * threes, 2)

    totals_ref[...] = jnp.zeros_like(totals_ref)
    terms_ref[75 * SPREAD :, :] = jnp.zeros((5 * SPREAD, TILE_PTS), jnp.float32)
    near_groups = lax.shift_right_logical(near_rows + ROW_GROUP - 1, 4)
    far_groups = lax.shift_right_logical(far_rows + ROW_GROUP - 1, 4)

    def add(step, carry):
        far = step >= near_groups
        base = jnp.where(far, room - ROW_GROUP * (step - near_groups + 1), step * ROW_GROUP)
        used = jnp.where(far, far_rows - ROW_GROUP * (step - near_groups), near_rows - ROW_GROUP * step)
        base = pl.multiple_of(base, ROW_GROUP)
        add_rows(base, far, used, packed, target, totals_ref, terms_ref)
        return carry

    lax.fori_loop(0, near_groups + far_groups, add, 0)


def add_rows(base, far, used, packed, target, totals_ref, terms_ref):
    group = ROW_GROUP
    span = pl.ds(base, group)

    def own(channel):
        return packed[pl.ds(base * POINT_ROWS + channel, group, stride=POINT_ROWS), :]

    valid = own(VALID) > 0.0
    m = [own(3 + c) + target[3 + c, span, :] for c in range(6)]
    residual = [jnp.where(valid, own(c) - target[c, span, :], 0.0) for c in range(3)]
    lever = [own(9 + c) for c in range(3)]
    later = own(12)
    early = 1.0 - later
    adjunct = [
        m[1] * m[2] - m[5] * m[5],
        m[0] * m[2] - m[4] * m[4],
        m[0] * m[1] - m[3] * m[3],
        m[4] * m[5] - m[3] * m[2],
        m[3] * m[5] - m[4] * m[1],
        m[3] * m[4] - m[0] * m[5],
    ]
    determinant = m[0] * adjunct[0] + m[3] * adjunct[3] + m[4] * adjunct[4]
    inv = [jnp.where(valid, entry / determinant, 0.0) for entry in adjunct]
    info = [[inv[0], inv[3], inv[4]], [inv[3], inv[1], inv[5]], [inv[4], inv[5], inv[2]]]

    def turned(column):
        return [
            lever[1] * column[2] - lever[2] * column[1],
            lever[2] * column[0] - lever[0] * column[2],
            lever[0] * column[1] - lever[1] * column[0],
        ] + list(column)

    weighted = [turned(info[i]) for i in range(3)]
    pulled = [
        info[i][0] * residual[0] + info[i][1] * residual[1] + info[i][2] * residual[2]
        for i in range(3)
    ]
    gradient = turned(pulled)
    gram = {}
    for b in range(6):
        column = turned([weighted[i][b] for i in range(3)])
        for a in range(b + 1):
            gram[a, b] = column[a]
    both = early * later
    terms = []
    for weight in (early * early, both, later * later):
        terms += [gram[pair] * weight for pair in PAIRS]
    for weight in (early, later):
        terms += [entry * weight for entry in gradient]
    for place, term in enumerate(terms):
        terms_ref[place * SPREAD : place * SPREAD + group, :] = term
    stacked = lax.broadcasted_iota(jnp.int32, (KNOT_DEV, TILE_PTS), 0)

    def add(first, count):
        total = totals_ref[...]
        for place in range(first, first + count, 2):
            parts, hots = [], []
            for r in (place, place + 1):
                r = jnp.where(far, group - 1 - r, r)
                high, low = split_two(terms_ref[pl.ds(r, SUM_ROWS, stride=SPREAD), :])
                parts.append(jnp.concatenate([high, low], axis=0))
                knots = packed[pl.ds((base + r) * POINT_ROWS + KNOT, 1), :].astype(jnp.int32)
                hots.append(jnp.where(stacked == knots, 1.0, 0.0).astype(jnp.bfloat16))
            sums = lax.dot_general(
                jnp.concatenate(parts, axis=1),
                jnp.concatenate(hots, axis=1),
                (((1,), (1,)), ((), ())),
                preferred_element_type=jnp.float32,
            )
            total = total + sums[0:SUM_ROWS] + sums[SUM_ROWS:]
        totals_ref[...] = total

    add(0, 12)

    @pl.when(used > 12)
    def _():
        add(12, group - 12)


def early_kernel(groups, *refs):
    points = refs[:groups]
    packed, rows_ref = refs[groups : groups + 2]
    near_rows, far_rows = arrange(points, packed, refs[groups + 2 :])
    rows_ref[0:8, :] = jnp.full((8, TILE_PTS), near_rows, jnp.int32)
    rows_ref[8:16, :] = jnp.full((8, TILE_PTS), far_rows, jnp.int32)


def near_kernel(packed, rows_ref, near, weights, totals_ref, *work):
    near_rows = jnp.max(rows_ref[0:8, :])
    weigh_table(near, weights, 0)
    process(packed, near_rows, jnp.int32(0), weights, totals_ref, work)


def far_kernel(packed, rows_ref, far, before, before_ref, weights, totals_ref, *work):
    far_rows = jnp.max(rows_ref[8:16, :])
    weights[0] = before[0]
    weigh_table(far, weights, 1)
    process(packed, jnp.int32(0), far_rows, weights, totals_ref, work)
    totals_ref[...] = totals_ref[...] + before_ref[...]


def other_kernel(groups, *refs):
    points = refs[:groups]
    weights, before_ref, totals_ref, packed = refs[groups : groups + 4]
    arranging, work = refs[groups + 4 : groups + 8], refs[groups + 8 :]
    near_rows, far_rows = arrange(points, packed, arranging)
    process(packed, near_rows, far_rows, weights, totals_ref, work)
    totals_ref[...] = totals_ref[...] + before_ref[...]


def arrange_shapes(groups, tiles):
    count = groups * tiles
    return [
        pltpu.VMEM((count * POINT_ROWS, TILE_PTS), jnp.float32),
        pltpu.VMEM((8, count), jnp.int32),
        pltpu.SMEM((8, count), jnp.int32),
        pltpu.SemaphoreType.DMA((1,)),
    ]


def process_shapes(groups, tiles):
    return [
        pltpu.VMEM((CHANNELS, row_room(groups, tiles), TILE_PTS), jnp.float32),
        pltpu.VMEM((SUM_ROWS * SPREAD, TILE_PTS), jnp.float32),
    ]


def packed_shape(groups, tiles):
    return (row_room(groups, tiles) * POINT_ROWS, TILE_PTS)


def early_rows(points):
    groups, tiles = len(points), (points[0].shape[0] - 8) // TILE_ROW
    return pl.pallas_call(
        functools.partial(early_kernel, groups),
        out_shape=(
            jax.ShapeDtypeStruct(packed_shape(groups, tiles), jnp.float32),
            jax.ShapeDtypeStruct((16, TILE_PTS), jnp.int32),
        ),
        in_specs=vmem(groups),
        out_specs=(pl.BlockSpec(memory_space=pltpu.VMEM),) * 2,
        scratch_shapes=arrange_shapes(groups, tiles),
        compiler_params=params(14),
    )(*points)


def own_totals(kernel, slots, packed, rows, table, *before):
    tiles = table.shape[1]
    return pl.pallas_call(
        kernel,
        out_shape=(
            jax.ShapeDtypeStruct((slots, CHANNELS * tiles, 2 * TILE_PTS), jnp.bfloat16),
            jax.ShapeDtypeStruct((SUM_ROWS, KNOT_DEV), jnp.float32),
        ),
        in_specs=vmem(3 + len(before)),
        out_specs=(pl.BlockSpec(memory_space=pltpu.VMEM),) * 2,
        scratch_shapes=process_shapes(2, tiles),
        compiler_params=params(14),
    )(packed, rows, table, *before)


def all_totals(points, weights, totals):
    groups, tiles = len(points), (points[0].shape[0] - 8) // TILE_ROW
    return pl.pallas_call(
        functools.partial(other_kernel, groups),
        out_shape=jax.ShapeDtypeStruct((SUM_ROWS, KNOT_DEV), jnp.float32),
        in_specs=vmem(groups + 2),
        out_specs=pl.BlockSpec(memory_space=pltpu.VMEM),
        scratch_shapes=[pltpu.VMEM(packed_shape(groups, tiles), jnp.float32)]
        + arrange_shapes(groups, tiles)
        + process_shapes(groups, tiles),
        compiler_params=params(24),
    )(*points, weights, totals)


def cholesky(matrix):
    factor = {}
    inverse = []
    for column in range(6):
        pivot = matrix[column, column]
        for inner in range(column):
            pivot = pivot - factor[column, inner] * factor[column, inner]
        inverse.append(1.0 / jnp.sqrt(pivot))
        for row in range(column + 1, 6):
            entry = matrix[column, row]
            for inner in range(column):
                entry = entry - factor[row, inner] * factor[column, inner]
            factor[row, column] = entry * inverse[column]
    return factor, inverse


def solve(system, right_side):
    factor, inverse = system
    forward = []
    for row in range(6):
        entry = right_side[row]
        for inner in range(row):
            entry = entry - factor[row, inner] * forward[inner]
        forward.append(entry * inverse[row])
    answer = [None] * 6
    for row in reversed(range(6)):
        entry = forward[row]
        for inner in range(row + 1, 6):
            entry = entry - factor[inner, row] * answer[inner]
        answer[row] = entry * inverse[row]
    return answer


def step_kernel(segs, members, sums, points_ref, adjusted_ref, out_ref, held, index_ref):
    tiles = index_ref.shape[0]
    seg = lax.axis_index("seg")
    at = TILE_ROW * tiles + 1
    index_ref[...] = jnp.take_along_axis(
        jnp.broadcast_to(points_ref[at : at + 1, :], index_ref.shape),
        lax.broadcasted_iota(jnp.int32, index_ref.shape, 0),
        axis=1,
        mode="promise_in_bounds",
    ).astype(jnp.int32)
    for place in range(3, 8):
        held[place * SUM_ROWS : (place + 1) * SUM_ROWS, :] = jnp.zeros(
            (SUM_ROWS, KNOT_DEV), jnp.float32
        )
    for place in range(3):
        wanted = seg + place - 1
        there = (wanted >= 0) & (wanted < segs)
        first = jnp.minimum(jnp.maximum(wanted, 0), segs - 1) * members
        total = sums[first]
        for other in range(1, members):
            total = total + sums[first + other]
        held[place * SUM_ROWS : (place + 1) * SUM_ROWS, :] = jnp.where(there, total, 0.0)
    shape = (8, KNOT_DEV)
    lanes = lax.broadcasted_iota(jnp.int32, shape, 1)
    rows = lax.broadcasted_iota(jnp.int32, shape, 0)

    def earlier(value):
        turned = pltpu.roll(value, 1, 1)
        return jnp.where(lanes == 0, pltpu.roll(turned, 1, 0), turned)

    def following(value):
        turned = pltpu.roll(value, KNOT_DEV - 1, 1)
        return jnp.where(lanes == KNOT_DEV - 1, pltpu.roll(turned, 7, 0), turned)

    def quantity(place):
        return held[pl.ds(place, 8, stride=SUM_ROWS), :]

    pair_place = {pair: place for place, pair in enumerate(PAIRS)}
    matrix, cross, cross_before = {}, {}, {}
    for pair, place in pair_place.items():
        value = quantity(place) + earlier(quantity(42 + place))
        matrix[pair] = value + damping if pair[0] == pair[1] else value
        cross[pair] = quantity(21 + place)
        cross_before[pair] = earlier(cross[pair])
    right_side = [quantity(63 + a) + earlier(quantity(69 + a)) for a in range(6)]
    system = cholesky(matrix)
    beyond = (rows >= 2) & (seg == segs - 1)
    first = [jnp.where(beyond, 0.0, -entry) for entry in solve(system, right_side)]
    before = [earlier(entry) for entry in first]
    after = [following(entry) for entry in first]
    corrected = []
    for a in range(6):
        total = right_side[a]
        for b in range(6):
            pair = (min(a, b), max(a, b))
            total = total + cross_before[pair] * before[b] + cross[pair] * after[b]
        corrected.append(total)
    second = [jnp.where(beyond, 0.0, -entry) for entry in solve(system, corrected)]
    upper = [following(entry) for entry in second]
    for a in range(6):
        out_ref[a] = second[a][1:2]
    low_rows = [jnp.broadcast_to(second[a][1:2], shape) for a in range(6)]
    high_rows = [jnp.broadcast_to(upper[a][1:2], shape) for a in range(6)]
    for begin in range(0, tiles, 8):
        span = slice(begin, begin + 8)
        knots = index_ref[span, :]

        def own(channel):
            return points_ref[channel * tiles + begin : channel * tiles + begin + 8, :]

        later = own(12)
        early = 1.0 - later
        pose = []
        for a in range(6):
            low = jnp.take_along_axis(low_rows[a], knots, axis=1, mode="promise_in_bounds")
            high = jnp.take_along_axis(high_rows[a], knots, axis=1, mode="promise_in_bounds")
            pose.append(early * low + later * high)
        lever = [own(c) for c in range(9, 12)]
        moved = [
            pose[1] * lever[2] - pose[2] * lever[1] + pose[3],
            pose[2] * lever[0] - pose[0] * lever[2] + pose[4],
            pose[0] * lever[1] - pose[1] * lever[0] + pose[5],
        ]
        for c in range(3):
            adjusted_ref[c, span, :] = own(c) + moved[c]


def local(positions, lever_arm, spline_time, covariance, partner, partner_side, tile_knot):
    tiles = positions.shape[2] // TILE_PTS
    strips = lax.axis_size("strip")
    members = lax.axis_size("tile")
    segs = lax.axis_size("seg")

    table, points = pl.pallas_call(
        pack_kernel,
        out_shape=(
            jax.ShapeDtypeStruct((CHANNELS, tiles, TILE_PTS), jnp.float32),
            jax.ShapeDtypeStruct((TILE_ROW * tiles + 8, TILE_PTS), jnp.float32),
        ),
        in_specs=[pl.BlockSpec(memory_space=pltpu.HBM)] * 7,
        out_specs=(pl.BlockSpec(memory_space=pltpu.VMEM),) * 2,
        scratch_shapes=[
            pltpu.VMEM((tiles, TILE_PTS), jnp.int32),
            pltpu.VMEM((2, 1, tiles), jnp.int32),
            pltpu.SemaphoreType.DMA((9,)),
        ],
        compiler_params=params(14),
    )(
        *[
            pltpu.with_memory_space_constraint(array, pltpu.HBM)
            for array in (
                positions.reshape(3, tiles, TILE_PTS),
                covariance.reshape(6, tiles, TILE_PTS),
                lever_arm.reshape(3, tiles, TILE_PTS),
                spline_time.reshape(tiles, TILE_PTS),
                partner.reshape(tiles, TILE_PTS),
                partner_side,
                tile_knot,
            )
        ]
    )

    def trade(first):
        pairs = []
        for strip in range(first, strips - 1, 2):
            pairs += [(strip, strip + 1), (strip + 1, strip)]
        return lax.ppermute(table, "strip", pairs)

    swap = [(member, member ^ 1) for member in range(members)]
    arrived = []
    for hop in range(2, members, 2):
        pairs = [((member + hop) % members, member) for member in range(members)]
        arrived.append(lax.ppermute(points, "tile", pairs))
    near, far = trade(0), trade(1)
    packed, rows = early_rows([points, lax.ppermute(points, "tile", swap)])
    weights, totals = own_totals(near_kernel, 1, packed, rows, near)
    arrived = lax.optimization_barrier((arrived, totals, far))[0]
    weights, totals = own_totals(far_kernel, 2, packed, rows, far, weights, totals)
    others = arrived + [lax.ppermute(group, "tile", swap) for group in arrived]
    sums = all_totals(others, weights, totals)
    all_sums = lax.all_gather(sums, ("seg", "tile"), axis=0)
    adjusted, corrections = pl.pallas_call(
        functools.partial(step_kernel, segs, members),
        out_shape=(
            jax.ShapeDtypeStruct((3, tiles, TILE_PTS), jnp.float32),
            jax.ShapeDtypeStruct((6, 1, KNOT_DEV), jnp.float32),
        ),
        in_specs=vmem(2),
        out_specs=(pl.BlockSpec(memory_space=pltpu.VMEM),) * 2,
        scratch_shapes=[
            pltpu.VMEM((8 * SUM_ROWS, KNOT_DEV), jnp.float32),
            pltpu.VMEM((tiles, KNOT_DEV), jnp.int32),
        ],
        compiler_params=params(6),
    )(all_sums, points)
    return adjusted.reshape(positions.shape), corrections.reshape(1, 6, KNOT_DEV)


def solution(mesh):
    in_specs = (
        P("strip", None, ("seg", "tile")),
        P("strip", None, ("seg", "tile")),
        P("strip", ("seg", "tile")),
        P("strip", None, ("seg", "tile")),
        P("strip", ("seg", "tile")),
        P("strip", ("seg", "tile")),
        P("strip", ("seg", "tile")),
    )
    out_specs = (P("strip", None, ("seg", "tile")), P("strip", None, "seg"))
    return jax.shard_map(local, mesh=mesh, in_specs=in_specs, out_specs=out_specs, check_vma=False)
```
